256 devices in a mesh: cfg: 2 (over core), seq: 32 (over z_hi, y, x), head: 4 (over z_lo).
Axes of the slice: x: 4, y: 4, z: 8 (z_hi: 2, z_lo: 4; z = z_hi * 4 + z_lo), core: 2. Of those that a mesh axis runs over, the one named last changes fastest.
Arguments:
- latent: bfloat16 [32768, 1152], P('seq')
- modulation: float32 [2, 6, 1152], P('cfg'), may hold values from -3 to 3
- w_qkv_space: bfloat16 [1152, 3, 1152], P(None, None, 'head')
- w_out_space: bfloat16 [1152, 1152], P('head'), may hold values from -0.1875 to 0.1875
- w_qkv_time: bfloat16 [1152, 3, 1152], P(None, None, 'head')
- w_out_time: bfloat16 [1152, 1152], P('head'), may hold values from -0.1875 to 0.1875
- clip_frames: int32 [4], replicated, may hold values from 1 to 32, 64 in all
- spatial_window: int32 [512], replicated, may hold values from 0 to 14, as said below
Outputs:
- guided: bfloat16 [32768, 1152], P('seq', 'cfg')
The draws below stay inside these ranges and needn't reach their ends.
Inputs may be any that keep to these rules, and one draw needn't show every extreme that they name: `clip_frames`: positive, summing to 64, the largest exactly 32. `spatial_window`: positions form 512 // 16 rows of 16; tiles of 8 x 8 are laid after an offset of 1 to 7 rows and 1 to 7 columns, so edge tiles are cut; row r, column c has number ((r + offset rows) // 8) * 3 + (c + offset columns) // 8; every number in the range occurs.
All inputs are finite; a program needn't handle non-finite values.
Results may differ from the reference program's by a relative error of at most 0.02.
Values may be sent and summed in bfloat16 or wider, within the bound.
A program may use at most 64 MiB of HBM per device.

```python
import math
import jax
import jax.numpy as jnp
import numpy as np
from jax import lax

D = 1152
HEADS = 16
HEAD_DIM = 72
POSITIONS = 512
CLIPS = 4
FRAMES = 64
TOKENS = 32768
TWIN = 16


def draw_latent(key, part):
    key = jax.random.fold_in(key, 11)
    key_col, key_row, key_base = jax.random.split(key, 3)
    col_scale = jnp.exp(jax.random.uniform(key_col, (1, D), jnp.float32, math.log(0.3), math.log(3.0)))
    row_scale = jnp.exp(jax.random.uniform(key_row, (TOKENS, 1), jnp.float32, math.log(0.3), math.log(3.0)))
    base_vals = jax.random.normal(key_base, (TOKENS, D), jnp.float32)
    return (base_vals * col_scale * row_scale).astype(jnp.bfloat16)


def draw_modulation(key, part):
    key = jax.random.fold_in(key, 53)
    key_base, key_sign, key_size = jax.random.split(key, 3)
    base_vals = jnp.clip(0.5 * jax.random.normal(key_base, (2, 6, D), jnp.float32), -3.0, 3.0)
    signs = jnp.where(jax.random.bernoulli(key_sign, 0.5, (2, 6, D)), 1.0, -1.0).astype(jnp.float32)
    sizes = jax.random.uniform(key_size, (2, 6, D), jnp.float32, 2.0, 3.0)
    rows = jnp.arange(6, dtype=jnp.int32)
    gate_rows = ((rows == 2) | (rows == 5))[None, :, None]
    return jnp.where(gate_rows, signs * sizes, base_vals).astype(jnp.float32)


def draw_spatial_window(key, part):
    key = jax.random.fold_in(key, 23)
    offsets = jax.random.randint(key, (2,), 1, 8, dtype=jnp.int32)
    places = jnp.arange(POSITIONS, dtype=jnp.int32)
    return (places // 16 + offsets[0]) // 8 * 3 + (places % 16 + offsets[1]) // 8


def draw_w_qkv_space(key, part):
    key = jax.random.fold_in(key, 37)
    key_base = jax.random.fold_in(key, 0)
    base = jnp.clip(jax.random.normal(key_base, (D, 3, D), jnp.float32), -4.0, 4.0) * D ** (-0.5)
    return base.astype(jnp.bfloat16)


def draw_w_qkv_time(key, part):
    key = jax.random.fold_in(key, 41)
    key_base = jax.random.fold_in(key, 0)
    base = jnp.clip(jax.random.normal(key_base, (D, 3, D), jnp.float32), -4.0, 4.0) * D ** (-0.5)
    return base.astype(jnp.bfloat16)


def steps_of(rng, shape, cuts, smallest, largest):
    def one(position, blocks):
        heights = jax.random.uniform(jax.random.fold_in(jax.random.fold_in(rng, 6), position), (blocks,), jnp.float32, smallest / len(cuts), largest / len(cuts))
        return jnp.repeat(jnp.exp(heights), shape[position] // blocks).reshape((-1,) + (1,) * (len(shape) - position - 1))

    factor_of = one(*cuts[0])
    for cut in cuts[1:]:
        factor_of = factor_of * one(*cut)
    return factor_of


def length_profile(count, total, most, lean):
    weights = [(1 << 20) // math.isqrt(grade ** lean) + 1 for grade in range(2, count + 1)]
    spare, holding = total - most - (count - 1), [1] * (count - 1)
    while spare > 0:
        movable = [i for i in range(count - 1) if holding[i] < most]
        pool, left = sum([weights[i] for i in movable]), spare
        for i in movable:
            extra = min(most - holding[i], max(1, left * weights[i] // pool), spare)
            holding[i] = holding[i] + extra
            spare = spare - extra
    return np.array([most] + holding)


def uneven(own_key, amount, total, most, slope):
    if amount == 2:
        one = jax.random.randint(own_key, (), max(1, total - most), min(most, total - 1) + 1)
        return jnp.stack([one, total - one])
    sizes = jnp.asarray(length_profile(amount, total, most, slope), jnp.int32)
    couples = (amount - 1) // 2
    source_of, sink = sizes[1:1 + 2 * couples:2], sizes[2:2 + 2 * couples:2]
    room = jnp.minimum(source_of - 1, most - sink)
    shifted = jax.random.randint(jax.random.fold_in(own_key, 1), (couples,), 0, 1 << 20) % (room + 1)
    sizes = sizes.at[1:1 + 2 * couples:2].set(source_of - shifted).at[2:2 + 2 * couples:2].set(sink + shifted)
    return sizes[jax.random.permutation(jax.random.fold_in(own_key, 2), amount)]


def bell_draw(rng, dims, deviation, most, cuts=(), kind=jnp.bfloat16):
    drawn = deviation * jax.random.normal(rng, dims, jnp.float32)
    if cuts:
        drawn = drawn * steps_of(rng, dims, cuts, -0.22, 0.18)
    return jnp.clip(drawn, -most, most).astype(kind)


def setup_inputs(seed: int = 0) -> dict:
    keys = jax.random.split(jax.random.key(seed), 9)
    latent = draw_latent(jax.random.fold_in(keys[8], 71), 0)
    modulation = draw_modulation(jax.random.fold_in(keys[8], 71), 0)
    w_qkv_space = draw_w_qkv_space(jax.random.fold_in(keys[8], 71), 0)
    w_out_space = bell_draw(keys[3], (D, D), D ** -0.5, 0.1875, ((0, 4),))
    w_qkv_time = draw_w_qkv_time(jax.random.fold_in(keys[8], 71), 0)
    w_out_time = bell_draw(keys[5], (D, D), D ** -0.5, 0.1875, ((0, 4),))
    clip_frames = uneven(keys[6], CLIPS, FRAMES, FRAMES // 2, 2).astype(jnp.int32)
    spatial_window = draw_spatial_window(jax.random.fold_in(keys[8], 71), 0)
    return dict(latent=latent, modulation=modulation, w_qkv_space=w_qkv_space, w_out_space=w_out_space, w_qkv_time=w_qkv_time, w_out_time=w_out_time, clip_frames=clip_frames, spatial_window=spatial_window)


GUIDE = 4.0
EPSILON = 1e-06

def modulate(token_rows, shift_vec, scale_vec):
    values = token_rows.astype(jnp.float32)
    centre = lax.optimization_barrier(jnp.mean(values, axis=-1, keepdims=True))
    centered = values - centre
    spread = lax.optimization_barrier(jnp.mean(centered * centered, axis=-1, keepdims=True))
    normed = centered * lax.rsqrt(spread + EPSILON)
    return (normed * (1.0 + shift_vec * 0.0 + scale_vec) + shift_vec).astype(jnp.bfloat16)

def attend(query_rows, key_rows, value_rows, allowed):
    scores = jnp.einsum('qhd,khd->hqk', query_rows.astype(jnp.float32), key_rows.astype(jnp.float32)) * HEAD_DIM ** (-0.5)
    scores = jnp.where(allowed[None], scores, -1e+30)
    row_top = lax.optimization_barrier(jnp.max(scores, axis=-1, keepdims=True))
    expo_terms = jnp.exp(scores - row_top)
    weights = (expo_terms / lax.optimization_barrier(jnp.sum(expo_terms, axis=-1, keepdims=True))).astype(jnp.bfloat16)
    output = jnp.einsum('hqk,khd->qhd', weights.astype(jnp.float32), value_rows.astype(jnp.float32))
    return output.astype(jnp.bfloat16)

def sublayer(token_rows, allowed, w_qkv, w_out, shift_vec, scale_vec, gate_vec):
    number_rows = token_rows.shape[0]
    modded = modulate(token_rows, shift_vec, scale_vec)
    packed = jnp.dot(modded, w_qkv.reshape(D, 3 * D), preferred_element_type=jnp.float32).astype(jnp.bfloat16)
    packed = packed.reshape(number_rows, 3, HEADS, HEAD_DIM)
    heads_out = attend(packed[:, 0], packed[:, 1], packed[:, 2], allowed)
    projected = jnp.dot(heads_out.reshape(number_rows, D), w_out, preferred_element_type=jnp.float32).astype(jnp.bfloat16)
    return (token_rows.astype(jnp.float32) + gate_vec * projected.astype(jnp.float32)).astype(jnp.bfloat16)

def window_mask(clip_frames, all_frames):
    clip_ends = jnp.cumsum(clip_frames).astype(jnp.int32)
    clip_starts = (clip_ends - clip_frames).astype(jnp.int32)
    frame_ids = jnp.arange(all_frames, dtype=jnp.int32)
    clip_of = lax.optimization_barrier(jnp.sum((frame_ids[:, None] >= clip_ends[None, :]).astype(jnp.int32), axis=1))
    clip_ids = jnp.arange(CLIPS, dtype=jnp.int32)
    start_of = lax.optimization_barrier(jnp.sum(jnp.where(clip_of[:, None] == clip_ids[None, :], clip_starts[None, :], 0), axis=1)).astype(jnp.int32)
    window = clip_of * all_frames + (frame_ids - start_of) // TWIN
    return window[:, None] == window[None, :]

def reference(latent, modulation, w_qkv_space, w_out_space, w_qkv_time, w_out_time, clip_frames, spatial_window):
    same_window = spatial_window[:, None] == spatial_window[None, :]
    same_span = window_mask(clip_frames, FRAMES)
    frames = latent.reshape(FRAMES, POSITIONS, D)
    results = []
    for branch in range(2):
        factors = modulation[branch]

        def space_frame(token_rows):
            return sublayer(token_rows, same_window, w_qkv_space, w_out_space, factors[0], factors[1], factors[2])
        after_space = lax.map(space_frame, frames)
        columns = jnp.transpose(after_space, (1, 0, 2))

        def time_column(token_rows):
            return sublayer(token_rows, same_span, w_qkv_time, w_out_time, factors[3], factors[4], factors[5])
        after_time = lax.map(time_column, columns)
        results.append(jnp.transpose(after_time, (1, 0, 2)).reshape(TOKENS, D).astype(jnp.float32))
    cond_rows, uncond = results
    return (uncond + GUIDE * (cond_rows - uncond)).astype(jnp.bfloat16)
```

```python
import functools

import jax
import jax.numpy as jnp
from jax import lax
from jax.experimental import pallas as pl
from jax.experimental.pallas import tpu as pltpu
from jax.sharding import PartitionSpec as P

MESH = pl.DeviceIdType.MESH
HEAD_DIM = 72
POSITIONS = 512
WIDTH = 1152
HALF = 576
LOCAL = 288
PAIR = 144
TWIN = 16
GUIDE = 4.0
EPSILON = 1e-06
NEG = -1e30
PAD = 128
RING = 8
PLANE = 16
GROUP = 16
EXP_SCALE = HEAD_DIM ** (-0.5) * 1.4426950408889634
BF = jnp.bfloat16
F32 = jnp.float32


def iota(shape, dim):
    return lax.broadcasted_iota(jnp.int32, shape, dim)


def modulated(rows, shift, scale):
    values = rows.astype(F32)
    centred = values - jnp.mean(values, axis=-1, keepdims=True)
    spread = jnp.mean(centred * centred, axis=-1, keepdims=True)
    normed = centred * lax.rsqrt(spread + EPSILON)
    return (normed * (1.0 + scale) + shift).astype(BF)


def softmax(scores):
    top = jnp.max(scores, axis=-1, keepdims=True)
    terms = jnp.exp2((scores - top) * EXP_SCALE)
    return (terms * (1.0 / jnp.sum(terms, axis=-1, keepdims=True))).astype(BF)


def dot(a, b):
    return lax.dot_general(a, b, (((1,), (0,)), ((), ())), preferred_element_type=F32)


def dot_t(a, b):
    return lax.dot_general(a, b, (((1,), (1,)), ((), ())), preferred_element_type=F32)


def head_mask(head, lanes):
    lane = iota((1, lanes), 1)
    return jnp.where((lane >= head * HEAD_DIM) & (lane < (head + 1) * HEAD_DIM), 1.0, 0.0)


def frame_window(frame, clip_ref):
    ends = [clip_ref[0]]
    for j in range(1, 4):
        ends.append(ends[-1] + clip_ref[j])
    clip = jnp.zeros_like(frame)
    start = jnp.zeros_like(frame)
    for end in ends:
        clip = clip + jnp.where(frame >= end, 1, 0)
        start = jnp.where(frame >= end, end, start)
    return clip * 64 + (frame - start) // TWIN


def kernel(
    sw_ref, clip_ref, lat, mod, wsp, wo, wt, out,
    modx, xb, qs, ks, vs, base, att, heads, wos, lats, xs, xt, wbuf, tbias, xn, os_, psend, precv, gs, g2, gz,
    mod_s, lat_s, wo_s, wo_r, wz_s, wz_r, wp_s, wp_r, za_s, za_r, xy_s, xy_r, sb_s, sb_r, pp_s, r1_s, r1_r, r2_s, r2_r,
):
    c = lax.axis_index("cfg")
    s = lax.axis_index("seq")
    h = lax.axis_index("head")
    zh = s // PLANE
    i = s % PLANE
    y = i // 4
    x = i % 4
    z = zh * 4 + h

    def on_z(zz):
        return (c, (zz // 4) * PLANE + i, zz % 4)

    def on_plane(ii):
        return (c, zh * PLANE + ii, h)

    sib = (1 - c, s, h)

    def remote(src, dst, send, recv, dev):
        return pltpu.make_async_remote_copy(
            src_ref=src, dst_ref=dst, send_sem=send, recv_sem=recv, device_id=dev, device_id_type=MESH
        )

    def landed(buf, recv):
        remote(buf, buf, recv, recv, sib).wait_recv()

    def sent(buf, send):
        remote(buf, buf, send, send, sib).wait_send()

    barrier = pltpu.get_barrier_semaphore()

    def greet_z(k, _):
        pl.semaphore_signal(barrier, inc=1, device_id=on_z((z + k) % RING), device_id_type=MESH)
        return 0

    def greet_plane(k, _):
        pl.semaphore_signal(barrier, inc=1, device_id=on_plane((i + k) % PLANE), device_id_type=MESH)
        return 0

    lax.fori_loop(1, RING, greet_z, 0)
    lax.fori_loop(1, PLANE, greet_plane, 0)
    pl.semaphore_signal(barrier, inc=1, device_id=sib, device_id_type=MESH)
    pl.semaphore_wait(barrier, RING - 1 + PLANE - 1 + 1)

    far = jnp.where(c == 0, 2, RING - 2)

    def shard_rows(j):
        return (i + 12 * j) % GROUP

    def weight_piece(j, t):
        first = shard_rows(j)
        flat = 36 * j + first + 16 * t
        return first + 16 * t, flat // 16

    hops = [RING - 1, far, 1]
    for j in range(3):
        for t in range(3):
            row, q = weight_piece(j, t)
            copy = remote(
                wt.at[pl.ds(row * GROUP, GROUP)], wbuf.at[q, y, x], wz_s.at[j, t], wz_r.at[j, t], on_z((z + hops[j]) % RING)
            )
            if t < 2:
                copy.start()
            else:
                pl.when(row < 36)(copy.start)

    mod_copy = remote(mod, modx, mod_s.at[0], mod_s.at[1], sib)
    mod_copy.start()
    lat_out = remote(
        lat.at[c, pl.ds(64 * (7 - z), 64)], lats.at[zh * 2 + c], lat_s.at[0], lat_s.at[1], on_z(7 - z)
    )
    lat_out.start()
    wo_rows = pl.ds(PAIR * c, PAIR)
    for k, hop in enumerate([1, RING - 1, far]):
        remote(wo.at[wo_rows], wos.at[h, wo_rows], wo_s.at[k], wo_r.at[k], on_z((z + hop) % RING)).start()

    oy = jnp.int32(7)
    ox = jnp.int32(7)
    for r in range(1, 8):
        oy = oy - jnp.where(sw_ref[16 * r] < 3, 1, 0)
        ox = ox - jnp.where(sw_ref[r] < 1, 1, 0)
    qj = iota((128, 384), 0)
    ki = iota((128, 384), 1)
    same = ((qj // 16 + 8 + oy) // 8 == (ki // 16 + oy) // 8) & ((qj % 16 + ox) // 8 == (ki % 16 + ox) // 8)
    base[...] = jnp.where(same, 0.0, NEG)

    def time_key(row):
        four = row % 4
        frame = (four // 2) * 32 + 2 * (row // 16) + four % 2
        return frame_window(frame, clip_ref) * 4 + (row % 16) // 4

    tbias[...] = jnp.where(time_key(iota((256, 1), 0)) == time_key(iota((1, 256), 1)), 0.0, NEG)

    for ref in (ks, vs):
        ref[0:PAD, :] = jnp.zeros((PAD, 384), BF)
        ref[PAD + POSITIONS :, :] = jnp.zeros((PAD, 384), BF)
        ref[PAD : PAD + POSITIONS, 256:384] = jnp.zeros((POSITIONS, 128), BF)
    qs[:, 256:384] = jnp.zeros((POSITIONS, 128), BF)

    shift1, scale1 = mod[0:1, :], mod[1:2, :]
    masks = [head_mask(n, 384) for n in range(4)]

    for f in range(2):

        def project(rb, _):
            rows = pl.ds(rb * 256, 256)
            values = modulated(lat[f, rows, :], shift1, scale1)
            qs[rows, 0:LOCAL] = dot(values, wsp[0]).astype(BF)
            ks[pl.ds(PAD + rb * 256, 256), 0:LOCAL] = dot(values, wsp[1]).astype(BF)
            vs[pl.ds(PAD + rb * 256, 256), 0:LOCAL] = dot(values, wsp[2]).astype(BF)
            return 0

        lax.fori_loop(0, 2, project, 0)

        def attend(k, _):
            query = qs[pl.ds(k * 128, 128), :]
            stacked = jnp.concatenate([query * m.astype(BF) for m in masks], axis=0)
            keys = ks[pl.ds(k * 128, 384), :]
            vals = vs[pl.ds(k * 128, 384), :]
            row = 8 * k - 8 + iota((1, 384), 1) // 16
            bias = base[...] + jnp.where((row >= 0) & (row < 32), 0.0, NEG)
            scores = dot_t(stacked, keys) + jnp.concatenate([bias] * 4, axis=0)
            mixed = dot(softmax(scores), vals)
            total = mixed[0:128] * masks[0]
            for n in range(1, 4):
                total = total + mixed[128 * n : 128 * (n + 1)] * masks[n]
            att[f, pl.ds(k * 128, 128), :] = total.astype(BF)
            for t in range(2):
                zd = 2 * k + t
                block = att.at[f, pl.ds(64 * zd, 64)]
                copy = remote(block, heads.at[h, zh * 2 + f], za_s.at[f, zd], za_r.at[f, z], on_z(zd))
                pl.when(zd != z)(copy.start)

                @pl.when(zd == z)
                def _():
                    heads[h, zh * 2 + f] = att[f, pl.ds(64 * zd, 64), :]

            return 0

        lax.fori_loop(0, 4, attend, 0)

        if f == 0:
            for j in range(3):
                for t in range(3):
                    row, q = weight_piece(j, t)
                    wait = functools.partial(landed, wbuf.at[q, y, x], wz_r.at[j, t])
                    if t < 2:
                        wait()
                    else:
                        pl.when(row < 36)(wait)
            for k in range(1, 4):
                to_x = (x + k) % 4
                to_y = (y + k) % 4
                piece = wbuf.at[0:4, y, x]
                remote(piece, piece, wp_s.at[0, k], wp_r.at[0, k], on_plane(4 * y + to_x)).start()
                piece = wbuf.at[4:7, y, x]
                remote(piece, piece, wp_s.at[1, k], wp_r.at[1, k], on_plane(4 * to_y + x)).start()
            piece = lats.at[(1 - zh) * 2 + c]
            landed(piece, lat_s.at[1])
            remote(piece, piece, lat_s.at[2], lat_s.at[3], sib).start()

    for k in range(1, 4):
        from_x = (x + 4 - k) % 4
        from_y = (y + 4 - k) % 4
        landed(wbuf.at[0:4, y, from_x], wp_r.at[0, k])
        landed(wbuf.at[4:7, from_y, x], wp_r.at[1, k])
    for k in range(1, 4):
        to_x = (x + k) % 4
        to_y = (y + k) % 4
        piece = wbuf.at[0:4, y]
        remote(piece, piece, wp_s.at[2, k], wp_r.at[2, k], on_plane(4 * to_y + x)).start()
        piece = wbuf.at[4:7, :, x]
        remote(piece, piece, wp_s.at[3, k], wp_r.at[3, k], on_plane(4 * y + to_x)).start()

    for k, hop in enumerate([RING - 1, 1, 2]):
        piece = wos.at[(h + hop) % 4, wo_rows]
        landed(piece, wo_r.at[k])
        remote(piece, piece, wo_s.at[3 + k], wo_r.at[3 + k], sib).start()
    wos[h] = wo[...]
    lats[pl.ds(zh * 2, 2)] = lat[:, pl.ds(64 * z, 64), :]
    landed(lats.at[(1 - zh) * 2 + (1 - c)], lat_s.at[3])
    for k, hop in enumerate([RING - 1, 1, 2]):
        landed(wos.at[(h + hop) % 4, pl.ds(PAIR * (1 - c), PAIR)], wo_r.at[3 + k])

    def take_heads(k, _):
        zz = (z + k) % RING
        for f in range(2):
            landed(heads.at[zz % 4, (zz // 4) * 2 + f], za_r.at[f, zz])
        return 0

    lax.fori_loop(1, RING, take_heads, 0)

    gate1 = mod[2:3, :]
    order = jnp.where(iota((256, 256), 1) == (iota((256, 256), 0) % 4) * 64 + iota((256, 256), 0) // 4, 1.0, 0.0).astype(BF)
    for n in range(3):
        cols = slice(384 * n, 384 * (n + 1))
        total = jnp.zeros((256, 384), F32)
        for g in range(4):
            total = total + dot(heads[g].reshape(256, 384)[:, 0:LOCAL], wos[g, :, cols])
        after = lats[:, :, cols].reshape(256, 384).astype(F32) + gate1[:, cols] * total.astype(BF).astype(F32)
        xs[:, :, cols] = dot(order, after.astype(BF)).astype(BF).reshape(PLANE, 16, 384)

    def give(k, _):
        to = (i + k) % PLANE
        remote(xs.at[to], xt.at[0, i], xy_s.at[to], xy_r.at[i], on_plane(to)).start()
        return 0

    lax.fori_loop(1, PLANE, give, 0)
    xt[0, i] = xs[i]
    remote(xs.at[i], xt.at[1, i], sb_s.at[i], sb_r.at[i], sib).start()

    def pass_on(k, _):
        source = (i + PLANE - k) % PLANE
        piece = xt.at[0, source]
        landed(piece, xy_r.at[source])
        remote(piece, xt.at[1, source], sb_s.at[source], sb_r.at[source], sib).start()
        return 0

    lax.fori_loop(1, PLANE, pass_on, 0)
    xn[0:256, :] = modulated(xt[0].reshape(256, WIDTH), mod[3:4, :], mod[4:5, :])

    def take_sibling(k, _):
        landed(xt.at[1, k], sb_r.at[k])
        return 0

    lax.fori_loop(0, PLANE, take_sibling, 0)
    mod_copy.wait()
    xn[256:512, :] = modulated(xt[1].reshape(256, WIDTH), modx[3:4, :], modx[4:5, :])

    for k in range(1, 4):
        from_x = (x + 4 - k) % 4
        from_y = (y + 4 - k) % 4
        landed(wbuf.at[0:4, from_y], wp_r.at[2, k])
        landed(wbuf.at[4:7, :, from_x], wp_r.at[3, k])

    def weight_rows(slot, first, count):
        if slot == 0:
            return wt[first * 16 : (first + count) * 16, :]
        flat = 36 * (slot - 1) + first
        return jnp.concatenate([wbuf[p // 16, (p % 16) // 4, p % 4] for p in range(flat, flat + count)], axis=0)

    pair_masks = [head_mask(n, PAIR) for n in range(2)]
    for slot in range(4):
        values = xn[...]
        query = dot_t(values, weight_rows(slot, 0, 9)).astype(BF)
        keys = dot_t(values, weight_rows(slot, 9, 9)).astype(BF)
        vals = dot_t(values, weight_rows(slot, 18, 9)).astype(BF)
        for b in range(2):
            rows = slice(256 * b, 256 * (b + 1))
            stacked = jnp.concatenate([query[rows] * m.astype(BF) for m in pair_masks], axis=0)
            scores = dot_t(stacked, keys[rows]) + jnp.concatenate([tbias[...]] * 2, axis=0)
            mixed = dot(softmax(scores), vals[rows])
            os_[slot, rows, :] = (mixed[0:256] * pair_masks[0] + mixed[256:512] * pair_masks[1]).astype(BF)

    def share(first):
        total = jnp.zeros((512, 640), F32)
        for slot in range(4):
            if slot == 0:
                weights = wt[27 * 16 : 36 * 16, pl.ds(first, 640)]
            else:
                flat = 36 * (slot - 1) + 27
                weights = jnp.concatenate(
                    [wbuf[p // 16, (p % 16) // 4, p % 4, :, pl.ds(first, 640)] for p in range(flat, flat + 9)], axis=0
                )
            total = total + dot(os_[slot], weights)
        return total

    theirs = pl.multiple_of(512 * (1 - c), 128)
    mine = pl.multiple_of(512 * c, 128)
    psend[...] = share(theirs).astype(BF)
    give_share = remote(psend, precv, pp_s.at[0], pp_s.at[1], sib)
    give_share.start()
    own = share(mine)
    give_share.wait()
    results = []
    for b in range(2):
        gate = (mod if b == 0 else modx)[5:6, pl.ds(mine, 640)]
        other = precv[256 * (1 - b) : 256 * (2 - b), :]
        total = (own[256 * b : 256 * (b + 1)] + other.astype(F32)).astype(BF).astype(F32)
        before = xt[b, :, :, pl.ds(mine, 640)].reshape(256, 640).astype(F32)
        results.append((before + gate * total).astype(BF).astype(F32))
    cond = jnp.where(c == 0, results[0], results[1])
    uncond = jnp.where(c == 0, results[1], results[0])
    guided = (uncond + GUIDE * (cond - uncond)).astype(BF)
    guided = jnp.where(c == 0, guided[:, 0:HALF], guided[:, 64 : 64 + HALF])
    gs[...] = guided.reshape(PLANE, 16, HALF)

    def back(k, _):
        to = (i + k) % PLANE
        remote(gs.at[to], g2.at[i], r1_s.at[to], r1_r.at[i], on_plane(to)).start()
        return 0

    lax.fori_loop(1, PLANE, back, 0)
    g2[i] = gs[i]

    def take_back(k, _):
        source = (i + PLANE - k) % PLANE
        landed(g2.at[source], r1_r.at[source])
        return 0

    lax.fori_loop(1, PLANE, take_back, 0)
    order = jnp.where(iota((256, 256), 1) == (iota((256, 256), 0) % 64) * 4 + iota((256, 256), 0) // 64, 1.0, 0.0).astype(BF)
    gz[...] = dot(order, g2[...].reshape(256, HALF)).astype(BF).reshape(4, 64, HALF)

    def spread(k, _):
        zd = (z + k) % RING
        place = out.at[:, pl.ds(64 * z, 64)]
        remote(gz.at[pl.ds((zd // 4) * 2, 2)], place, r2_s.at[zd], r2_r.at[z], on_z(zd)).start()
        return 0

    lax.fori_loop(1, RING, spread, 0)
    out[:, pl.ds(64 * z, 64), :] = gz[pl.ds(2 * zh, 2)]

    def take_last(k, _):
        zz = (z + k) % RING
        landed(out.at[:, pl.ds(64 * zz, 64)], r2_r.at[zz])
        return 0

    lax.fori_loop(1, RING, take_last, 0)

    for j in range(3):
        for t in range(3):
            row, q = weight_piece(j, t)
            wait = functools.partial(sent, wt.at[pl.ds(row * GROUP, GROUP)], wz_s.at[j, t])
            if t < 2:
                wait()
            else:
                pl.when(row < 36)(wait)
    lat_out.wait_send()
    sent(lats.at[0], lat_s.at[2])
    for k in range(6):
        sent(wo.at[wo_rows], wo_s.at[k])
    for k in range(1, 4):
        sent(wbuf.at[0:4, y, x], wp_s.at[0, k])
        sent(wbuf.at[4:7, y, x], wp_s.at[1, k])
        sent(wbuf.at[0:4, y], wp_s.at[2, k])
        sent(wbuf.at[4:7, :, x], wp_s.at[3, k])

    def done_z(k, _):
        zz = (z + k) % RING
        for f in range(2):
            sent(att.at[f, pl.ds(64 * zz, 64)], za_s.at[f, zz])
        sent(gz.at[0:2], r2_s.at[zz])
        return 0

    lax.fori_loop(1, RING, done_z, 0)

    def done_plane(k, _):
        ii = (i + k) % PLANE
        sent(xs.at[ii], xy_s.at[ii])
        sent(gs.at[ii], r1_s.at[ii])
        return 0

    lax.fori_loop(1, PLANE, done_plane, 0)

    def done_sibling(k, _):
        sent(xt.at[0, k], sb_s.at[k])
        return 0

    lax.fori_loop(0, PLANE, done_sibling, 0)


def shards(
    latent,
    modulation,
    w_qkv_space,
    w_out_space,
    w_qkv_time,
    w_out_time,
    clip_frames,
    spatial_window,
):
    c = lax.axis_index("cfg")
    lat = latent.reshape(2, POSITIONS, WIDTH)
    wsp = jnp.transpose(w_qkv_space, (1, 0, 2))
    half = lax.dynamic_slice_in_dim(w_qkv_time, c * PAIR, PAIR, 2)
    wt = jnp.concatenate(
        [
            jnp.transpose(half, (1, 2, 0)).reshape(3 * PAIR, WIDTH),
            lax.dynamic_slice_in_dim(w_out_time, c * PAIR, PAIR, 0),
        ],
        axis=0,
    )
    dma = pltpu.SemaphoreType.DMA
    vmem = pl.BlockSpec(memory_space=pltpu.VMEM)
    smem = pl.BlockSpec(memory_space=pltpu.SMEM)
    out = pl.pallas_call(
        kernel,
        out_shape=jax.ShapeDtypeStruct((2, POSITIONS, HALF), BF),
        in_specs=[smem, smem] + [vmem] * 5,
        out_specs=vmem,
        scratch_shapes=[
            pltpu.VMEM((6, WIDTH), F32),
            pltpu.VMEM((8, 128), BF),
            pltpu.VMEM((POSITIONS, 384), BF),
            pltpu.VMEM((PAD + POSITIONS + PAD, 384), BF),
            pltpu.VMEM((PAD + POSITIONS + PAD, 384), BF),
            pltpu.VMEM((128, 384), F32),
            pltpu.VMEM((2, POSITIONS, 384), BF),
            pltpu.VMEM((4, 4, 64, 384), BF),
            pltpu.VMEM((4, LOCAL, WIDTH), BF),
            pltpu.VMEM((4, 64, WIDTH), BF),
            pltpu.VMEM((PLANE, 16, WIDTH), BF),
            pltpu.VMEM((2, PLANE, 16, WIDTH), BF),
            pltpu.VMEM((7, 4, 4, GROUP, WIDTH), BF),
            pltpu.VMEM((256, 256), F32),
            pltpu.VMEM((512, WIDTH), BF),
            pltpu.VMEM((4, 512, PAIR), BF),
            pltpu.VMEM((512, 640), BF),
            pltpu.VMEM((512, 640), BF),
            pltpu.VMEM((PLANE, 16, HALF), BF),
            pltpu.VMEM((PLANE, 16, HALF), BF),
            pltpu.VMEM((4, 64, HALF), BF),
            dma((2,)),
            dma((4,)),
            dma((6,)),
            dma((6,)),
            dma((3, 3)),
            dma((3, 3)),
            dma((4, 4)),
            dma((4, 4)),
            dma((2, RING)),
            dma((2, RING)),
            dma((PLANE,)),
            dma((PLANE,)),
            dma((PLANE,)),
            dma((PLANE,)),
            dma((2,)),
            dma((PLANE,)),
            dma((PLANE,)),
            dma((RING,)),
            dma((RING,)),
        ],
        compiler_params=pltpu.CompilerParams(
            collective_id=0, has_side_effects=True, vmem_limit_bytes=56 * 1024 * 1024
        ),
        name="sublayers",
    )(spatial_window, clip_frames, lat, modulation[0], wsp, w_out_space, wt)
    return out.reshape(2 * POSITIONS, HALF)


def solution(mesh):
    return jax.shard_map(
        shards,
        mesh=mesh,
        in_specs=(
            P("seq", None),
            P("cfg", None, None),
            P(None, None, "head"),
            P("head", None),
            P(None, None, "head"),
            P("head", None),
            P(),
            P(),
        ),
        out_specs=P("seq", "cfg"),
        check_vma=False,
    )
```

```python
import functools

import jax
import jax.numpy as jnp
from jax import lax
from jax.experimental import pallas as pl
from jax.experimental.pallas import tpu as pltpu
from jax.sharding import PartitionSpec as P

MESH = pl.DeviceIdType.MESH
HEAD_DIM = 72
POSITIONS = 512
WIDTH = 1152
HALF = 576
LOCAL = 288
PAIR = 144
TWIN = 16
GUIDE = 4.0
EPSILON = 1e-06
NEG = -1e30
PAD = 128
RING = 8
PLANE = 16
GROUP = 16
EXP_SCALE = HEAD_DIM ** (-0.5) * 1.4426950408889634
BF = jnp.bfloat16
F32 = jnp.float32


def iota(shape, dim):
    return lax.broadcasted_iota(jnp.int32, shape, dim)


def modulated(rows, shift, scale):
    values = rows.astype(F32)
    centred = values - jnp.mean(values, axis=-1, keepdims=True)
    spread = jnp.mean(centred * centred, axis=-1, keepdims=True)
    normed = centred * lax.rsqrt(spread + EPSILON)
    return (normed * (1.0 + scale) + shift).astype(BF)


def softmax(scores):
    top = jnp.max(scores, axis=-1, keepdims=True)
    terms = jnp.exp2((scores - top) * EXP_SCALE)
    return (terms * (1.0 / jnp.sum(terms, axis=-1, keepdims=True))).astype(BF)


def dot(a, b):
    return lax.dot_general(a, b, (((1,), (0,)), ((), ())), preferred_element_type=F32)


def dot_t(a, b):
    return lax.dot_general(a, b, (((1,), (1,)), ((), ())), preferred_element_type=F32)


def head_mask(head, lanes):
    lane = iota((1, lanes), 1)
    return jnp.where((lane >= head * HEAD_DIM) & (lane < (head + 1) * HEAD_DIM), 1.0, 0.0)


def frame_window(frame, clip_ref):
    ends = [clip_ref[0]]
    for j in range(1, 4):
        ends.append(ends[-1] + clip_ref[j])
    clip = jnp.zeros_like(frame)
    start = jnp.zeros_like(frame)
    for end in ends:
        clip = clip + jnp.where(frame >= end, 1, 0)
        start = jnp.where(frame >= end, end, start)
    return clip * 64 + (frame - start) // TWIN


def kernel(
    sw_ref, clip_ref, lat, mod, wsp, wo, wt, out,
    modx, qs, ks, vs, base, att, packed, heads, wsib, wos, lats, xs, xt, wbuf, tbias, xn, os_, psend, precv, gs, g2, gz, tr,
    mod_s, lat_s, wz_s, wz_r, wp_s, wp_r, za_s, za_r, xy_s, xy_r, sb_s, sb_r, pp_s, r1_s, r1_r, r2_s, r2_r,
):
    c = lax.axis_index("cfg")
    s = lax.axis_index("seq")
    h = lax.axis_index("head")
    zh = s // PLANE
    i = s % PLANE
    y = i // 4
    x = i % 4
    z = zh * 4 + h

    def on_z(zz):
        return (c, (zz // 4) * PLANE + i, zz % 4)

    def on_plane(ii):
        return (c, zh * PLANE + ii, h)

    sib = (1 - c, s, h)

    def remote(src, dst, send, recv, dev):
        return pltpu.make_async_remote_copy(
            src_ref=src, dst_ref=dst, send_sem=send, recv_sem=recv, device_id=dev, device_id_type=MESH
        )

    def landed(buf, recv):
        remote(buf, buf, recv, recv, sib).wait_recv()

    def sent(buf, send):
        remote(buf, buf, send, send, sib).wait_send()

    barrier = pltpu.get_barrier_semaphore()

    def greet_z(k, _):
        pl.semaphore_signal(barrier, inc=1, device_id=on_z((z + k) % RING), device_id_type=MESH)
        return 0

    def greet_plane(k, _):
        pl.semaphore_signal(barrier, inc=1, device_id=on_plane((i + k) % PLANE), device_id_type=MESH)
        return 0

    lax.fori_loop(1, RING, greet_z, 0)
    lax.fori_loop(1, PLANE, greet_plane, 0)
    pl.semaphore_signal(barrier, inc=1, device_id=sib, device_id_type=MESH)
    pl.semaphore_wait(barrier, RING - 1 + PLANE - 1 + 1)

    far = jnp.where(c == 0, 2, RING - 2)
    hops = [RING - 1, far, 1]

    def piece_of(j, t):
        if t == 0:
            row = (i + 7 * j) % GROUP
            return row, (9 * j + row) // 16, row < 9
        row = (i + 12 * j) % GROUP + 16 * (t - 1)
        return 9 + row, 2 + (36 * j + row) // 16, row < 36

    def each_piece(step, act):
        for j in range(3):
            for t in step:
                row, q, there = piece_of(j, t)
                pl.when(there)(functools.partial(act, j, t, row, q))

    def start_piece(j, t, row, q):
        remote(
            wt.at[pl.ds(row * GROUP, GROUP)], wbuf.at[q, y, x], wz_s.at[j, t], wz_r.at[j, t], on_z((z + hops[j]) % RING)
        ).start()

    def take_piece(j, t, row, q):
        landed(wbuf.at[q, y, x], wz_r.at[j, t])

    def sent_piece(j, t, row, q):
        sent(wt.at[pl.ds(row * GROUP, GROUP)], wz_s.at[j, t])

    each_piece([0], start_piece)
    each_piece([1, 2, 3], start_piece)

    pushed = []

    def push(index, ref, dev):
        remote(ref, ref, wp_s.at[index], wp_r.at[index], dev).start()
        pushed.append((ref, index))

    def first_phase(index, cut_a, cut_b):
        for k in range(1, 4):
            push(index + k - 1, wbuf.at[cut_a, y, x], on_plane(4 * y + (x + k) % 4))
            push(index + k + 2, wbuf.at[cut_b, y, x], on_plane(4 * ((y + k) % 4) + x))

    def first_landed(index, cut_a, cut_b):
        for k in range(1, 4):
            landed(wbuf.at[cut_a, y, (x + 4 - k) % 4], wp_r.at[index + k - 1])
            landed(wbuf.at[cut_b, (y + 4 - k) % 4, x], wp_r.at[index + k + 2])

    def second_phase(index, cut_a, cut_b, ks_):
        for k in ks_:
            push(index + k - 1, wbuf.at[cut_a, y], on_plane(4 * ((y + k) % 4) + x))
            push(index + k + 2, wbuf.at[cut_b, :, x], on_plane(4 * y + (x + k) % 4))

    def second_landed(index, cut_a, cut_b, ks_):
        for k in ks_:
            landed(wbuf.at[cut_a, (y + 4 - k) % 4], wp_r.at[index + k - 1])
            landed(wbuf.at[cut_b, :, (x + 4 - k) % 4], wp_r.at[index + k + 2])

    space_a, space_b = slice(0, 1), slice(1, 2)
    time_a, time_b = slice(2, 6), slice(6, 9)

    mod_copy = remote(mod, modx, mod_s.at[0], mod_s.at[1], sib)
    mod_copy.start()
    lat_out = remote(
        lat.at[c, pl.ds(64 * (7 - z), 64)], lats.at[zh * 2 + c], lat_s.at[0], lat_s.at[1], on_z(7 - z)
    )
    lat_out.start()
    oy = jnp.int32(7)
    ox = jnp.int32(7)
    for r in range(1, 8):
        oy = oy - jnp.where(sw_ref[16 * r] < 3, 1, 0)
        ox = ox - jnp.where(sw_ref[r] < 1, 1, 0)
    qj = iota((128, 384), 0)
    ki = iota((128, 384), 1)
    same = ((qj // 16 + 8 + oy) // 8 == (ki // 16 + oy) // 8) & ((qj % 16 + ox) // 8 == (ki % 16 + ox) // 8)
    base[...] = jnp.where(same, 0.0, NEG)

    def time_key(row):
        four = row % 4
        frame = (four // 2) * 32 + 2 * (row // 16) + four % 2
        return frame_window(frame, clip_ref) * 4 + (row % 16) // 4

    tbias[...] = jnp.where(time_key(iota((256, 1), 0)) == time_key(iota((1, 256), 1)), 0.0, NEG)

    for ref in (ks, vs):
        ref[0:PAD, :] = jnp.zeros((PAD, 384), BF)
        ref[PAD + POSITIONS :, :] = jnp.zeros((PAD, 384), BF)
        ref[PAD : PAD + POSITIONS, 256:384] = jnp.zeros((POSITIONS, 128), BF)
    qs[:, 256:384] = jnp.zeros((POSITIONS, 128), BF)

    shift1, scale1 = mod[0:1, :], mod[1:2, :]
    masks = [head_mask(n, 384) for n in range(4)]

    for f in range(2):

        def project(rb, _):
            rows = pl.ds(rb * 256, 256)
            values = modulated(lat[f, rows, :], shift1, scale1)
            qs[rows, 0:LOCAL] = dot_t(values, wsp[0]).astype(BF)
            ks[pl.ds(PAD + rb * 256, 256), 0:LOCAL] = dot_t(values, wsp[1]).astype(BF)
            vs[pl.ds(PAD + rb * 256, 256), 0:LOCAL] = dot_t(values, wsp[2]).astype(BF)
            return 0

        lax.fori_loop(0, 2, project, 0)
        if f == 0:
            each_piece([0], take_piece)
            first_phase(0, space_a, space_b)

        def attend(k, _):
            query = qs[pl.ds(k * 128, 128), :]
            stacked = jnp.concatenate([query * m.astype(BF) for m in masks], axis=0)
            keys = ks[pl.ds(k * 128, 384), :]
            vals = vs[pl.ds(k * 128, 384), :]
            row = 8 * k - 8 + iota((1, 384), 1) // 16
            bias = base[...] + jnp.where((row >= 0) & (row < 32), 0.0, NEG)
            scores = dot_t(stacked, keys) + jnp.concatenate([bias] * 4, axis=0)
            mixed = dot(softmax(scores), vals)
            total = mixed[0:128] * masks[0]
            for n in range(1, 4):
                total = total + mixed[128 * n : 128 * (n + 1)] * masks[n]
            for t in range(2):
                zd = 2 * k + t
                part = total[64 * t : 64 * (t + 1)]
                rest = part[0:16, 256:384]
                for r in range(1, 4):
                    rest = rest + pltpu.roll(part[16 * r : 16 * (r + 1), 256:384], 32 * r, 1)
                whole = jnp.concatenate([part[:, 0:128], part[:, 128:256], rest], axis=0)
                att[f, zd] = whole.astype(BF)
                copy = remote(att.at[f, zd], packed.at[h, zh * 2 + f], za_s.at[f, zd], za_r.at[f, z], on_z(zd))
                pl.when(zd != z)(copy.start)

                @pl.when(zd == z)
                def _():
                    packed[h, zh * 2 + f] = att[f, zd]

            return 0

        lax.fori_loop(0, 4, attend, 0)

        if f == 0:
            each_piece([1, 2, 3], take_piece)
            first_phase(6, time_a, time_b)
            first_landed(0, space_a, space_b)
            second_phase(12, space_a, space_b, (1, 2, 3))
            piece = lats.at[(1 - zh) * 2 + c]
            landed(piece, lat_s.at[1])
            remote(piece, piece, lat_s.at[2], lat_s.at[3], sib).start()

    first_landed(6, time_a, time_b)
    second_phase(18, time_a, time_b, (1, 3))
    second_landed(12, space_a, space_b, (1, 2, 3))
    remote(wbuf.at[0:2], wsib, wp_s.at[32], wp_r.at[32], sib).start()
    wos[h] = wo[...]
    lats[pl.ds(zh * 2, 2)] = lat[:, pl.ds(64 * z, 64), :]
    landed(lats.at[(1 - zh) * 2 + (1 - c)], lat_s.at[3])
    landed(wsib, wp_r.at[32])
    for p in range(27):
        shard, row = (h + 1 + p // 9) % 4, 16 * (p % 9)
        place = (p // 16, (p % 16) // 4, p % 4)
        wos[shard, pl.ds(PAIR * c + row, 16), :] = wbuf[place]
        wos[shard, pl.ds(PAIR * (1 - c) + row, 16), :] = wsib[place]

    def take_heads(k, _):
        zz = (z + k) % RING
        for f in range(2):
            landed(packed.at[zz % 4, (zz // 4) * 2 + f], za_r.at[f, zz])
        return 0

    lax.fori_loop(1, RING, take_heads, 0)

    def unpack(k, _):
        block = packed[k // 4, k % 4]
        heads[k // 4, k % 4, :, 0:128] = block[0:64]
        heads[k // 4, k % 4, :, 128:256] = block[64:128]
        rest = block[128:144].astype(F32)
        parts = [rest] + [pltpu.roll(rest, 128 - 32 * r, 1) for r in range(1, 4)]
        heads[k // 4, k % 4, :, 256:384] = jnp.concatenate(parts, axis=0).astype(BF)
        return 0

    lax.fori_loop(0, 16, unpack, 0)

    gate1 = mod[2:3, :]
    order = jnp.where(iota((256, 256), 1) == (iota((256, 256), 0) % 4) * 64 + iota((256, 256), 0) // 4, 1.0, 0.0).astype(BF)
    for n in range(3):
        cols = slice(384 * n, 384 * (n + 1))
        total = jnp.zeros((256, 384), F32)
        for g in range(4):
            total = total + dot(heads[g].reshape(256, 384)[:, 0:LOCAL], wos[g, :, cols])
        after = lats[:, :, cols].reshape(256, 384).astype(F32) + gate1[:, cols] * total.astype(BF).astype(F32)
        xs[:, :, cols] = dot(order, after.astype(BF)).astype(BF).reshape(PLANE, 16, 384)

    def give(k, _):
        to = (i + k) % PLANE
        remote(xs.at[to], xt.at[0, i], xy_s.at[to], xy_r.at[i], on_plane(to)).start()
        return 0

    lax.fori_loop(1, PLANE, give, 0)
    second_landed(18, time_a, time_b, (1, 3))
    push(24, wbuf.at[2:4, (y + 3) % 4], on_plane(4 * ((y + 1) % 4) + x))
    push(25, wbuf.at[4:6, (y + 1) % 4], on_plane(4 * ((y + 3) % 4) + x))
    push(26, wbuf.at[6:7, :, (x + 3) % 4], on_plane(4 * y + (x + 1) % 4))
    push(27, wbuf.at[7:9, :, (x + 1) % 4], on_plane(4 * y + (x + 3) % 4))
    xt[0, i] = xs[i]
    remote(xs.at[i], xt.at[1, i], sb_s.at[i], sb_r.at[i], sib).start()

    def pass_on(k, _):
        source = (i + PLANE - k) % PLANE
        piece = xt.at[0, source]
        landed(piece, xy_r.at[source])
        remote(piece, xt.at[1, source], sb_s.at[source], sb_r.at[source], sib).start()
        return 0

    lax.fori_loop(1, PLANE, pass_on, 0)
    xn[0:256, :] = modulated(xt[0].reshape(256, WIDTH), mod[3:4, :], mod[4:5, :])

    def take_sibling(k, _):
        landed(xt.at[1, k], sb_r.at[k])
        return 0

    lax.fori_loop(0, PLANE, take_sibling, 0)
    mod_copy.wait()
    xn[256:512, :] = modulated(xt[1].reshape(256, WIDTH), modx[3:4, :], modx[4:5, :])

    landed(wbuf.at[2:4, (y + 2) % 4], wp_r.at[24])
    landed(wbuf.at[4:6, (y + 2) % 4], wp_r.at[25])
    landed(wbuf.at[6:7, :, (x + 2) % 4], wp_r.at[26])
    landed(wbuf.at[7:9, :, (x + 2) % 4], wp_r.at[27])

    def at_flat(flat):
        return 2 + flat // 16, (flat % 16) // 4, flat % 4

    def weight_rows(slot, first, count):
        if slot == 0:
            return wt[(9 + first) * 16 : (9 + first + count) * 16, :]
        flat = 36 * (slot - 1) + first
        return jnp.concatenate([wbuf[at_flat(p)] for p in range(flat, flat + count)], axis=0)

    pair_masks = [head_mask(n, PAIR) for n in range(2)]
    for slot in range(4):
        values = xn[...]
        query = dot_t(values, weight_rows(slot, 0, 9)).astype(BF)
        keys = dot_t(values, weight_rows(slot, 9, 9)).astype(BF)
        vals = dot_t(values, weight_rows(slot, 18, 9)).astype(BF)
        for b in range(2):
            rows = slice(256 * b, 256 * (b + 1))
            stacked = jnp.concatenate([query[rows] * m.astype(BF) for m in pair_masks], axis=0)
            scores = dot_t(stacked, keys[rows]) + jnp.concatenate([tbias[...]] * 2, axis=0)
            mixed = dot(softmax(scores), vals[rows])
            os_[slot, rows, :] = (mixed[0:256] * pair_masks[0] + mixed[256:512] * pair_masks[1]).astype(BF)

    def share(first):
        total = jnp.zeros((512, 640), F32)
        for slot in range(4):
            if slot == 0:
                weights = wt[36 * 16 : 45 * 16, pl.ds(first, 640)]
            else:
                flat = 36 * (slot - 1) + 27
                weights = jnp.concatenate(
                    [wbuf[at_flat(p) + (slice(None), pl.ds(first, 640))] for p in range(flat, flat + 9)], axis=0
                )
            total = total + dot(os_[slot], weights)
        return total

    theirs = pl.multiple_of(512 * (1 - c), 128)
    mine = pl.multiple_of(512 * c, 128)
    psend[...] = share(theirs).astype(BF)
    give_share = remote(psend, precv, pp_s.at[0], pp_s.at[1], sib)
    give_share.start()
    own = share(mine)
    give_share.wait()
    results = []
    for b in range(2):
        gate = (mod if b == 0 else modx)[5:6, pl.ds(mine, 640)]
        other = precv[256 * (1 - b) : 256 * (2 - b), :]
        total = (own[256 * b : 256 * (b + 1)] + other.astype(F32)).astype(BF).astype(F32)
        before = xt[b, :, :, pl.ds(mine, 640)].reshape(256, 640).astype(F32)
        results.append((before + gate * total).astype(BF).astype(F32))
    cond = jnp.where(c == 0, results[0], results[1])
    uncond = jnp.where(c == 0, results[1], results[0])
    guided = (uncond + GUIDE * (cond - uncond)).astype(BF)
    guided = jnp.where(c == 0, guided[:, 0:HALF], guided[:, 64 : 64 + HALF])
    gs[...] = guided.reshape(PLANE, 16, HALF)

    def back(k, _):
        to = (i + k) % PLANE
        remote(gs.at[to], g2.at[i], r1_s.at[to], r1_r.at[i], on_plane(to)).start()
        return 0

    lax.fori_loop(1, PLANE, back, 0)
    g2[i] = gs[i]

    def take_back(k, _):
        source = (i + PLANE - k) % PLANE
        landed(g2.at[source], r1_r.at[source])
        return 0

    lax.fori_loop(1, PLANE, take_back, 0)
    order = jnp.where(iota((256, 256), 1) == (iota((256, 256), 0) % 64) * 4 + iota((256, 256), 0) // 64, 1.0, 0.0).astype(BF)
    gz[...] = dot(order, g2[...].reshape(256, HALF)).astype(BF).reshape(4, 64, HALF)

    left, right = on_z((z + RING - 1) % RING), on_z((z + 1) % RING)
    own_block, other_block = gz.at[pl.ds(2 * zh, 2)], gz.at[pl.ds(2 * (1 - zh), 2)]

    def slot(zz):
        return out.at[:, pl.ds(64 * zz, 64)]

    def inner(hh):
        return zh * 4 + hh

    def outer(hh):
        return (1 - zh) * 4 + hh

    out[:, pl.ds(64 * z, 64), :] = gz[pl.ds(2 * zh, 2)]
    for role in range(4):

        @pl.when(h == role)
        def _():
            waits = []

            def go(side, src, zz, index, transit=False):
                dst = tr if transit else slot(zz)
                recv = r2_r.at[RING] if transit else r2_r.at[zz]
                remote(src, dst, r2_s.at[side, index], recv, [left, right][side]).start()
                waits.append((side, index))

            def event(side, zz, forward):
                landed(slot(zz), r2_r.at[zz])
                if forward:
                    go(side, slot(zz), zz, zz)

            if role < 2:
                go(0, other_block, z, RING, transit=role == 1)
            else:
                go(1, other_block, z, RING, transit=role == 2)
            if role > 0:
                go(0, own_block, z, z)
            if role < 3:
                go(1, own_block, z, z)
            if role in (0, 3):
                landed(tr, r2_r.at[RING])
                source = inner(1 if role == 0 else 2)
                go(0 if role == 0 else 1, tr, source, source)
            lefts = [inner(k) for k in range(role + 1, 4)] + [outer(0), outer(1)]
            rights = [inner(k) for k in range(role - 1, -1, -1)] + [outer(3), outer(2)]
            for k in range(max(len(lefts), len(rights))):
                if k < len(lefts):
                    event(0, lefts[k], role > 0)
                if k < len(rights):
                    event(1, rights[k], role < 3)
            for side, index in waits:
                sent(gz.at[0:2], r2_s.at[side, index])

    each_piece([0, 1, 2, 3], sent_piece)
    lat_out.wait_send()
    sent(lats.at[0], lat_s.at[2])
    for ref, index in pushed:
        sent(ref, wp_s.at[index])
    sent(wsib, wp_s.at[32])

    def done_z(k, _):
        zz = (z + k) % RING
        for f in range(2):
            sent(att.at[f, zz], za_s.at[f, zz])
        return 0

    lax.fori_loop(1, RING, done_z, 0)

    def done_plane(k, _):
        ii = (i + k) % PLANE
        sent(xs.at[ii], xy_s.at[ii])
        sent(gs.at[ii], r1_s.at[ii])
        return 0

    lax.fori_loop(1, PLANE, done_plane, 0)

    def done_sibling(k, _):
        sent(xt.at[0, k], sb_s.at[k])
        return 0

    lax.fori_loop(0, PLANE, done_sibling, 0)


def shards(
    latent,
    modulation,
    w_qkv_space,
    w_out_space,
    w_qkv_time,
    w_out_time,
    clip_frames,
    spatial_window,
):
    c = lax.axis_index("cfg")
    lat = latent.reshape(2, POSITIONS, WIDTH)
    wsp = jnp.transpose(w_qkv_space, (1, 2, 0))
    half = lax.dynamic_slice_in_dim(w_qkv_time, c * PAIR, PAIR, 2)
    wt = jnp.concatenate(
        [
            lax.dynamic_slice_in_dim(w_out_space, c * PAIR, PAIR, 0),
            jnp.transpose(half, (1, 2, 0)).reshape(3 * PAIR, WIDTH),
            lax.dynamic_slice_in_dim(w_out_time, c * PAIR, PAIR, 0),
        ],
        axis=0,
    )
    dma = pltpu.SemaphoreType.DMA
    vmem = pl.BlockSpec(memory_space=pltpu.VMEM)
    smem = pl.BlockSpec(memory_space=pltpu.SMEM)
    out = pl.pallas_call(
        kernel,
        out_shape=jax.ShapeDtypeStruct((2, POSITIONS, HALF), BF),
        in_specs=[smem, smem] + [vmem] * 5,
        out_specs=vmem,
        scratch_shapes=[
            pltpu.VMEM((6, WIDTH), F32),
            pltpu.VMEM((POSITIONS, 384), BF),
            pltpu.VMEM((PAD + POSITIONS + PAD, 384), BF),
            pltpu.VMEM((PAD + POSITIONS + PAD, 384), BF),
            pltpu.VMEM((128, 384), F32),
            pltpu.VMEM((2, RING, 144, 128), BF),
            pltpu.VMEM((4, 4, 144, 128), BF),
            pltpu.VMEM((4, 4, 64, 384), BF),
            pltpu.VMEM((2, 4, 4, GROUP, WIDTH), BF),
            pltpu.VMEM((4, LOCAL, WIDTH), BF),
            pltpu.VMEM((4, 64, WIDTH), BF),
            pltpu.VMEM((PLANE, 16, WIDTH), BF),
            pltpu.VMEM((2, PLANE, 16, WIDTH), BF),
            pltpu.VMEM((9, 4, 4, GROUP, WIDTH), BF),
            pltpu.VMEM((256, 256), F32),
            pltpu.VMEM((512, WIDTH), BF),
            pltpu.VMEM((4, 512, PAIR), BF),
            pltpu.VMEM((512, 640), BF),
            pltpu.VMEM((512, 640), BF),
            pltpu.VMEM((PLANE, 16, HALF), BF),
            pltpu.VMEM((PLANE, 16, HALF), BF),
            pltpu.VMEM((4, 64, HALF), BF),
            pltpu.VMEM((2, 64, HALF), BF),
            dma((2,)),
            dma((4,)),
            dma((3, 4)),
            dma((3, 4)),
            dma((33,)),
            dma((33,)),
            dma((2, RING)),
            dma((2, RING)),
            dma((PLANE,)),
            dma((PLANE,)),
            dma((PLANE,)),
            dma((PLANE,)),
            dma((2,)),
            dma((PLANE,)),
            dma((PLANE,)),
            dma((2, RING + 1)),
            dma((RING + 1,)),
        ],
        compiler_params=pltpu.CompilerParams(
            collective_id=0, has_side_effects=True, vmem_limit_bytes=56 * 1024 * 1024
        ),
        name="sublayers",
    )(spatial_window, clip_frames, lat, modulation[0], wsp, w_out_space, wt)
    return out.reshape(2 * POSITIONS, HALF)


def solution(mesh):
    return jax.shard_map(
        shards,
        mesh=mesh,
        in_specs=(
            P("seq", None),
            P("cfg", None, None),
            P(None, None, "head"),
            P("head", None),
            P(None, None, "head"),
            P("head", None),
            P(),
            P(),
        ),
        out_specs=P("seq", "cfg"),
        check_vma=False,
    )
```

```python
import functools

import jax
import jax.numpy as jnp
from jax import lax
from jax.experimental import pallas as pl
from jax.experimental.pallas import tpu as pltpu
from jax.sharding import PartitionSpec as P

MESH = pl.DeviceIdType.MESH
HEAD_DIM = 72
POSITIONS = 512
WIDTH = 1152
HALF = 576
LOCAL = 288
PAIR = 144
TWIN = 16
GUIDE = 4.0
EPSILON = 1e-06
NEG = -1e30
PAD = 128
RING = 8
PLANE = 16
GROUP = 16
EXP_SCALE = HEAD_DIM ** (-0.5) * 1.4426950408889634
BF = jnp.bfloat16
F32 = jnp.float32


def iota(shape, dim):
    return lax.broadcasted_iota(jnp.int32, shape, dim)


def modulated(rows, shift, scale):
    values = rows.astype(F32)
    centred = values - jnp.mean(values, axis=-1, keepdims=True)
    spread = jnp.mean(centred * centred, axis=-1, keepdims=True)
    normed = centred * lax.rsqrt(spread + EPSILON)
    return (normed * (1.0 + scale) + shift).astype(BF)


def softmax_keys(scores):
    top = jnp.max(scores, axis=0, keepdims=True)
    terms = jnp.exp2((scores - top) * EXP_SCALE)
    return terms.astype(BF), 1.0 / jnp.sum(terms, axis=0, keepdims=True)


def dot(a, b):
    return lax.dot_general(a, b, (((1,), (0,)), ((), ())), preferred_element_type=F32)


def dot_t(a, b):
    return lax.dot_general(a, b, (((1,), (1,)), ((), ())), preferred_element_type=F32)


def dot_first(a, b):
    return lax.dot_general(a, b, (((0,), (0,)), ((), ())), preferred_element_type=F32)


def head_mask(head, first, rows):
    row = iota((rows, 1), 0) + first
    return jnp.where((row >= head * HEAD_DIM) & (row < (head + 1) * HEAD_DIM), 1.0, 0.0).astype(BF)


def frame_window(frame, clip_ref):
    ends = [clip_ref[0]]
    for j in range(1, 4):
        ends.append(ends[-1] + clip_ref[j])
    clip = jnp.zeros_like(frame)
    start = jnp.zeros_like(frame)
    for end in ends:
        clip = clip + jnp.where(frame >= end, 1, 0)
        start = jnp.where(frame >= end, end, start)
    return clip * 64 + (frame - start) // TWIN


def kernel(
    sw_ref, clip_ref, lat, mod, wsp, wo, wt, out,
    modx, qt, ks, vt, base, att, heads, wsib, wos, lats, xs, xt, wbuf, tbias, xn, ot, psend, precv, gs, g2, gz, tr,
    mod_s, lat_s, wz_s, wz_r, wp_s, wp_r, za_s, za_r, xy_s, xy_r, sb_s, sb_r, pp_s, r1_s, r1_r, r2_s, r2_r,
):
    c = lax.axis_index("cfg")
    s = lax.axis_index("seq")
    h = lax.axis_index("head")
    zh = s // PLANE
    i = s % PLANE
    y = i // 4
    x = i % 4
    z = zh * 4 + h

    def on_z(zz):
        return (c, (zz // 4) * PLANE + i, zz % 4)

    def on_plane(ii):
        return (c, zh * PLANE + ii, h)

    sib = (1 - c, s, h)
    left, right = on_z((z + RING - 1) % RING), on_z((z + 1) % RING)

    def remote(src, dst, send, recv, dev):
        return pltpu.make_async_remote_copy(
            src_ref=src, dst_ref=dst, send_sem=send, recv_sem=recv, device_id=dev, device_id_type=MESH
        )

    def landed(buf, recv):
        remote(buf, buf, recv, recv, sib).wait_recv()

    def sent(buf, send):
        remote(buf, buf, send, send, sib).wait_send()

    barrier = pltpu.get_barrier_semaphore()

    def greet_z(k, _):
        pl.semaphore_signal(barrier, inc=1, device_id=on_z((z + k) % RING), device_id_type=MESH)
        return 0

    def greet_plane(k, _):
        pl.semaphore_signal(barrier, inc=1, device_id=on_plane((i + k) % PLANE), device_id_type=MESH)
        return 0

    lax.fori_loop(1, RING, greet_z, 0)
    lax.fori_loop(1, PLANE, greet_plane, 0)
    pl.semaphore_signal(barrier, inc=1, device_id=sib, device_id_type=MESH)
    pl.semaphore_wait(barrier, RING - 1 + PLANE - 1 + 1)

    far = jnp.where(c == 0, 2, RING - 2)
    hops = [RING - 1, far, 1]
    index_a, index_b = 4 * y + x, 4 * x + y
    SPACE = [(0, index_a, 0, 9, [0, 1]), (1, index_b, 0, 9, [1, 2])]
    TIME = [
        (3, index_a, 2, 36, [0]),
        (4, index_a, 2, 36, [0, 1]),
        (5, index_a, 2, 36, [1]),
        (6, index_b, 2, 36, [1, 2]),
        (7, index_b, 2, 36, [2]),
    ]

    def each_sent(rows, act):
        for q, place, first, per, slots in rows:
            flat = 16 * (q - first) + place
            for j in slots:
                source = wt.at[(9 if per == 36 else 0) + flat - per * j]
                pl.when(flat // per == j)(functools.partial(act, q, place, j, source))

    def start_piece(q, place, j, source):
        remote(source, wbuf.at[q, place], wz_s.at[q, j], wz_r.at[q], on_z((z + hops[j]) % RING)).start()

    def sent_piece(q, place, j, source):
        sent(source, wz_s.at[q, j])

    def take_pieces(rows):
        for q, place, first, per, _ in rows:
            there = 16 * (q - first) + place < 3 * per
            pl.when(there)(functools.partial(landed, wbuf.at[q, place], wz_r.at[q]))

    each_sent(SPACE, start_piece)

    pushed = []

    def push(index, ref, dev):
        remote(ref, ref, wp_s.at[index], wp_r.at[index], dev).start()
        pushed.append((ref, index))

    def first_phase(index, cut_a, cut_b):
        for k in range(1, 4):
            push(index + k - 1, wbuf.at[cut_a, index_a], on_plane(4 * y + (x + k) % 4))
            push(index + k + 2, wbuf.at[cut_b, index_b], on_plane(4 * ((y + k) % 4) + x))

    def first_landed(index, cut_a, cut_b):
        for k in range(1, 4):
            landed(wbuf.at[cut_a, 4 * y + (x + 4 - k) % 4], wp_r.at[index + k - 1])
            landed(wbuf.at[cut_b, 4 * x + (y + 4 - k) % 4], wp_r.at[index + k + 2])

    def second_phase(index, cut_a, cut_b, steps):
        for k in steps:
            push(index + k - 1, wbuf.at[cut_a, pl.ds(4 * y, 4)], on_plane(4 * ((y + k) % 4) + x))
            push(index + k + 2, wbuf.at[cut_b, pl.ds(4 * x, 4)], on_plane(4 * y + (x + k) % 4))

    def second_landed(index, cut_a, cut_b, steps):
        for k in steps:
            landed(wbuf.at[cut_a, pl.ds(4 * ((y + 4 - k) % 4), 4)], wp_r.at[index + k - 1])
            landed(wbuf.at[cut_b, pl.ds(4 * ((x + 4 - k) % 4), 4)], wp_r.at[index + k + 2])

    space_a, space_b = slice(0, 1), slice(1, 2)
    time_a, time_b = slice(3, 6), slice(6, 8)

    mod_copy = remote(mod, modx, mod_s.at[0], mod_s.at[1], sib)
    mod_copy.start()
    lat_out = remote(
        lat.at[c, pl.ds(64 * (7 - z), 64)], lats.at[zh * 2 + c], lat_s.at[0], lat_s.at[1], on_z(7 - z)
    )
    oy = jnp.int32(7)
    ox = jnp.int32(7)
    for r in range(1, 8):
        oy = oy - jnp.where(sw_ref[16 * r] < 3, 1, 0)
        ox = ox - jnp.where(sw_ref[r] < 1, 1, 0)
    qj = iota((384, 128), 1)
    ki = iota((384, 128), 0)
    same = ((qj // 16 + 8 + oy) // 8 == (ki // 16 + oy) // 8) & ((qj % 16 + ox) // 8 == (ki % 16 + ox) // 8)
    base[...] = jnp.where(same, 0.0, NEG)

    def time_key(row):
        four = row % 4
        frame = (four // 2) * 32 + 2 * (row // 16) + four % 2
        return frame_window(frame, clip_ref) * 4 + (row % 16) // 4

    tbias[...] = jnp.where(time_key(iota((256, 1), 0)) == time_key(iota((1, 256), 1)), 0.0, NEG)

    for f in range(2):
        ks[f, 0:PAD, :] = jnp.zeros((PAD, 384), BF)
        ks[f, PAD + POSITIONS :, :] = jnp.zeros((PAD, 384), BF)
        ks[f, PAD : PAD + POSITIONS, 256:384] = jnp.zeros((POSITIONS, 128), BF)
        vt[f, :, 0:PAD] = jnp.zeros((LOCAL, PAD), BF)
        vt[f, :, PAD + POSITIONS :] = jnp.zeros((LOCAL, PAD), BF)
        qt[f, LOCAL:384, :] = jnp.zeros((384 - LOCAL, POSITIONS), BF)

    shift1, scale1 = mod[0:1, :], mod[1:2, :]
    masks = [head_mask(0, 0, 256), head_mask(1, 0, 256), head_mask(2, 0, 256), head_mask(3, 128, 256)]

    for f in range(2):
        for rb in range(2):
            rows = slice(rb * 256, (rb + 1) * 256)
            values = modulated(lat[f, rows, :], shift1, scale1)
            qt[f, 0:LOCAL, rows] = dot_t(wsp[0], values).astype(BF)
            ks[f, PAD + rb * 256 : PAD + (rb + 1) * 256, 0:LOCAL] = dot_t(values, wsp[1]).astype(BF)
            vt[f, :, PAD + rb * 256 : PAD + (rb + 1) * 256] = dot_t(wsp[2], values).astype(BF)
        if f == 0:
            take_pieces(SPACE)
            first_phase(0, space_a, space_b)
            each_sent(TIME, start_piece)
            lat_out.start()

    low = iota((1, 128), 1) < 64

    def attend(k, f):
        cols = pl.ds(pl.multiple_of(k * 128, 128), 128)
        around = pl.ds(pl.multiple_of(k * 128, 128), 384)
        keys = ks[f, around, :]
        query = qt[f, :, cols]
        three = jnp.concatenate([query[0:256] * m for m in masks[0:3]], axis=1)
        row = 8 * k - 8 + iota((384, 1), 0) // 16
        bias = base[...] + jnp.where((row >= 0) & (row < 32), 0.0, NEG)
        scores = jnp.concatenate(
            [dot(keys[:, 0:256], three), dot(keys[:, 128:384], query[128:384] * masks[3])], axis=1
        ) + jnp.concatenate([bias] * 4, axis=1)
        weights, over = softmax_keys(scores)
        mixed = dot(vt[f, :, around], weights)
        parts = [
            mixed[HEAD_DIM * n : HEAD_DIM * (n + 1), 128 * n : 128 * (n + 1)] * over[:, 128 * n : 128 * (n + 1)]
            for n in range(4)
        ]
        return jnp.concatenate(parts, axis=0)

    for step in range(2):
        for k in (2 * step, 2 * step + 1):
            first, second = attend(k, 0), attend(k, 1)
            att[2 * k] = jnp.where(low, first, pltpu.roll(second, 64, 1)).astype(BF)
            att[2 * k + 1] = jnp.where(low, pltpu.roll(first, 64, 1), second).astype(BF)
        for zd in range(4 * step, 4 * step + 4):
            place = heads.at[pl.ds(LOCAL * h, LOCAL), pl.ds(pl.multiple_of(128 * zh, 128), 128)]
            copy = remote(att.at[zd], place, za_s.at[zd], za_r.at[z], on_z(zd))
            pl.when(z != zd)(copy.start)

            @pl.when(z == zd)
            def _():
                heads[pl.ds(LOCAL * h, LOCAL), pl.ds(pl.multiple_of(128 * zh, 128), 128)] = att[zd]

        if step == 0:
            first_landed(0, space_a, space_b)
            second_phase(12, space_a, space_b, (1, 2, 3))
            take_pieces(TIME)
            first_phase(6, time_a, time_b)

    piece = lats.at[(1 - zh) * 2 + c]
    landed(piece, lat_s.at[1])
    remote(piece, piece, lat_s.at[2], lat_s.at[3], sib).start()
    first_landed(6, time_a, time_b)
    second_phase(18, time_a, time_b, (1, 3))
    second_landed(12, space_a, space_b, (1, 2, 3))
    remote(wbuf.at[0:2], wsib, wp_s.at[32], wp_r.at[32], sib).start()
    wos[h] = wo[...]
    lats[pl.ds(zh * 2, 2)] = lat[:, pl.ds(64 * z, 64), :]
    landed(lats.at[(1 - zh) * 2 + (1 - c)], lat_s.at[3])
    landed(wsib, wp_r.at[32])
    for p in range(27):
        shard, row = (h + 1 + p // 9) % 4, 16 * (p % 9)
        place = (p // 16, p % 16)
        wos[shard, pl.ds(PAIR * c + row, 16), :] = wbuf[place]
        wos[shard, pl.ds(PAIR * (1 - c) + row, 16), :] = wsib[place]

    def take_heads(k, _):
        zz = (z + k) % RING
        landed(heads.at[pl.ds(LOCAL * (zz % 4), LOCAL), pl.ds(pl.multiple_of(128 * (zz // 4), 128), 128)], za_r.at[zz])
        return 0

    lax.fori_loop(1, RING, take_heads, 0)

    straight = [
        remote(wt.at[9:25], wbuf.at[2], wp_s.at[28], wp_r.at[28], left),
        remote(wt.at[33:45], wbuf.at[8, 0:12], wp_s.at[29], wp_r.at[29], right),
    ]
    for copy in straight:
        copy.start()

    gate1 = mod[2:3, :]
    order = jnp.where(iota((256, 256), 1) == (iota((256, 256), 0) % 4) * 64 + iota((256, 256), 0) // 4, 1.0, 0.0).astype(BF)
    for n in range(3):
        cols = slice(384 * n, 384 * (n + 1))
        total = dot_first(heads[...], wos[:, :, cols].reshape(WIDTH, 384))
        after = lats[:, :, cols].reshape(256, 384).astype(F32) + gate1[:, cols] * total.astype(BF).astype(F32)
        xs[:, :, cols] = dot(order, after.astype(BF)).astype(BF).reshape(PLANE, 16, 384)

    def give(k, _):
        to = (i + k) % PLANE
        remote(xs.at[to], xt.at[0, i], xy_s.at[to], xy_r.at[i], on_plane(to)).start()
        return 0

    lax.fori_loop(1, PLANE, give, 0)
    second_landed(18, time_a, time_b, (1, 3))
    push(24, wbuf.at[time_a, pl.ds(4 * ((y + 3) % 4), 2)], on_plane(4 * ((y + 1) % 4) + x))
    push(25, wbuf.at[time_a, pl.ds(4 * ((y + 1) % 4) + 2, 2)], on_plane(4 * ((y + 3) % 4) + x))
    push(26, wbuf.at[time_b, pl.ds(4 * ((x + 3) % 4), 2)], on_plane(4 * y + (x + 1) % 4))
    push(27, wbuf.at[time_b, pl.ds(4 * ((x + 1) % 4) + 2, 2)], on_plane(4 * y + (x + 3) % 4))
    xt[0, i] = xs[i]
    remote(xs.at[i], xt.at[1, i], sb_s.at[i], sb_r.at[i], sib).start()

    def pass_on(k, _):
        source = (i + PLANE - k) % PLANE
        piece = xt.at[0, source]
        landed(piece, xy_r.at[source])
        remote(piece, xt.at[1, source], sb_s.at[source], sb_r.at[source], sib).start()
        return 0

    lax.fori_loop(1, PLANE, pass_on, 0)
    xn[0:256, :] = modulated(xt[0].reshape(256, WIDTH), mod[3:4, :], mod[4:5, :])

    def take_sibling(k, _):
        landed(xt.at[1, k], sb_r.at[k])
        return 0

    lax.fori_loop(0, PLANE, take_sibling, 0)
    mod_copy.wait()
    xn[256:512, :] = modulated(xt[1].reshape(256, WIDTH), modx[3:4, :], modx[4:5, :])

    landed(wbuf.at[time_a, pl.ds(4 * ((y + 2) % 4), 2)], wp_r.at[24])
    landed(wbuf.at[time_a, pl.ds(4 * ((y + 2) % 4) + 2, 2)], wp_r.at[25])
    landed(wbuf.at[time_b, pl.ds(4 * ((x + 2) % 4), 2)], wp_r.at[26])
    landed(wbuf.at[time_b, pl.ds(4 * ((x + 2) % 4) + 2, 2)], wp_r.at[27])
    for copy in straight:
        copy.wait()

    def groups(slot, first, count):
        if slot == 0:
            return [wt.at[9 + first + p] for p in range(count)]
        flats = range(36 * (slot - 1) + first, 36 * (slot - 1) + first + count)
        return [wbuf.at[2 + flat // 16, flat % 16] for flat in flats]

    pair_masks = [head_mask(n, 0, PAIR) for n in range(2)]
    for slot in range(4):
        weights = jnp.concatenate([ref[...] for ref in groups(slot, 0, 27)], axis=0)
        three = dot_t(weights, xn[...]).astype(BF)
        for b in range(2):
            cols = slice(256 * b, 256 * (b + 1))
            query, keys, vals = [three[PAIR * n : PAIR * (n + 1), cols] for n in range(3)]
            stacked = jnp.concatenate([query * m for m in pair_masks], axis=1)
            scores = dot_first(keys, stacked) + jnp.concatenate([tbias[...]] * 2, axis=1)
            terms, over = softmax_keys(scores)
            mixed = dot(vals, terms)
            parts = [
                mixed[HEAD_DIM * n : HEAD_DIM * (n + 1), 256 * n : 256 * (n + 1)] * over[:, 256 * n : 256 * (n + 1)]
                for n in range(2)
            ]
            ot[PAIR * slot : PAIR * (slot + 1), cols] = jnp.concatenate(parts, axis=0).astype(BF)

    def share(first):
        refs = [ref for slot in range(4) for ref in groups(slot, 27, 9)]
        return dot_first(ot[...], jnp.concatenate([ref[:, pl.ds(first, 640)] for ref in refs], axis=0))

    theirs = pl.multiple_of(512 * (1 - c), 128)
    mine = pl.multiple_of(512 * c, 128)
    psend[...] = share(theirs).astype(BF)
    give_share = remote(psend, precv, pp_s.at[0], pp_s.at[1], sib)
    give_share.start()
    own = share(mine)
    give_share.wait()
    results = []
    for b in range(2):
        gate = (mod if b == 0 else modx)[5:6, pl.ds(mine, 640)]
        other = precv[256 * (1 - b) : 256 * (2 - b), :]
        total = (own[256 * b : 256 * (b + 1)] + other.astype(F32)).astype(BF).astype(F32)
        before = xt[b, :, :, pl.ds(mine, 640)].reshape(256, 640).astype(F32)
        results.append((before + gate * total).astype(BF).astype(F32))
    cond = jnp.where(c == 0, results[0], results[1])
    uncond = jnp.where(c == 0, results[1], results[0])
    guided = (uncond + GUIDE * (cond - uncond)).astype(BF)
    guided = jnp.where(c == 0, guided[:, 0:HALF], guided[:, 64 : 64 + HALF])
    gs[...] = guided.reshape(PLANE, 16, HALF)

    def back(k, _):
        to = (i + k) % PLANE
        remote(gs.at[to], g2.at[i], r1_s.at[to], r1_r.at[i], on_plane(to)).start()
        return 0

    lax.fori_loop(1, PLANE, back, 0)
    g2[i] = gs[i]

    def take_back(k, _):
        source = (i + PLANE - k) % PLANE
        landed(g2.at[source], r1_r.at[source])
        return 0

    lax.fori_loop(1, PLANE, take_back, 0)
    order = jnp.where(iota((256, 256), 1) == (iota((256, 256), 0) % 64) * 4 + iota((256, 256), 0) // 64, 1.0, 0.0).astype(BF)
    gz[...] = dot(order, g2[...].reshape(256, HALF)).astype(BF).reshape(4, 64, HALF)

    own_block, other_block = [[gz.at[2 * side + f] for f in range(2)] for side in (zh, 1 - zh)]

    def slot(zz):
        return [out.at[f, pl.ds(64 * zz, 64)] for f in range(2)]

    def inner(hh):
        return zh * 4 + hh

    def outer(hh):
        return (1 - zh) * 4 + hh

    out[:, pl.ds(64 * z, 64), :] = gz[pl.ds(2 * zh, 2)]
    for role in range(4):

        @pl.when(h == role)
        def _():
            waits = []

            def go(side, src, zz, index, f, transit=False):
                dst = tr.at[f] if transit else slot(zz)[f]
                recv = r2_r.at[f, RING] if transit else r2_r.at[f, zz]
                remote(src[f], dst, r2_s.at[side, f, index], recv, [left, right][side]).start()
                waits.append((side, f, index))

            def event(side, zz, forward, f):
                landed(slot(zz)[f], r2_r.at[f, zz])
                if forward:
                    go(side, slot(zz), zz, zz, f)

            for f in range(2):
                if role < 2:
                    go(0, other_block, z, RING, f, transit=role == 1)
                else:
                    go(1, other_block, z, RING, f, transit=role == 2)
                if role > 0:
                    go(0, own_block, z, z, f)
                if role < 3:
                    go(1, own_block, z, z, f)
            if role in (0, 3):
                source = inner(1 if role == 0 else 2)
                for f in range(2):
                    landed(tr.at[f], r2_r.at[f, RING])
                    go(0 if role == 0 else 1, [tr.at[0], tr.at[1]], source, source, f)
            lefts = [inner(k) for k in range(role + 1, 4)] + [outer(0), outer(1)]
            rights = [inner(k) for k in range(role - 1, -1, -1)] + [outer(3), outer(2)]
            for k in range(max(len(lefts), len(rights))):
                for f in range(2):
                    if k < len(lefts):
                        event(0, lefts[k], role > 0, f)
                    if k < len(rights):
                        event(1, rights[k], role < 3, f)
            for side, f, index in waits:
                sent(gz.at[0], r2_s.at[side, f, index])

    each_sent(SPACE + TIME, sent_piece)
    lat_out.wait_send()
    sent(lats.at[0], lat_s.at[2])
    for ref, index in pushed:
        sent(ref, wp_s.at[index])
    sent(wsib, wp_s.at[32])

    def done_z(k, _):
        zz = (z + k) % RING
        sent(att.at[zz], za_s.at[zz])
        return 0

    lax.fori_loop(1, RING, done_z, 0)

    def done_plane(k, _):
        ii = (i + k) % PLANE
        sent(xs.at[ii], xy_s.at[ii])
        sent(gs.at[ii], r1_s.at[ii])
        return 0

    lax.fori_loop(1, PLANE, done_plane, 0)

    def done_sibling(k, _):
        sent(xt.at[0, k], sb_s.at[k])
        return 0

    lax.fori_loop(0, PLANE, done_sibling, 0)


def shards(
    latent,
    modulation,
    w_qkv_space,
    w_out_space,
    w_qkv_time,
    w_out_time,
    clip_frames,
    spatial_window,
):
    c = lax.axis_index("cfg")
    lat = latent.reshape(2, POSITIONS, WIDTH)
    wsp = jnp.transpose(w_qkv_space, (1, 2, 0))
    half = lax.dynamic_slice_in_dim(w_qkv_time, c * PAIR, PAIR, 2)
    wt = jnp.concatenate(
        [
            lax.dynamic_slice_in_dim(w_out_space, c * PAIR, PAIR, 0),
            jnp.transpose(half, (1, 2, 0)).reshape(3 * PAIR, WIDTH),
            lax.dynamic_slice_in_dim(w_out_time, c * PAIR, PAIR, 0),
        ],
        axis=0,
    ).reshape(45, GROUP, WIDTH)
    dma = pltpu.SemaphoreType.DMA
    vmem = pl.BlockSpec(memory_space=pltpu.VMEM)
    smem = pl.BlockSpec(memory_space=pltpu.SMEM)
    out = pl.pallas_call(
        kernel,
        out_shape=jax.ShapeDtypeStruct((2, POSITIONS, HALF), BF),
        in_specs=[smem, smem] + [vmem] * 5,
        out_specs=vmem,
        scratch_shapes=[
            pltpu.VMEM((6, WIDTH), F32),
            pltpu.VMEM((2, 384, POSITIONS), BF),
            pltpu.VMEM((2, PAD + POSITIONS + PAD, 384), BF),
            pltpu.VMEM((2, LOCAL, PAD + POSITIONS + PAD), BF),
            pltpu.VMEM((384, 128), F32),
            pltpu.VMEM((RING, LOCAL, 128), BF),
            pltpu.VMEM((WIDTH, 256), BF),
            pltpu.VMEM((2, 16, GROUP, WIDTH), BF),
            pltpu.VMEM((4, LOCAL, WIDTH), BF),
            pltpu.VMEM((4, 64, WIDTH), BF),
            pltpu.VMEM((PLANE, 16, WIDTH), BF),
            pltpu.VMEM((2, PLANE, 16, WIDTH), BF),
            pltpu.VMEM((9, 16, GROUP, WIDTH), BF),
            pltpu.VMEM((256, 256), F32),
            pltpu.VMEM((512, WIDTH), BF),
            pltpu.VMEM((4 * PAIR, 512), BF),
            pltpu.VMEM((512, 640), BF),
            pltpu.VMEM((512, 640), BF),
            pltpu.VMEM((PLANE, 16, HALF), BF),
            pltpu.VMEM((PLANE, 16, HALF), BF),
            pltpu.VMEM((4, 64, HALF), BF),
            pltpu.VMEM((2, 64, HALF), BF),
            dma((2,)),
            dma((4,)),
            dma((9, 3)),
            dma((9,)),
            dma((33,)),
            dma((33,)),
            dma((RING,)),
            dma((RING,)),
            dma((PLANE,)),
            dma((PLANE,)),
            dma((PLANE,)),
            dma((PLANE,)),
            dma((2,)),
            dma((PLANE,)),
            dma((PLANE,)),
            dma((2, 2, RING + 1)),
            dma((2, RING + 1)),
        ],
        compiler_params=pltpu.CompilerParams(
            collective_id=0, has_side_effects=True, vmem_limit_bytes=56 * 1024 * 1024
        ),
        name="sublayers",
    )(spatial_window, clip_frames, lat, modulation[0], wsp, w_out_space, wt)
    return out.reshape(2 * POSITIONS, HALF)


def solution(mesh):
    return jax.shard_map(
        shards,
        mesh=mesh,
        in_specs=(
            P("seq", None),
            P("cfg", None, None),
            P(None, None, "head"),
            P("head", None),
            P(None, None, "head"),
            P("head", None),
            P(),
            P(),
        ),
        out_specs=P("seq", "cfg"),
        check_vma=False,
    )
```

```python
import functools

import jax
import jax.numpy as jnp
from jax import lax
from jax.experimental import pallas as pl
from jax.experimental.pallas import tpu as pltpu
from jax.sharding import PartitionSpec as P

MESH = pl.DeviceIdType.MESH
HEAD_DIM = 72
POSITIONS = 512
WIDTH = 1152
HALF = 576
LOCAL = 288
PAIR = 144
TWIN = 16
GUIDE = 4.0
EPSILON = 1e-06
NEG = -1e30
PAD = 128
RING = 8
PLANE = 16
GROUP = 16
EXP_SCALE = HEAD_DIM ** (-0.5) * 1.4426950408889634
BF = jnp.bfloat16
F32 = jnp.float32


def iota(shape, dim):
    return lax.broadcasted_iota(jnp.int32, shape, dim)


def modulated(rows, shift, scale):
    values = rows.astype(F32)
    centred = values - jnp.mean(values, axis=-1, keepdims=True)
    spread = jnp.mean(centred * centred, axis=-1, keepdims=True)
    normed = centred * lax.rsqrt(spread + EPSILON)
    return (normed * (1.0 + scale) + shift).astype(BF)


def softmax_keys(scores):
    top = jnp.max(scores, axis=0, keepdims=True)
    terms = jnp.exp2((scores - top) * EXP_SCALE)
    return terms.astype(BF), 1.0 / jnp.sum(terms, axis=0, keepdims=True)


def dot(a, b):
    return lax.dot_general(a, b, (((1,), (0,)), ((), ())), preferred_element_type=F32)


def dot_t(a, b):
    return lax.dot_general(a, b, (((1,), (1,)), ((), ())), preferred_element_type=F32)


def dot_first(a, b):
    return lax.dot_general(a, b, (((0,), (0,)), ((), ())), preferred_element_type=F32)


def head_mask(head, first, rows):
    row = iota((rows, 1), 0) + first
    return jnp.where((row >= head * HEAD_DIM) & (row < (head + 1) * HEAD_DIM), 1.0, 0.0).astype(BF)


def frame_window(frame, clip_ref):
    ends = [clip_ref[0]]
    for j in range(1, 4):
        ends.append(ends[-1] + clip_ref[j])
    clip = jnp.zeros_like(frame)
    start = jnp.zeros_like(frame)
    for end in ends:
        clip = clip + jnp.where(frame >= end, 1, 0)
        start = jnp.where(frame >= end, end, start)
    return clip * 64 + (frame - start) // TWIN


def kernel(
    sw_ref, clip_ref, lat_in, mod, wsp_in, wo, wqt, wot, out,
    modx, lat, wsp, wt, qt, ks, vt, base, att, heads, wsib, wos, lats, xs, xt, wbuf, tbias, xn, ot, psend, precv,
    gs_a, gs_b, g2_a, g2_b, gz_a, gz_b, tr_a, tr_b, land_a, land_b,
    ld, mod_s, lat_s, wz_s, wz_r, wp_s, wp_r, za_s, za_r, xy_s, xy_r, sb_s, sb_r, pp_s, r1_s, r1_r, r2_s, r2_r,
):
    c = lax.axis_index("cfg")
    s = lax.axis_index("seq")
    h = lax.axis_index("head")
    zh = s // PLANE
    i = s % PLANE
    y = i // 4
    x = i % 4
    z = zh * 4 + h

    def on_z(zz):
        return (c, (zz // 4) * PLANE + i, zz % 4)

    def on_plane(ii):
        return (c, zh * PLANE + ii, h)

    sib = (1 - c, s, h)
    left, right = on_z((z + RING - 1) % RING), on_z((z + 1) % RING)

    def block_of(zz):
        return 64 * (2 * (zz % 4) + zz // 4)

    first_rows, last_rows = slice(0, 256), slice(256, 512)
    loads = [
        (wo.at[pl.ds(9 * c, 9)], wt.at[0:9]),
        (lat_in.at[:, first_rows], lat.at[:, first_rows]),
        (wsp_in, wsp),
        (wqt.at[0, pl.ds(9 * c, 9)], wt.at[9:18]),
        (wqt.at[1, pl.ds(9 * c, 9)], wt.at[18:27]),
        (wqt.at[2, pl.ds(9 * c, 9)], wt.at[27:36]),
        (wot.at[pl.ds(9 * c, 9)], wt.at[36:45]),
        (lat_in.at[:, last_rows], lat.at[:, last_rows]),
        (wo, wos.at[h]),
    ]
    loads = [pltpu.make_async_copy(src, dst, ld.at[k]) for k, (src, dst) in enumerate(loads)]
    for copy in loads:
        copy.start()

    def remote(src, dst, send, recv, dev):
        return pltpu.make_async_remote_copy(
            src_ref=src, dst_ref=dst, send_sem=send, recv_sem=recv, device_id=dev, device_id_type=MESH
        )

    def landed(buf, recv):
        remote(buf, buf, recv, recv, sib).wait_recv()

    def sent(buf, send):
        remote(buf, buf, send, send, sib).wait_send()

    barrier = pltpu.get_barrier_semaphore()

    def greet_z(k, _):
        pl.semaphore_signal(barrier, inc=1, device_id=on_z((z + k) % RING), device_id_type=MESH)
        return 0

    def greet_plane(k, _):
        pl.semaphore_signal(barrier, inc=1, device_id=on_plane((i + k) % PLANE), device_id_type=MESH)
        return 0

    lax.fori_loop(1, RING, greet_z, 0)
    lax.fori_loop(1, PLANE, greet_plane, 0)
    pl.semaphore_signal(barrier, inc=1, device_id=sib, device_id_type=MESH)
    pl.semaphore_wait(barrier, RING - 1 + PLANE - 1 + 1)

    far = jnp.where(c == 0, 2, RING - 2)
    hops = [RING - 1, far, 1]
    index_a, index_b = 4 * y + x, 4 * x + y
    SPACE = [(0, index_a, 0, 9, [0, 1]), (1, index_b, 0, 9, [1, 2])]
    TIME = [
        (3, index_a, 2, 36, [0]),
        (4, index_a, 2, 36, [0, 1]),
        (5, index_a, 2, 36, [1]),
        (6, index_b, 2, 36, [1, 2]),
        (7, index_b, 2, 36, [2]),
    ]

    def each_sent(rows, act):
        for q, place, first, per, slots in rows:
            flat = 16 * (q - first) + place
            for j in slots:
                source = wt.at[(9 if per == 36 else 0) + flat - per * j]
                pl.when(flat // per == j)(functools.partial(act, q, place, j, source))

    def start_piece(q, place, j, source):
        remote(source, wbuf.at[q, place], wz_s.at[q, j], wz_r.at[q], on_z((z + hops[j]) % RING)).start()

    def sent_piece(q, place, j, source):
        sent(source, wz_s.at[q, j])

    def take_pieces(rows):
        for q, place, first, per, _ in rows:
            there = 16 * (q - first) + place < 3 * per
            pl.when(there)(functools.partial(landed, wbuf.at[q, place], wz_r.at[q]))

    loads[0].wait()
    each_sent(SPACE, start_piece)

    pushed = []

    def push(index, ref, dev):
        remote(ref, ref, wp_s.at[index], wp_r.at[index], dev).start()
        pushed.append((ref, index))

    def first_phase(index, cut_a, cut_b):
        for k in range(1, 4):
            push(index + k - 1, wbuf.at[cut_a, index_a], on_plane(4 * y + (x + k) % 4))
            push(index + k + 2, wbuf.at[cut_b, index_b], on_plane(4 * ((y + k) % 4) + x))

    def first_landed(index, cut_a, cut_b):
        for k in range(1, 4):
            landed(wbuf.at[cut_a, 4 * y + (x + 4 - k) % 4], wp_r.at[index + k - 1])
            landed(wbuf.at[cut_b, 4 * x + (y + 4 - k) % 4], wp_r.at[index + k + 2])

    def second_phase(index, cut_a, cut_b, steps):
        for k in steps:
            push(index + k - 1, wbuf.at[cut_a, pl.ds(4 * y, 4)], on_plane(4 * ((y + k) % 4) + x))
            push(index + k + 2, wbuf.at[cut_b, pl.ds(4 * x, 4)], on_plane(4 * y + (x + k) % 4))

    def second_landed(index, cut_a, cut_b, steps):
        for k in steps:
            landed(wbuf.at[cut_a, pl.ds(4 * ((y + 4 - k) % 4), 4)], wp_r.at[index + k - 1])
            landed(wbuf.at[cut_b, pl.ds(4 * ((x + 4 - k) % 4), 4)], wp_r.at[index + k + 2])

    space_a, space_b = slice(0, 1), slice(1, 2)
    time_a, time_b = slice(3, 6), slice(6, 8)

    mod_copy = remote(mod, modx, mod_s.at[0], mod_s.at[1], sib)
    mod_copy.start()
    lat_out = remote(
        lat_in.at[c, pl.ds(block_of(7 - z), 64)], lats.at[zh * 2 + c], lat_s.at[0], lat_s.at[1], on_z(7 - z)
    )
    oy = jnp.int32(7)
    ox = jnp.int32(7)
    for r in range(1, 8):
        oy = oy - jnp.where(sw_ref[16 * r] < 3, 1, 0)
        ox = ox - jnp.where(sw_ref[r] < 1, 1, 0)
    qj = iota((384, 128), 1)
    ki = iota((384, 128), 0)
    same = ((qj // 16 + 8 + oy) // 8 == (ki // 16 + oy) // 8) & ((qj % 16 + ox) // 8 == (ki % 16 + ox) // 8)
    base[...] = jnp.where(same, 0.0, NEG)

    def time_key(row):
        four = row % 4
        frame = (four // 2) * 32 + 2 * (row // 16) + four % 2
        return frame_window(frame, clip_ref) * 4 + (row % 16) // 4

    tbias[...] = jnp.where(time_key(iota((256, 1), 0)) == time_key(iota((1, 256), 1)), 0.0, NEG)

    for f in range(2):
        ks[f, 0:PAD, :] = jnp.zeros((PAD, 384), BF)
        ks[f, PAD + POSITIONS :, :] = jnp.zeros((PAD, 384), BF)
        ks[f, PAD : PAD + POSITIONS, 256:384] = jnp.zeros((POSITIONS, 128), BF)
        vt[f, :, 0:PAD] = jnp.zeros((LOCAL, PAD), BF)
        vt[f, :, PAD + POSITIONS :] = jnp.zeros((LOCAL, PAD), BF)
        qt[f, LOCAL:384, :] = jnp.zeros((384 - LOCAL, POSITIONS), BF)

    shift1, scale1 = mod[0], mod[1]
    masks = [head_mask(0, 0, 256), head_mask(1, 0, 256), head_mask(2, 0, 256), head_mask(3, 128, 256)]

    loads[1].wait()
    loads[2].wait()

    def project(rb):
        rows = slice(rb * 256, (rb + 1) * 256)
        padded = slice(PAD + rb * 256, PAD + (rb + 1) * 256)
        for f in range(2):
            values = modulated(lat[f, rows, :], shift1, scale1)
            qt[f, 0:LOCAL, rows] = dot_t(wsp[0], values).astype(BF)
            ks[f, padded, 0:LOCAL] = dot_t(values, wsp[1]).astype(BF)
            vt[f, :, padded] = dot_t(wsp[2], values).astype(BF)

    low = iota((1, 128), 1) < 64

    def attend(k, f):
        cols = pl.ds(pl.multiple_of(k * 128, 128), 128)
        around = pl.ds(pl.multiple_of(k * 128, 128), 384)
        keys = ks[f, around, :]
        query = qt[f, :, cols]
        three = jnp.concatenate([query[0:256] * m for m in masks[0:3]], axis=1)
        row = 8 * k - 8 + iota((384, 1), 0) // 16
        bias = base[...] + jnp.where((row >= 0) & (row < 32), 0.0, NEG)
        scores = jnp.concatenate(
            [dot(keys[:, 0:256], three), dot(keys[:, 128:384], query[128:384] * masks[3])], axis=1
        ) + jnp.concatenate([bias] * 4, axis=1)
        weights, over = softmax_keys(scores)
        mixed = dot(vt[f, :, around], weights)
        parts = [
            mixed[HEAD_DIM * n : HEAD_DIM * (n + 1), 128 * n : 128 * (n + 1)] * over[:, 128 * n : 128 * (n + 1)]
            for n in range(4)
        ]
        return jnp.concatenate(parts, axis=0)

    def attend_both(k):
        first, second = attend(k, 0), attend(k, 1)
        att[k] = jnp.where(low, first, pltpu.roll(second, 64, 1)).astype(BF)
        att[k + 4] = jnp.where(low, pltpu.roll(first, 64, 1), second).astype(BF)

    def send_heads(k):
        for zd in (k, k + 4):
            place = heads.at[pl.ds(LOCAL * h, LOCAL), pl.ds(pl.multiple_of(128 * zh, 128), 128)]
            copy = remote(att.at[zd], place, za_s.at[zd], za_r.at[z], on_z(zd))
            pl.when(z != zd)(copy.start)

            @pl.when(z == zd)
            def _():
                heads[pl.ds(LOCAL * h, LOCAL), pl.ds(pl.multiple_of(128 * zh, 128), 128)] = att[zd]

    project(0)
    take_pieces(SPACE)
    first_phase(0, space_a, space_b)
    for copy in loads[3:7]:
        copy.wait()
    each_sent(TIME, start_piece)
    lat_out.start()
    attend_both(0)
    send_heads(0)
    loads[7].wait()
    project(1)
    first_landed(0, space_a, space_b)
    second_phase(12, space_a, space_b, (1, 2, 3))
    attend_both(1)
    attend_both(2)
    send_heads(1)
    send_heads(2)
    take_pieces(TIME)
    first_phase(6, time_a, time_b)
    attend_both(3)
    send_heads(3)

    piece = lats.at[(1 - zh) * 2 + c]
    landed(piece, lat_s.at[1])
    remote(piece, piece, lat_s.at[2], lat_s.at[3], sib).start()
    first_landed(6, time_a, time_b)
    second_phase(18, time_a, time_b, (1, 3))
    second_landed(12, space_a, space_b, (1, 2, 3))
    remote(wbuf.at[0:2], wsib, wp_s.at[32], wp_r.at[32], sib).start()
    loads[8].wait()
    lats[pl.ds(zh * 2, 2)] = lat[:, pl.ds(block_of(z), 64), :]
    landed(lats.at[(1 - zh) * 2 + (1 - c)], lat_s.at[3])
    landed(wsib, wp_r.at[32])
    for p in range(27):
        shard, row = (h + 1 + p // 9) % 4, p % 9
        place = (p // 16, p % 16)
        wos[shard, 9 * c + row] = wbuf[place]
        wos[shard, 9 * (1 - c) + row] = wsib[place]

    def take_heads(k, _):
        zz = (z + k) % RING
        landed(heads.at[pl.ds(LOCAL * (zz % 4), LOCAL), pl.ds(pl.multiple_of(128 * (zz // 4), 128), 128)], za_r.at[zz])
        return 0

    lax.fori_loop(1, RING, take_heads, 0)

    straight = [
        remote(wt.at[9:25], wbuf.at[2], wp_s.at[28], wp_r.at[28], left),
        remote(wt.at[33:45], wbuf.at[8, 0:12], wp_s.at[29], wp_r.at[29], right),
    ]
    for copy in straight:
        copy.start()

    gate1 = mod[2]
    order = jnp.where(iota((256, 256), 1) == (iota((256, 256), 0) % 4) * 64 + iota((256, 256), 0) // 4, 1.0, 0.0).astype(BF)
    for n in range(3):
        cols = slice(384 * n, 384 * (n + 1))
        total = dot_first(heads[...], wos[:, :, :, cols].reshape(WIDTH, 384))
        after = lats[:, :, cols].reshape(256, 384).astype(F32) + gate1[:, cols] * total.astype(BF).astype(F32)
        xs[:, :, cols] = dot(order, after.astype(BF)).astype(BF).reshape(PLANE, 16, 384)

    def give(k, _):
        to = (i + k) % PLANE
        remote(xs.at[to], xt.at[0, i], xy_s.at[to], xy_r.at[i], on_plane(to)).start()
        return 0

    lax.fori_loop(1, PLANE, give, 0)
    second_landed(18, time_a, time_b, (1, 3))
    push(24, wbuf.at[time_a, pl.ds(4 * ((y + 3) % 4), 2)], on_plane(4 * ((y + 1) % 4) + x))
    push(25, wbuf.at[time_a, pl.ds(4 * ((y + 1) % 4) + 2, 2)], on_plane(4 * ((y + 3) % 4) + x))
    push(26, wbuf.at[time_b, pl.ds(4 * ((x + 3) % 4), 2)], on_plane(4 * y + (x + 1) % 4))
    push(27, wbuf.at[time_b, pl.ds(4 * ((x + 1) % 4) + 2, 2)], on_plane(4 * y + (x + 3) % 4))
    xt[0, i] = xs[i]
    remote(xs.at[i], xt.at[1, i], sb_s.at[i], sb_r.at[i], sib).start()

    def pass_on(k, _):
        source = (i + PLANE - k) % PLANE
        piece = xt.at[0, source]
        landed(piece, xy_r.at[source])
        remote(piece, xt.at[1, source], sb_s.at[source], sb_r.at[source], sib).start()
        return 0

    lax.fori_loop(1, PLANE, pass_on, 0)
    xn[0:256, :] = modulated(xt[0].reshape(256, WIDTH), mod[3], mod[4])

    def take_sibling(k, _):
        landed(xt.at[1, k], sb_r.at[k])
        return 0

    lax.fori_loop(0, PLANE, take_sibling, 0)
    mod_copy.wait()
    xn[256:512, :] = modulated(xt[1].reshape(256, WIDTH), modx[3], modx[4])

    def groups(slot, first, count):
        if slot == 0:
            return [wt.at[9 + first + p] for p in range(count)]
        flats = range(36 * (slot - 1) + first, 36 * (slot - 1) + first + count)
        return [wbuf.at[2 + flat // 16, flat % 16] for flat in flats]

    pair_masks = [head_mask(n, 0, PAIR) for n in range(2)]
    def time_heads(slot):
        weights = jnp.concatenate([ref[...] for ref in groups(slot, 0, 27)], axis=0)
        three = dot_t(weights, xn[...]).astype(BF)
        for b in range(2):
            cols = slice(256 * b, 256 * (b + 1))
            query, keys, vals = [three[PAIR * n : PAIR * (n + 1), cols] for n in range(3)]
            stacked = jnp.concatenate([query * m for m in pair_masks], axis=1)
            scores = dot_first(keys, stacked) + jnp.concatenate([tbias[...]] * 2, axis=1)
            terms, over = softmax_keys(scores)
            mixed = dot(vals, terms)
            parts = [
                mixed[HEAD_DIM * n : HEAD_DIM * (n + 1), 256 * n : 256 * (n + 1)] * over[:, 256 * n : 256 * (n + 1)]
                for n in range(2)
            ]
            ot[PAIR * slot : PAIR * (slot + 1), cols] = jnp.concatenate(parts, axis=0).astype(BF)

    time_heads(0)
    landed(wbuf.at[time_a, pl.ds(4 * ((y + 2) % 4), 2)], wp_r.at[24])
    landed(wbuf.at[time_a, pl.ds(4 * ((y + 2) % 4) + 2, 2)], wp_r.at[25])
    landed(wbuf.at[time_b, pl.ds(4 * ((x + 2) % 4), 2)], wp_r.at[26])
    landed(wbuf.at[time_b, pl.ds(4 * ((x + 2) % 4) + 2, 2)], wp_r.at[27])
    for copy in straight:
        copy.wait()
    for slot in range(1, 4):
        time_heads(slot)

    def share(first):
        refs = [ref for slot in range(4) for ref in groups(slot, 27, 9)]
        return dot_first(ot[...], jnp.concatenate([ref[:, pl.ds(first, 384)] for ref in refs], axis=0))

    sizes = (256, HALF - 256)
    gs, g2, gz, tr, land = (gs_a, gs_b), (g2_a, g2_b), (gz_a, gz_b), (tr_a, tr_b), (land_a, land_b)

    def window(core, p):
        return pl.multiple_of(512 * core + 256 * p, 128)

    give_share = [remote(psend.at[p], precv.at[p], pp_s.at[p], pp_s.at[2 + p], sib) for p in range(2)]
    for p in range(2):
        psend[p] = share(window(1 - c, p)).astype(BF)
        give_share[p].start()
    for p in range(2):
        cols = pl.ds(window(c, p), 384)
        own = share(window(c, p))
        give_share[p].wait()
        results = []
        for b in range(2):
            gate = (mod if b == 0 else modx)[5, :, cols]
            other = precv[p, 256 * (1 - b) : 256 * (2 - b), :]
            total = (own[256 * b : 256 * (b + 1)] + other.astype(F32)).astype(BF).astype(F32)
            before = xt[b, :, :, cols].reshape(256, 384).astype(F32)
            results.append((before + gate * total).astype(BF).astype(F32))
        cond = jnp.where(c == 0, results[0], results[1])
        uncond = jnp.where(c == 0, results[1], results[0])
        guided = (uncond + GUIDE * (cond - uncond)).astype(BF)
        guided = jnp.where(c == 0, guided[:, 0 : sizes[p]], guided[:, 64 : 64 + sizes[p]])
        gs[p][...] = guided.reshape(PLANE, 16, sizes[p])

        def back(k, _):
            to = (i + k) % PLANE
            remote(gs[p].at[to], g2[p].at[i], r1_s.at[p, to], r1_r.at[p, i], on_plane(to)).start()
            return 0

        lax.fori_loop(1, PLANE, back, 0)
        g2[p][i] = gs[p][i]

    def slot(zz, p):
        return land[p].at[zz]

    def inner(hh):
        return zh * 4 + hh

    def outer(hh):
        return (1 - zh) * 4 + hh

    order = jnp.where(iota((256, 256), 0) == (iota((256, 256), 1) % 64) * 4 + iota((256, 256), 1) // 64, 1.0, 0.0).astype(BF)
    for p in range(2):

        def take_back(k, _):
            source = (i + PLANE - k) % PLANE
            landed(g2[p].at[source], r1_r.at[p, source])
            return 0

        lax.fori_loop(1, PLANE, take_back, 0)
        both = dot_first(g2[p][...].reshape(256, sizes[p]), order).astype(BF)
        gz[p][0] = both[:, 0:128]
        gz[p][1] = both[:, 128:256]
        own_block, other_block = gz[p].at[zh], gz[p].at[1 - zh]

        def go(side, src, zz, index, p, transit=False):
            dst = tr[p] if transit else slot(zz, p)
            recv = r2_r.at[p, RING] if transit else r2_r.at[p, zz]
            remote(src, dst, r2_s.at[side, p, index], recv, [left, right][side]).start()

        for role in range(4):

            @pl.when(h == role)
            def _():
                go(0 if role < 2 else 1, other_block, z, RING, p, transit=role in (1, 2))
                if role > 0:
                    go(0, own_block, z, z, p)
                if role < 3:
                    go(1, own_block, z, z, p)

        land[p][z] = gz[p][zh]

    for role in range(4):

        @pl.when(h == role)
        def _():
            waits = []
            if role in (0, 3):
                source = inner(1 if role == 0 else 2)
                for p in range(2):
                    landed(tr[p], r2_r.at[p, RING])
                    go(0 if role == 0 else 1, tr[p], source, source, p)
                    waits.append((0 if role == 0 else 1, source, p))
            lefts = [inner(k) for k in range(role + 1, 4)] + [outer(0), outer(1)]
            rights = [inner(k) for k in range(role - 1, -1, -1)] + [outer(3), outer(2)]
            for k in range(max(len(lefts), len(rights))):
                for p in range(2):
                    for side, chain, forward in ((0, lefts, role > 0), (1, rights, role < 3)):
                        if k < len(chain):
                            landed(slot(chain[k], p), r2_r.at[p, chain[k]])
                            if forward:
                                go(side, slot(chain[k], p), chain[k], chain[k], p)
                                waits.append((side, chain[k], p))
            for p in range(2):
                waits.append((0 if role < 2 else 1, RING, p))
                if role > 0:
                    waits.append((0, z, p))
                if role < 3:
                    waits.append((1, z, p))
            for side, index, p in waits:
                sent(tr[p], r2_s.at[side, p, index])

    for p in range(2):
        rows = slice(256 * p, 256 * p + sizes[p])
        for k in range(4):
            first, second = land[p][k].astype(F32), land[p][k + 4].astype(F32)
            out[rows, 128 * k : 128 * (k + 1)] = jnp.where(low, first, pltpu.roll(second, 64, 1)).astype(BF)
            out[rows, 512 + 128 * k : 512 + 128 * (k + 1)] = jnp.where(low, pltpu.roll(first, 64, 1), second).astype(BF)

    each_sent(SPACE + TIME, sent_piece)
    lat_out.wait_send()
    sent(lats.at[0], lat_s.at[2])
    for ref, index in pushed:
        sent(ref, wp_s.at[index])
    sent(wsib, wp_s.at[32])

    def done_z(k, _):
        zz = (z + k) % RING
        sent(att.at[zz], za_s.at[zz])
        return 0

    lax.fori_loop(1, RING, done_z, 0)

    def done_plane(k, _):
        ii = (i + k) % PLANE
        sent(xs.at[ii], xy_s.at[ii])
        for p in range(2):
            sent(gs[p].at[ii], r1_s.at[p, ii])
        return 0

    lax.fori_loop(1, PLANE, done_plane, 0)

    def done_sibling(k, _):
        sent(xt.at[0, k], sb_s.at[k])
        return 0

    lax.fori_loop(0, PLANE, done_sibling, 0)


def shards(
    latent,
    modulation,
    w_qkv_space,
    w_out_space,
    w_qkv_time,
    w_out_time,
    clip_frames,
    spatial_window,
):
    lat = latent.reshape(2, POSITIONS, WIDTH)
    wsp = jnp.transpose(w_qkv_space, (1, 2, 0))
    wqt = jnp.transpose(w_qkv_time, (1, 2, 0)).reshape(3, 18, GROUP, WIDTH)
    wo = w_out_space.reshape(18, GROUP, WIDTH)
    wot = w_out_time.reshape(18, GROUP, WIDTH)
    dma = pltpu.SemaphoreType.DMA
    vmem = pl.BlockSpec(memory_space=pltpu.VMEM)
    smem = pl.BlockSpec(memory_space=pltpu.SMEM)
    anywhere = pl.BlockSpec(memory_space=pl.ANY)
    out = pl.pallas_call(
        kernel,
        out_shape=jax.ShapeDtypeStruct((HALF, 2 * POSITIONS), BF),
        in_specs=[smem, smem, anywhere, vmem] + [anywhere] * 4,
        out_specs=vmem,
        scratch_shapes=[
            pltpu.VMEM((6, 1, WIDTH), F32),
            pltpu.VMEM((2, POSITIONS, WIDTH), BF),
            pltpu.VMEM((3, LOCAL, WIDTH), BF),
            pltpu.VMEM((45, GROUP, WIDTH), BF),
            pltpu.VMEM((2, 384, POSITIONS), BF),
            pltpu.VMEM((2, PAD + POSITIONS + PAD, 384), BF),
            pltpu.VMEM((2, LOCAL, PAD + POSITIONS + PAD), BF),
            pltpu.VMEM((384, 128), F32),
            pltpu.VMEM((RING, LOCAL, 128), BF),
            pltpu.VMEM((WIDTH, 256), BF),
            pltpu.VMEM((2, 16, GROUP, WIDTH), BF),
            pltpu.VMEM((4, 18, GROUP, WIDTH), BF),
            pltpu.VMEM((4, 64, WIDTH), BF),
            pltpu.VMEM((PLANE, 16, WIDTH), BF),
            pltpu.VMEM((2, PLANE, 16, WIDTH), BF),
            pltpu.VMEM((9, 16, GROUP, WIDTH), BF),
            pltpu.VMEM((256, 256), F32),
            pltpu.VMEM((512, WIDTH), BF),
            pltpu.VMEM((4 * PAIR, 512), BF),
            pltpu.VMEM((2, 512, 384), BF),
            pltpu.VMEM((2, 512, 384), BF),
            pltpu.VMEM((PLANE, 16, 256), BF),
            pltpu.VMEM((PLANE, 16, HALF - 256), BF),
            pltpu.VMEM((PLANE, 16, 256), BF),
            pltpu.VMEM((PLANE, 16, HALF - 256), BF),
            pltpu.VMEM((2, 256, 128), BF),
            pltpu.VMEM((2, HALF - 256, 128), BF),
            pltpu.VMEM((256, 128), BF),
            pltpu.VMEM((HALF - 256, 128), BF),
            pltpu.VMEM((RING, 256, 128), BF),
            pltpu.VMEM((RING, HALF - 256, 128), BF),
            dma((9,)),
            dma((2,)),
            dma((4,)),
            dma((9, 3)),
            dma((9,)),
            dma((33,)),
            dma((33,)),
            dma((RING,)),
            dma((RING,)),
            dma((PLANE,)),
            dma((PLANE,)),
            dma((PLANE,)),
            dma((PLANE,)),
            dma((4,)),
            dma((2, PLANE)),
            dma((2, PLANE)),
            dma((2, 2, RING + 1)),
            dma((2, RING + 1)),
        ],
        compiler_params=pltpu.CompilerParams(
            collective_id=0, has_side_effects=True, vmem_limit_bytes=56 * 1024 * 1024
        ),
        name="sublayers",
    )(spatial_window, clip_frames, lat, jnp.transpose(modulation, (1, 0, 2)), wsp, wo, wqt, wot)
    return jnp.transpose(out)


def solution(mesh):
    return jax.shard_map(
        shards,
        mesh=mesh,
        in_specs=(
            P("seq", None),
            P("cfg", None, None),
            P(None, None, "head"),
            P("head", None),
            P(None, None, "head"),
            P("head", None),
            P(),
            P(),
        ),
        out_specs=P("seq", "cfg"),
        check_vma=False,
    )
```

```python
import functools

import jax
import jax.numpy as jnp
from jax import lax
from jax.experimental import pallas as pl
from jax.experimental.pallas import tpu as pltpu
from jax.sharding import PartitionSpec as P

MESH = pl.DeviceIdType.MESH
HEAD_DIM = 72
POSITIONS = 512
WIDTH = 1152
HALF = 576
LOCAL = 288
PAIR = 144
TWIN = 16
GUIDE = 4.0
EPSILON = 1e-06
NEG = -1e30
PAD = 128
RING = 8
PLANE = 16
GROUP = 16
EXP_SCALE = HEAD_DIM ** (-0.5) * 1.4426950408889634
BF = jnp.bfloat16
F32 = jnp.float32


def iota(shape, dim):
    return lax.broadcasted_iota(jnp.int32, shape, dim)


def modulated(rows, shift, scale):
    values = rows.astype(F32)
    centred = values - jnp.mean(values, axis=-1, keepdims=True)
    spread = jnp.mean(centred * centred, axis=-1, keepdims=True)
    normed = centred * lax.rsqrt(spread + EPSILON)
    return (normed * (1.0 + scale) + shift).astype(BF)


def softmax_keys(scores):
    top = jnp.max(scores, axis=0, keepdims=True)
    terms = jnp.exp2((scores - top) * EXP_SCALE)
    return terms.astype(BF), 1.0 / jnp.sum(terms, axis=0, keepdims=True)


def dot(a, b):
    return lax.dot_general(a, b, (((1,), (0,)), ((), ())), preferred_element_type=F32)


def dot_t(a, b):
    return lax.dot_general(a, b, (((1,), (1,)), ((), ())), preferred_element_type=F32)


def dot_first(a, b):
    return lax.dot_general(a, b, (((0,), (0,)), ((), ())), preferred_element_type=F32)


def head_mask(head, first, rows):
    row = iota((rows, 1), 0) + first
    return jnp.where((row >= head * HEAD_DIM) & (row < (head + 1) * HEAD_DIM), 1.0, 0.0).astype(BF)


def frame_window(frame, clip_ref):
    ends = [clip_ref[0]]
    for j in range(1, 4):
        ends.append(ends[-1] + clip_ref[j])
    clip = jnp.zeros_like(frame)
    start = jnp.zeros_like(frame)
    for end in ends:
        clip = clip + jnp.where(frame >= end, 1, 0)
        start = jnp.where(frame >= end, end, start)
    return clip * 64 + (frame - start) // TWIN


def kernel(
    sw_ref, clip_ref, lat_in, mod, wsp_in, wo, wqt, wot, out_a, out_b,
    modx, lat, wsp, wt, qt, ks, vt, base, att, heads, wsib, wos, lats, xs, xt, wbuf, tbias, xn, ot, psend, precv,
    gs_a, gs_b, g2_a, g2_b, gz_a, gz_b, tr_a, tr_b, land_a, land_b,
    ld, mod_s, lat_s, wz_s, wz_r, wp_s, wp_r, za_s, za_r, xy_s, xy_r, sb_s, sb_r, pp_s, r1_s, r1_r, r2_s, r2_r,
):
    c = lax.axis_index("cfg")
    s = lax.axis_index("seq")
    h = lax.axis_index("head")
    zh = s // PLANE
    i = s % PLANE
    y = i // 4
    x = i % 4
    z = zh * 4 + h

    def on_z(zz):
        return (c, (zz // 4) * PLANE + i, zz % 4)

    def on_plane(ii):
        return (c, zh * PLANE + ii, h)

    sib = (1 - c, s, h)
    left, right = on_z((z + RING - 1) % RING), on_z((z + 1) % RING)

    def block_of(zz):
        return 64 * (2 * (zz % 4) + zz // 4)

    first_rows, last_rows = slice(0, 256), slice(256, 512)
    loads = [
        (wo.at[pl.ds(9 * c, 9)], wt.at[0:9]),
        (lat_in.at[:, first_rows], lat.at[:, first_rows]),
        (wsp_in, wsp),
        (wqt.at[0, pl.ds(9 * c, 9)], wt.at[9:18]),
        (wqt.at[1, pl.ds(9 * c, 9)], wt.at[18:27]),
        (wqt.at[2, pl.ds(9 * c, 9)], wt.at[27:36]),
        (wot.at[pl.ds(9 * c, 9)], wt.at[36:45]),
        (lat_in.at[:, last_rows], lat.at[:, last_rows]),
        (wo, wos.at[h]),
    ]
    loads = [pltpu.make_async_copy(src, dst, ld.at[k]) for k, (src, dst) in enumerate(loads)]
    for copy in loads:
        copy.start()

    def remote(src, dst, send, recv, dev):
        return pltpu.make_async_remote_copy(
            src_ref=src, dst_ref=dst, send_sem=send, recv_sem=recv, device_id=dev, device_id_type=MESH
        )

    def landed(buf, recv):
        remote(buf, buf, recv, recv, sib).wait_recv()

    def sent(buf, send):
        remote(buf, buf, send, send, sib).wait_send()

    barrier = pltpu.get_barrier_semaphore()

    def greet_z(k, _):
        pl.semaphore_signal(barrier, inc=1, device_id=on_z((z + k) % RING), device_id_type=MESH)
        return 0

    def greet_plane(k, _):
        pl.semaphore_signal(barrier, inc=1, device_id=on_plane((i + k) % PLANE), device_id_type=MESH)
        return 0

    lax.fori_loop(1, RING, greet_z, 0)
    lax.fori_loop(1, PLANE, greet_plane, 0)
    pl.semaphore_signal(barrier, inc=1, device_id=sib, device_id_type=MESH)
    pl.semaphore_wait(barrier, RING - 1 + PLANE - 1 + 1)

    far = jnp.where(c == 0, 2, RING - 2)
    hops = [RING - 1, far, 1]
    index_a, index_b = 4 * y + x, 4 * x + y
    SPACE = [(0, index_a, 0, 9, [0, 1]), (1, index_b, 0, 9, [1, 2])]
    TIME = [
        (3, index_a, 2, 36, [0]),
        (4, index_a, 2, 36, [0, 1]),
        (5, index_a, 2, 36, [1]),
        (6, index_b, 2, 36, [1, 2]),
        (7, index_b, 2, 36, [2]),
    ]

    def each_sent(rows, act):
        for q, place, first, per, slots in rows:
            flat = 16 * (q - first) + place
            for j in slots:
                source = wt.at[(9 if per == 36 else 0) + flat - per * j]
                pl.when(flat // per == j)(functools.partial(act, q, place, j, source))

    def start_piece(q, place, j, source):
        remote(source, wbuf.at[q, place], wz_s.at[q, j], wz_r.at[q], on_z((z + hops[j]) % RING)).start()

    def sent_piece(q, place, j, source):
        sent(source, wz_s.at[q, j])

    def take_pieces(rows):
        for q, place, first, per, _ in rows:
            there = 16 * (q - first) + place < 3 * per
            pl.when(there)(functools.partial(landed, wbuf.at[q, place], wz_r.at[q]))

    loads[0].wait()
    each_sent(SPACE, start_piece)

    pushed = []

    def push(index, ref, dev):
        remote(ref, ref, wp_s.at[index], wp_r.at[index], dev).start()
        pushed.append((ref, index))

    def first_phase(index, cut_a, cut_b):
        for k in range(1, 4):
            push(index + k - 1, wbuf.at[cut_a, index_a], on_plane(4 * y + (x + k) % 4))
            push(index + k + 2, wbuf.at[cut_b, index_b], on_plane(4 * ((y + k) % 4) + x))

    def first_landed(index, cut_a, cut_b):
        for k in range(1, 4):
            landed(wbuf.at[cut_a, 4 * y + (x + 4 - k) % 4], wp_r.at[index + k - 1])
            landed(wbuf.at[cut_b, 4 * x + (y + 4 - k) % 4], wp_r.at[index + k + 2])

    def second_phase(index, cut_a, cut_b, steps):
        for k in steps:
            push(index + k - 1, wbuf.at[cut_a, pl.ds(4 * y, 4)], on_plane(4 * ((y + k) % 4) + x))
            push(index + k + 2, wbuf.at[cut_b, pl.ds(4 * x, 4)], on_plane(4 * y + (x + k) % 4))

    def second_landed(index, cut_a, cut_b, steps):
        for k in steps:
            landed(wbuf.at[cut_a, pl.ds(4 * ((y + 4 - k) % 4), 4)], wp_r.at[index + k - 1])
            landed(wbuf.at[cut_b, pl.ds(4 * ((x + 4 - k) % 4), 4)], wp_r.at[index + k + 2])

    space_a, space_b = slice(0, 1), slice(1, 2)
    time_a, time_b = slice(3, 6), slice(6, 8)

    mod_copy = remote(mod, modx, mod_s.at[0], mod_s.at[1], sib)
    mod_copy.start()
    lat_out = remote(
        lat_in.at[c, pl.ds(block_of(7 - z), 64)], lats.at[zh * 2 + c], lat_s.at[0], lat_s.at[1], on_z(7 - z)
    )
    oy = jnp.int32(7)
    ox = jnp.int32(7)
    for r in range(1, 8):
        oy = oy - jnp.where(sw_ref[16 * r] < 3, 1, 0)
        ox = ox - jnp.where(sw_ref[r] < 1, 1, 0)
    qj = iota((384, 128), 1)
    ki = iota((384, 128), 0)
    same = ((qj // 16 + 8 + oy) // 8 == (ki // 16 + oy) // 8) & ((qj % 16 + ox) // 8 == (ki % 16 + ox) // 8)
    base[...] = jnp.where(same, 0.0, NEG)

    for f in range(2):
        ks[f, 0:PAD, :] = jnp.zeros((PAD, 384), BF)
        ks[f, PAD + POSITIONS :, :] = jnp.zeros((PAD, 384), BF)
        ks[f, PAD : PAD + POSITIONS, 256:384] = jnp.zeros((POSITIONS, 128), BF)
        vt[f, :, 0:PAD] = jnp.zeros((LOCAL, PAD), BF)
        vt[f, :, PAD + POSITIONS :] = jnp.zeros((LOCAL, PAD), BF)
        qt[f, LOCAL:384, :] = jnp.zeros((384 - LOCAL, POSITIONS), BF)

    shift1, scale1 = mod[0], mod[1]
    masks = [head_mask(0, 0, 256), head_mask(1, 0, 256), head_mask(2, 0, 256), head_mask(3, 128, 256)]

    loads[1].wait()
    loads[2].wait()

    def project(rb, f):
        rows = slice(rb * 256, (rb + 1) * 256)
        padded = slice(PAD + rb * 256, PAD + (rb + 1) * 256)
        values = modulated(lat[f, rows, :], shift1, scale1)
        qt[f, 0:LOCAL, rows] = dot_t(wsp[0], values).astype(BF)
        ks[f, padded, 0:LOCAL] = dot_t(values, wsp[1]).astype(BF)
        vt[f, :, padded] = dot_t(wsp[2], values).astype(BF)

    low = iota((1, 128), 1) < 64

    def attend(k, f):
        cols = pl.ds(pl.multiple_of(k * 128, 128), 128)
        around = pl.ds(pl.multiple_of(k * 128, 128), 384)
        keys = ks[f, around, :]
        query = qt[f, :, cols]
        three = jnp.concatenate([query[0:256] * m for m in masks[0:3]], axis=1)
        row = 8 * k - 8 + iota((384, 1), 0) // 16
        bias = base[...] + jnp.where((row >= 0) & (row < 32), 0.0, NEG)
        scores = jnp.concatenate(
            [dot(keys[:, 0:256], three), dot(keys[:, 128:384], query[128:384] * masks[3])], axis=1
        ) + jnp.concatenate([bias] * 4, axis=1)
        weights, over = softmax_keys(scores)
        mixed = dot(vt[f, :, around], weights)
        parts = [
            mixed[HEAD_DIM * n : HEAD_DIM * (n + 1), 128 * n : 128 * (n + 1)] * over[:, 128 * n : 128 * (n + 1)]
            for n in range(4)
        ]
        return jnp.concatenate(parts, axis=0)

    def attend_both(k):
        first, second = attend(k, 0), attend(k, 1)
        att[k] = jnp.where(low, first, pltpu.roll(second, 64, 1)).astype(BF)
        att[k + 4] = jnp.where(low, pltpu.roll(first, 64, 1), second).astype(BF)

    def send_heads(k):
        for zd in (k, k + 4):
            place = heads.at[pl.ds(LOCAL * h, LOCAL), pl.ds(pl.multiple_of(128 * zh, 128), 128)]
            copy = remote(att.at[zd], place, za_s.at[zd], za_r.at[z], on_z(zd))
            pl.when(z != zd)(copy.start)

            @pl.when(z == zd)
            def _():
                heads[pl.ds(LOCAL * h, LOCAL), pl.ds(pl.multiple_of(128 * zh, 128), 128)] = att[zd]

    for copy in loads[3:7]:
        copy.wait()
    each_sent(TIME, start_piece)
    lat_out.start()
    project(0, 0)
    take_pieces(SPACE)
    first_phase(0, space_a, space_b)
    project(0, 1)
    attend_both(0)
    send_heads(0)
    first_landed(0, space_a, space_b)
    second_phase(12, space_a, space_b, (1, 2, 3))
    take_pieces(TIME)
    first_phase(6, time_a, time_b)
    loads[7].wait()
    project(1, 0)
    project(1, 1)
    for k in range(1, 4):
        attend_both(k)
        send_heads(k)

    def time_key(row):
        four = row % 4
        frame = (four // 2) * 32 + 2 * (row // 16) + four % 2
        return frame_window(frame, clip_ref) * 4 + (row % 16) // 4

    tbias[...] = jnp.where(time_key(iota((256, 1), 0)) == time_key(iota((1, 256), 1)), 0.0, NEG)

    piece = lats.at[(1 - zh) * 2 + c]
    landed(piece, lat_s.at[1])
    remote(piece, piece, lat_s.at[2], lat_s.at[3], sib).start()
    first_landed(6, time_a, time_b)
    second_phase(18, time_a, time_b, (1, 3))
    second_landed(12, space_a, space_b, (1, 2, 3))
    remote(wbuf.at[0:2], wsib, wp_s.at[32], wp_r.at[32], sib).start()
    loads[8].wait()
    lats[pl.ds(zh * 2, 2)] = lat[:, pl.ds(block_of(z), 64), :]
    landed(lats.at[(1 - zh) * 2 + (1 - c)], lat_s.at[3])
    landed(wsib, wp_r.at[32])
    for p in range(27):
        shard, row = (h + 1 + p // 9) % 4, p % 9
        place = (p // 16, p % 16)
        wos[shard, 9 * c + row] = wbuf[place]
        wos[shard, 9 * (1 - c) + row] = wsib[place]

    def take_heads(k, _):
        zz = (z + k) % RING
        landed(heads.at[pl.ds(LOCAL * (zz % 4), LOCAL), pl.ds(pl.multiple_of(128 * (zz // 4), 128), 128)], za_r.at[zz])
        return 0

    lax.fori_loop(1, RING, take_heads, 0)

    straight = [
        remote(wt.at[9:25], wbuf.at[2], wp_s.at[28], wp_r.at[28], left),
        remote(wt.at[33:45], wbuf.at[8, 0:12], wp_s.at[29], wp_r.at[29], right),
    ]
    for copy in straight:
        copy.start()

    gate1 = mod[2]
    order = jnp.where(iota((256, 256), 1) == (iota((256, 256), 0) % 4) * 64 + iota((256, 256), 0) // 4, 1.0, 0.0).astype(BF)
    for n in range(3):
        cols = slice(384 * n, 384 * (n + 1))
        total = dot_first(heads[...], wos[:, :, :, cols].reshape(WIDTH, 384))
        after = lats[:, :, cols].reshape(256, 384).astype(F32) + gate1[:, cols] * total.astype(BF).astype(F32)
        xs[:, :, cols] = dot(order, after.astype(BF)).astype(BF).reshape(PLANE, 16, 384)

    def give(k, _):
        to = (i + k) % PLANE
        remote(xs.at[to], xt.at[0, i], xy_s.at[to], xy_r.at[i], on_plane(to)).start()
        return 0

    lax.fori_loop(1, PLANE, give, 0)
    second_landed(18, time_a, time_b, (1, 3))
    push(24, wbuf.at[time_a, pl.ds(4 * ((y + 3) % 4), 2)], on_plane(4 * ((y + 1) % 4) + x))
    push(25, wbuf.at[time_a, pl.ds(4 * ((y + 1) % 4) + 2, 2)], on_plane(4 * ((y + 3) % 4) + x))
    push(26, wbuf.at[time_b, pl.ds(4 * ((x + 3) % 4), 2)], on_plane(4 * y + (x + 1) % 4))
    push(27, wbuf.at[time_b, pl.ds(4 * ((x + 1) % 4) + 2, 2)], on_plane(4 * y + (x + 3) % 4))
    xt[0, i] = xs[i]
    remote(xs.at[i], xt.at[1, i], sb_s.at[i], sb_r.at[i], sib).start()

    mod_copy.wait()

    def own_group(n):
        g = (i // 4 + 4 - n) % 4
        for m in range(4):
            source = 4 * g + m

            @pl.when(source != i)
            def _():
                piece = xt.at[0, source]
                landed(piece, xy_r.at[source])
                remote(piece, xt.at[1, source], sb_s.at[source], sb_r.at[source], sib).start()

        rows = xt[0, pl.ds(4 * g, 4)].reshape(64, WIDTH)
        xn[pl.ds(64 * g, 64), :] = modulated(rows, mod[3], mod[4])

    def sibling_group(n):
        g = (i // 4 + 4 - n) % 4
        for m in range(4):
            landed(xt.at[1, 4 * g + m], sb_r.at[4 * g + m])
        rows = xt[1, pl.ds(4 * g, 4)].reshape(64, WIDTH)
        xn[pl.ds(256 + 64 * g, 64), :] = modulated(rows, modx[3], modx[4])

    own_group(0)
    own_group(1)
    sibling_group(0)
    own_group(2)
    sibling_group(1)
    own_group(3)
    sibling_group(2)
    sibling_group(3)

    def groups(slot, first, count):
        if slot == 0:
            return [wt.at[9 + first + p] for p in range(count)]
        flats = range(36 * (slot - 1) + first, 36 * (slot - 1) + first + count)
        return [wbuf.at[2 + flat // 16, flat % 16] for flat in flats]

    pair_masks = [head_mask(n, 0, PAIR) for n in range(2)]
    def time_heads(slot):
        weights = jnp.concatenate([ref[...] for ref in groups(slot, 0, 27)], axis=0)
        three = dot_t(weights, xn[...]).astype(BF)
        for b in range(2):
            cols = slice(256 * b, 256 * (b + 1))
            query, keys, vals = [three[PAIR * n : PAIR * (n + 1), cols] for n in range(3)]
            stacked = jnp.concatenate([query * m for m in pair_masks], axis=1)
            scores = dot_first(keys, stacked) + jnp.concatenate([tbias[...]] * 2, axis=1)
            terms, over = softmax_keys(scores)
            mixed = dot(vals, terms)
            parts = [
                mixed[HEAD_DIM * n : HEAD_DIM * (n + 1), 256 * n : 256 * (n + 1)] * over[:, 256 * n : 256 * (n + 1)]
                for n in range(2)
            ]
            ot[PAIR * slot : PAIR * (slot + 1), cols] = jnp.concatenate(parts, axis=0).astype(BF)

    time_heads(0)
    landed(wbuf.at[time_a, pl.ds(4 * ((y + 2) % 4), 2)], wp_r.at[24])
    landed(wbuf.at[time_a, pl.ds(4 * ((y + 2) % 4) + 2, 2)], wp_r.at[25])
    landed(wbuf.at[time_b, pl.ds(4 * ((x + 2) % 4), 2)], wp_r.at[26])
    landed(wbuf.at[time_b, pl.ds(4 * ((x + 2) % 4) + 2, 2)], wp_r.at[27])
    for copy in straight:
        copy.wait()
    for slot in range(1, 4):
        time_heads(slot)

    def share(first):
        refs = [ref for slot in range(4) for ref in groups(slot, 27, 9)]
        return dot_first(ot[...], jnp.concatenate([ref[:, pl.ds(first, 384)] for ref in refs], axis=0))

    sizes = (256, HALF - 256)
    gs, g2, gz, tr, land = (gs_a, gs_b), (g2_a, g2_b), (gz_a, gz_b), (tr_a, tr_b), (land_a, land_b)

    def window(core, p):
        return pl.multiple_of(512 * core + 256 * p, 128)

    give_share = [remote(psend.at[p], precv.at[p], pp_s.at[p], pp_s.at[2 + p], sib) for p in range(2)]
    for p in range(2):
        psend[p] = share(window(1 - c, p)).astype(BF)
        give_share[p].start()
    for p in range(2):
        cols = pl.ds(window(c, p), 384)
        own = share(window(c, p))
        give_share[p].wait()
        results = []
        for b in range(2):
            gate = (mod if b == 0 else modx)[5, :, cols]
            other = precv[p, 256 * (1 - b) : 256 * (2 - b), :]
            total = (own[256 * b : 256 * (b + 1)] + other.astype(F32)).astype(BF).astype(F32)
            before = xt[b, :, :, cols].reshape(256, 384).astype(F32)
            results.append((before + gate * total).astype(BF).astype(F32))
        cond = jnp.where(c == 0, results[0], results[1])
        uncond = jnp.where(c == 0, results[1], results[0])
        guided = (uncond + GUIDE * (cond - uncond)).astype(BF)
        guided = jnp.where(c == 0, guided[:, 0 : sizes[p]], guided[:, 64 : 64 + sizes[p]])
        gs[p][...] = guided.reshape(PLANE, 16, sizes[p])

        def back(k, _):
            to = (i + k) % PLANE
            remote(gs[p].at[to], g2[p].at[i], r1_s.at[p, to], r1_r.at[p, i], on_plane(to)).start()
            return 0

        lax.fori_loop(1, PLANE, back, 0)
        g2[p][i] = gs[p][i]

    def slot(zz, p):
        return land[p].at[zz]

    def inner(hh):
        return zh * 4 + hh

    def outer(hh):
        return (1 - zh) * 4 + hh

    order = jnp.where(iota((256, 256), 0) == (iota((256, 256), 1) % 64) * 4 + iota((256, 256), 1) // 64, 1.0, 0.0).astype(BF)
    for p in range(2):

        def take_back(k, _):
            source = (i + PLANE - k) % PLANE
            landed(g2[p].at[source], r1_r.at[p, source])
            return 0

        lax.fori_loop(1, PLANE, take_back, 0)
        both = dot_first(g2[p][...].reshape(256, sizes[p]), order).astype(BF)
        gz[p][0] = both[:, 0:128]
        gz[p][1] = both[:, 128:256]
        own_block, other_block = gz[p].at[zh], gz[p].at[1 - zh]

        def go(side, src, zz, index, p, transit=False):
            dst = tr[p] if transit else slot(zz, p)
            recv = r2_r.at[p, RING] if transit else r2_r.at[p, zz]
            remote(src, dst, r2_s.at[side, p, index], recv, [left, right][side]).start()

        for role in range(4):

            @pl.when(h == role)
            def _():
                go(0 if role < 2 else 1, other_block, z, RING, p, transit=role in (1, 2))
                if role > 0:
                    go(0, own_block, z, z, p)
                if role < 3:
                    go(1, own_block, z, z, p)

        land[p][z] = gz[p][zh]

    for role in range(4):

        @pl.when(h == role)
        def _():
            waits = []
            if role in (0, 3):
                source = inner(1 if role == 0 else 2)
                for p in range(2):
                    landed(tr[p], r2_r.at[p, RING])
                    go(0 if role == 0 else 1, tr[p], source, source, p)
                    waits.append((0 if role == 0 else 1, source, p))
            lefts = [inner(k) for k in range(role + 1, 4)] + [outer(0), outer(1)]
            rights = [inner(k) for k in range(role - 1, -1, -1)] + [outer(3), outer(2)]
            for k in range(max(len(lefts), len(rights))):
                for p in range(2):
                    for side, chain, forward in ((0, lefts, role > 0), (1, rights, role < 3)):
                        if k < len(chain):
                            landed(slot(chain[k], p), r2_r.at[p, chain[k]])
                            if forward:
                                go(side, slot(chain[k], p), chain[k], chain[k], p)
                                waits.append((side, chain[k], p))
            for p in range(2):
                waits.append((0 if role < 2 else 1, RING, p))
                if role > 0:
                    waits.append((0, z, p))
                if role < 3:
                    waits.append((1, z, p))
            for side, index, p in waits:
                sent(tr[p], r2_s.at[side, p, index])

    for p in range(2):
        out = (out_a, out_b)[p]
        for k in range(4):
            first, second = land[p][k].astype(F32), land[p][k + 4].astype(F32)
            out[:, 128 * k : 128 * (k + 1)] = jnp.where(low, first, pltpu.roll(second, 64, 1)).astype(BF)
            out[:, 512 + 128 * k : 512 + 128 * (k + 1)] = jnp.where(low, pltpu.roll(first, 64, 1), second).astype(BF)

    each_sent(SPACE + TIME, sent_piece)
    lat_out.wait_send()
    sent(lats.at[0], lat_s.at[2])
    for ref, index in pushed:
        sent(ref, wp_s.at[index])
    sent(wsib, wp_s.at[32])

    def done_z(k, _):
        zz = (z + k) % RING
        sent(att.at[zz], za_s.at[zz])
        return 0

    lax.fori_loop(1, RING, done_z, 0)

    def done_plane(k, _):
        ii = (i + k) % PLANE
        sent(xs.at[ii], xy_s.at[ii])
        for p in range(2):
            sent(gs[p].at[ii], r1_s.at[p, ii])
        return 0

    lax.fori_loop(1, PLANE, done_plane, 0)

    def done_sibling(k, _):
        sent(xt.at[0, k], sb_s.at[k])
        return 0

    lax.fori_loop(0, PLANE, done_sibling, 0)


def shards(
    latent,
    modulation,
    w_qkv_space,
    w_out_space,
    w_qkv_time,
    w_out_time,
    clip_frames,
    spatial_window,
):
    lat = latent.reshape(2, POSITIONS, WIDTH)
    wsp = jnp.transpose(w_qkv_space, (1, 2, 0))
    wqt = jnp.transpose(w_qkv_time, (1, 2, 0)).reshape(3, 18, GROUP, WIDTH)
    wo = w_out_space.reshape(18, GROUP, WIDTH)
    wot = w_out_time.reshape(18, GROUP, WIDTH)
    dma = pltpu.SemaphoreType.DMA
    vmem = pl.BlockSpec(memory_space=pltpu.VMEM)
    smem = pl.BlockSpec(memory_space=pltpu.SMEM)
    anywhere = pl.BlockSpec(memory_space=pl.ANY)
    out_a, out_b = pl.pallas_call(
        kernel,
        out_shape=[jax.ShapeDtypeStruct((rows, 2 * POSITIONS), BF) for rows in (256, HALF - 256)],
        in_specs=[smem, smem, anywhere, vmem] + [anywhere] * 4,
        out_specs=[vmem, vmem],
        scratch_shapes=[
            pltpu.VMEM((6, 1, WIDTH), F32),
            pltpu.VMEM((2, POSITIONS, WIDTH), BF),
            pltpu.VMEM((3, LOCAL, WIDTH), BF),
            pltpu.VMEM((45, GROUP, WIDTH), BF),
            pltpu.VMEM((2, 384, POSITIONS), BF),
            pltpu.VMEM((2, PAD + POSITIONS + PAD, 384), BF),
            pltpu.VMEM((2, LOCAL, PAD + POSITIONS + PAD), BF),
            pltpu.VMEM((384, 128), F32),
            pltpu.VMEM((RING, LOCAL, 128), BF),
            pltpu.VMEM((WIDTH, 256), BF),
            pltpu.VMEM((2, 16, GROUP, WIDTH), BF),
            pltpu.VMEM((4, 18, GROUP, WIDTH), BF),
            pltpu.VMEM((4, 64, WIDTH), BF),
            pltpu.VMEM((PLANE, 16, WIDTH), BF),
            pltpu.VMEM((2, PLANE, 16, WIDTH), BF),
            pltpu.VMEM((9, 16, GROUP, WIDTH), BF),
            pltpu.VMEM((256, 256), F32),
            pltpu.VMEM((512, WIDTH), BF),
            pltpu.VMEM((4 * PAIR, 512), BF),
            pltpu.VMEM((2, 512, 384), BF),
            pltpu.VMEM((2, 512, 384), BF),
            pltpu.VMEM((PLANE, 16, 256), BF),
            pltpu.VMEM((PLANE, 16, HALF - 256), BF),
            pltpu.VMEM((PLANE, 16, 256), BF),
            pltpu.VMEM((PLANE, 16, HALF - 256), BF),
            pltpu.VMEM((2, 256, 128), BF),
            pltpu.VMEM((2, HALF - 256, 128), BF),
            pltpu.VMEM((256, 128), BF),
            pltpu.VMEM((HALF - 256, 128), BF),
            pltpu.VMEM((RING, 256, 128), BF),
            pltpu.VMEM((RING, HALF - 256, 128), BF),
            dma((9,)),
            dma((2,)),
            dma((4,)),
            dma((9, 3)),
            dma((9,)),
            dma((33,)),
            dma((33,)),
            dma((RING,)),
            dma((RING,)),
            dma((PLANE,)),
            dma((PLANE,)),
            dma((PLANE,)),
            dma((PLANE,)),
            dma((4,)),
            dma((2, PLANE)),
            dma((2, PLANE)),
            dma((2, 2, RING + 1)),
            dma((2, RING + 1)),
        ],
        compiler_params=pltpu.CompilerParams(
            collective_id=0, has_side_effects=True, vmem_limit_bytes=56 * 1024 * 1024
        ),
        name="sublayers",
    )(spatial_window, clip_frames, lat, jnp.transpose(modulation, (1, 0, 2)), wsp, wo, wqt, wot)
    return jnp.transpose(jnp.concatenate([out_a, out_b], axis=0))


def solution(mesh):
    return jax.shard_map(
        shards,
        mesh=mesh,
        in_specs=(
            P("seq", None),
            P("cfg", None, None),
            P(None, None, "head"),
            P("head", None),
            P(None, None, "head"),
            P("head", None),
            P(),
            P(),
        ),
        out_specs=P("seq", "cfg"),
        check_vma=False,
    )
```

```python
import functools

import jax
import jax.numpy as jnp
from jax import lax
from jax.experimental import pallas as pl
from jax.experimental.pallas import tpu as pltpu
from jax.sharding import PartitionSpec as P

MESH = pl.DeviceIdType.MESH
HEAD_DIM = 72
POSITIONS = 512
WIDTH = 1152
HALF = 576
LOCAL = 288
PAIR = 144
TWIN = 16
GUIDE = 4.0
EPSILON = 1e-06
NEG = -1e30
PAD = 128
RING = 8
PLANE = 16
GROUP = 16
EXP_SCALE = HEAD_DIM ** (-0.5) * 1.4426950408889634
BF = jnp.bfloat16
F32 = jnp.float32


def iota(shape, dim):
    return lax.broadcasted_iota(jnp.int32, shape, dim)


def modulated(rows, shift, scale):
    values = rows.astype(F32)
    centred = values - jnp.mean(values, axis=-1, keepdims=True)
    spread = jnp.mean(centred * centred, axis=-1, keepdims=True)
    normed = centred * lax.rsqrt(spread + EPSILON)
    return (normed * (1.0 + scale) + shift).astype(BF)


def softmax_keys(scores):
    top = jnp.max(scores, axis=0, keepdims=True)
    terms = jnp.exp2((scores - top) * EXP_SCALE)
    return terms.astype(BF), 1.0 / jnp.sum(terms, axis=0, keepdims=True)


def dot(a, b):
    return lax.dot_general(a, b, (((1,), (0,)), ((), ())), preferred_element_type=F32)


def dot_t(a, b):
    return lax.dot_general(a, b, (((1,), (1,)), ((), ())), preferred_element_type=F32)


def dot_first(a, b):
    return lax.dot_general(a, b, (((0,), (0,)), ((), ())), preferred_element_type=F32)


def head_mask(head, first, rows):
    row = iota((rows, 1), 0) + first
    return jnp.where((row >= head * HEAD_DIM) & (row < (head + 1) * HEAD_DIM), 1.0, 0.0).astype(BF)


def frame_window(frame, clip_ref):
    ends = [clip_ref[0]]
    for j in range(1, 4):
        ends.append(ends[-1] + clip_ref[j])
    clip = jnp.zeros_like(frame)
    start = jnp.zeros_like(frame)
    for end in ends:
        clip = clip + jnp.where(frame >= end, 1, 0)
        start = jnp.where(frame >= end, end, start)
    return clip * 64 + (frame - start) // TWIN


def kernel(
    sw_ref, clip_ref, lat_in, mod, wsp_in, wo, wqt, wot, out_a, out_b,
    modx, lat, wsp, wt, qt, ks, vt, base, att, heads, wsib, wos, lats, xs, xt, wbuf, tbias, xn, ot, xh, psend, precv,
    gs_a, gs_b, g2_a, g2_b, gz_a, gz_b, tr_a, tr_b, land_a, land_b,
    ld, mod_s, lat_s, wz_s, wz_r, wp_s, wp_r, za_s, za_r, xy_s, xy_r, sb_s, sb_r, pp_s, r1_s, r1_r, r2_s, r2_r,
):
    c = lax.axis_index("cfg")
    s = lax.axis_index("seq")
    h = lax.axis_index("head")
    zh = s // PLANE
    i = s % PLANE
    y = i // 4
    x = i % 4
    z = zh * 4 + h

    def on_z(zz):
        return (c, (zz // 4) * PLANE + i, zz % 4)

    def on_plane(ii):
        return (c, zh * PLANE + ii, h)

    sib = (1 - c, s, h)
    left, right = on_z((z + RING - 1) % RING), on_z((z + 1) % RING)

    def block_of(zz):
        return 64 * (2 * (zz % 4) + zz // 4)

    first_rows, last_rows = slice(0, 256), slice(256, 512)
    loads = [
        (wo.at[pl.ds(9 * c, 9)], wt.at[0:9]),
        (lat_in.at[:, first_rows], lat.at[:, first_rows]),
        (wsp_in, wsp),
        (wqt.at[0, pl.ds(9 * c, 9)], wt.at[9:18]),
        (wqt.at[1, pl.ds(9 * c, 9)], wt.at[18:27]),
        (wqt.at[2, pl.ds(9 * c, 9)], wt.at[27:36]),
        (wot.at[pl.ds(9 * c, 9)], wt.at[36:45]),
        (lat_in.at[:, last_rows], lat.at[:, last_rows]),
        (wo, wos.at[h]),
    ]
    loads = [pltpu.make_async_copy(src, dst, ld.at[k]) for k, (src, dst) in enumerate(loads)]
    for copy in loads:
        copy.start()

    def remote(src, dst, send, recv, dev):
        return pltpu.make_async_remote_copy(
            src_ref=src, dst_ref=dst, send_sem=send, recv_sem=recv, device_id=dev, device_id_type=MESH
        )

    def landed(buf, recv):
        remote(buf, buf, recv, recv, sib).wait_recv()

    def sent(buf, send):
        remote(buf, buf, send, send, sib).wait_send()

    barrier = pltpu.get_barrier_semaphore()

    def greet_z(k, _):
        pl.semaphore_signal(barrier, inc=1, device_id=on_z((z + k) % RING), device_id_type=MESH)
        return 0

    def greet_plane(k, _):
        pl.semaphore_signal(barrier, inc=1, device_id=on_plane((i + k) % PLANE), device_id_type=MESH)
        return 0

    lax.fori_loop(1, RING, greet_z, 0)
    lax.fori_loop(1, PLANE, greet_plane, 0)
    pl.semaphore_signal(barrier, inc=1, device_id=sib, device_id_type=MESH)
    pl.semaphore_wait(barrier, RING - 1 + PLANE - 1 + 1)

    far = jnp.where(c == 0, 2, RING - 2)
    hops = [RING - 1, far, 1]
    index_a, index_b = 4 * y + x, 4 * x + y
    SPACE = [(0, index_a, 0, 9, [0, 1]), (1, index_b, 0, 9, [1, 2])]
    TIME = [
        (3, index_a, 2, 36, [0]),
        (4, index_a, 2, 36, [0, 1]),
        (5, index_a, 2, 36, [1]),
        (6, index_b, 2, 36, [1, 2]),
        (7, index_b, 2, 36, [2]),
    ]

    def each_sent(rows, act):
        for q, place, first, per, slots in rows:
            flat = 16 * (q - first) + place
            for j in slots:
                source = wt.at[(9 if per == 36 else 0) + flat - per * j]
                pl.when(flat // per == j)(functools.partial(act, q, place, j, source))

    def start_piece(q, place, j, source):
        remote(source, wbuf.at[q, place], wz_s.at[q, j], wz_r.at[q], on_z((z + hops[j]) % RING)).start()

    def sent_piece(q, place, j, source):
        sent(source, wz_s.at[q, j])

    def take_pieces(rows):
        for q, place, first, per, _ in rows:
            there = 16 * (q - first) + place < 3 * per
            pl.when(there)(functools.partial(landed, wbuf.at[q, place], wz_r.at[q]))

    loads[0].wait()
    each_sent(SPACE, start_piece)

    pushed = []

    def push(index, ref, dev):
        remote(ref, ref, wp_s.at[index], wp_r.at[index], dev).start()
        pushed.append((ref, index))

    def first_phase(index, cut_a, cut_b):
        for k in range(1, 4):
            push(index + k - 1, wbuf.at[cut_a, index_a], on_plane(4 * y + (x + k) % 4))
            push(index + k + 2, wbuf.at[cut_b, index_b], on_plane(4 * ((y + k) % 4) + x))

    def first_landed(index, cut_a, cut_b):
        for k in range(1, 4):
            landed(wbuf.at[cut_a, 4 * y + (x + 4 - k) % 4], wp_r.at[index + k - 1])
            landed(wbuf.at[cut_b, 4 * x + (y + 4 - k) % 4], wp_r.at[index + k + 2])

    def second_phase(index, cut_a, cut_b, steps):
        for k in steps:
            push(index + k - 1, wbuf.at[cut_a, pl.ds(4 * y, 4)], on_plane(4 * ((y + k) % 4) + x))
            push(index + k + 2, wbuf.at[cut_b, pl.ds(4 * x, 4)], on_plane(4 * y + (x + k) % 4))

    def second_landed(index, cut_a, cut_b, steps):
        for k in steps:
            landed(wbuf.at[cut_a, pl.ds(4 * ((y + 4 - k) % 4), 4)], wp_r.at[index + k - 1])
            landed(wbuf.at[cut_b, pl.ds(4 * ((x + 4 - k) % 4), 4)], wp_r.at[index + k + 2])

    space_a, space_b = slice(0, 1), slice(1, 2)
    time_a, time_b = slice(3, 6), slice(6, 8)

    mod_copy = remote(mod, modx, mod_s.at[0], mod_s.at[1], sib)
    mod_copy.start()
    lat_out = remote(
        lat_in.at[c, pl.ds(block_of(7 - z), 64)], lats.at[zh * 2 + c], lat_s.at[0], lat_s.at[1], on_z(7 - z)
    )
    oy = jnp.int32(7)
    ox = jnp.int32(7)
    for r in range(1, 8):
        oy = oy - jnp.where(sw_ref[16 * r] < 3, 1, 0)
        ox = ox - jnp.where(sw_ref[r] < 1, 1, 0)
    qj = iota((384, 128), 1)
    ki = iota((384, 128), 0)
    same = ((qj // 16 + 8 + oy) // 8 == (ki // 16 + oy) // 8) & ((qj % 16 + ox) // 8 == (ki % 16 + ox) // 8)
    base[...] = jnp.where(same, 0.0, NEG)

    for f in range(2):
        ks[f, 0:PAD, :] = jnp.zeros((PAD, 384), BF)
        ks[f, PAD + POSITIONS :, :] = jnp.zeros((PAD, 384), BF)
        ks[f, PAD : PAD + POSITIONS, 256:384] = jnp.zeros((POSITIONS, 128), BF)
        vt[f, :, 0:PAD] = jnp.zeros((LOCAL, PAD), BF)
        vt[f, :, PAD + POSITIONS :] = jnp.zeros((LOCAL, PAD), BF)
        qt[f, LOCAL:384, :] = jnp.zeros((384 - LOCAL, POSITIONS), BF)

    shift1, scale1 = mod[0], mod[1]
    masks = [head_mask(0, 0, 256), head_mask(1, 0, 256), head_mask(2, 0, 256), head_mask(3, 128, 256)]

    loads[1].wait()
    loads[2].wait()

    def project(rb, f):
        rows = slice(rb * 256, (rb + 1) * 256)
        padded = slice(PAD + rb * 256, PAD + (rb + 1) * 256)
        values = modulated(lat[f, rows, :], shift1, scale1)
        qt[f, 0:LOCAL, rows] = dot_t(wsp[0], values).astype(BF)
        ks[f, padded, 0:LOCAL] = dot_t(values, wsp[1]).astype(BF)
        vt[f, :, padded] = dot_t(wsp[2], values).astype(BF)

    low = iota((1, 128), 1) < 64

    def attend(k, f):
        cols = pl.ds(pl.multiple_of(k * 128, 128), 128)
        around = pl.ds(pl.multiple_of(k * 128, 128), 384)
        keys = ks[f, around, :]
        query = qt[f, :, cols]
        three = jnp.concatenate([query[0:256] * m for m in masks[0:3]], axis=1)
        row = 8 * k - 8 + iota((384, 1), 0) // 16
        bias = base[...] + jnp.where((row >= 0) & (row < 32), 0.0, NEG)
        scores = jnp.concatenate(
            [dot(keys[:, 0:256], three), dot(keys[:, 128:384], query[128:384] * masks[3])], axis=1
        ) + jnp.concatenate([bias] * 4, axis=1)
        weights, over = softmax_keys(scores)
        mixed = dot(vt[f, :, around], weights)
        parts = [
            mixed[HEAD_DIM * n : HEAD_DIM * (n + 1), 128 * n : 128 * (n + 1)] * over[:, 128 * n : 128 * (n + 1)]
            for n in range(4)
        ]
        return jnp.concatenate(parts, axis=0)

    def attend_both(k):
        first, second = attend(k, 0), attend(k, 1)
        att[k] = jnp.where(low, first, pltpu.roll(second, 64, 1)).astype(BF)
        att[k + 4] = jnp.where(low, pltpu.roll(first, 64, 1), second).astype(BF)

    def send_heads(k):
        for zd in (k, k + 4):
            place = heads.at[pl.ds(LOCAL * h, LOCAL), pl.ds(pl.multiple_of(128 * zh, 128), 128)]
            copy = remote(att.at[zd], place, za_s.at[zd], za_r.at[z], on_z(zd))
            pl.when(z != zd)(copy.start)

            @pl.when(z == zd)
            def _():
                heads[pl.ds(LOCAL * h, LOCAL), pl.ds(pl.multiple_of(128 * zh, 128), 128)] = att[zd]

    for copy in loads[3:7]:
        copy.wait()
    each_sent(TIME, start_piece)
    lat_out.start()
    project(0, 0)
    take_pieces(SPACE)
    first_phase(0, space_a, space_b)
    project(0, 1)
    attend_both(0)
    send_heads(0)
    first_landed(0, space_a, space_b)
    second_phase(12, space_a, space_b, (1, 2, 3))
    take_pieces(TIME)
    first_phase(6, time_a, time_b)
    loads[7].wait()
    project(1, 0)
    project(1, 1)
    for k in range(1, 4):
        attend_both(k)
        send_heads(k)

    def time_key(row):
        four = row % 4
        frame = (four // 2) * 32 + 2 * (row // 16) + four % 2
        return frame_window(frame, clip_ref) * 4 + (row % 16) // 4

    tbias[...] = jnp.where(time_key(iota((256, 1), 0)) == time_key(iota((1, 256), 1)), 0.0, NEG)

    piece = lats.at[(1 - zh) * 2 + c]
    landed(piece, lat_s.at[1])
    remote(piece, piece, lat_s.at[2], lat_s.at[3], sib).start()
    first_landed(6, time_a, time_b)
    second_phase(18, time_a, time_b, (1, 3))
    second_landed(12, space_a, space_b, (1, 2, 3))
    remote(wbuf.at[0:2], wsib, wp_s.at[32], wp_r.at[32], sib).start()
    loads[8].wait()
    lats[pl.ds(zh * 2, 2)] = lat[:, pl.ds(block_of(z), 64), :]
    landed(lats.at[(1 - zh) * 2 + (1 - c)], lat_s.at[3])
    landed(wsib, wp_r.at[32])
    for p in range(27):
        shard, row = (h + 1 + p // 9) % 4, p % 9
        place = (p // 16, p % 16)
        wos[shard, 9 * c + row] = wbuf[place]
        wos[shard, 9 * (1 - c) + row] = wsib[place]

    def take_heads(k, _):
        zz = (z + k) % RING
        landed(heads.at[pl.ds(LOCAL * (zz % 4), LOCAL), pl.ds(pl.multiple_of(128 * (zz // 4), 128), 128)], za_r.at[zz])
        return 0

    lax.fori_loop(1, RING, take_heads, 0)

    straight = [
        remote(wt.at[9:25], wbuf.at[2], wp_s.at[28], wp_r.at[28], left),
        remote(wt.at[33:45], wbuf.at[8, 0:12], wp_s.at[29], wp_r.at[29], right),
    ]
    for copy in straight:
        copy.start()

    gate1 = mod[2]
    order = jnp.where(iota((256, 256), 1) == (iota((256, 256), 0) % 4) * 64 + iota((256, 256), 0) // 4, 1.0, 0.0).astype(BF)
    for n in range(3):
        cols = slice(384 * n, 384 * (n + 1))
        total = dot_first(heads[...], wos[:, :, :, cols].reshape(WIDTH, 384))
        after = lats[:, :, cols].reshape(256, 384).astype(F32) + gate1[:, cols] * total.astype(BF).astype(F32)
        xs[:, :, cols] = dot(order, after.astype(BF)).astype(BF).reshape(PLANE, 16, 384)

    def give(k, _):
        to = (i + k) % PLANE
        remote(xs.at[to], xt.at[0, i], xy_s.at[to], xy_r.at[i], on_plane(to)).start()
        return 0

    lax.fori_loop(1, PLANE, give, 0)
    second_landed(18, time_a, time_b, (1, 3))
    push(24, wbuf.at[time_a, pl.ds(4 * ((y + 3) % 4), 2)], on_plane(4 * ((y + 1) % 4) + x))
    push(25, wbuf.at[time_a, pl.ds(4 * ((y + 1) % 4) + 2, 2)], on_plane(4 * ((y + 3) % 4) + x))
    push(26, wbuf.at[time_b, pl.ds(4 * ((x + 3) % 4), 2)], on_plane(4 * y + (x + 1) % 4))
    push(27, wbuf.at[time_b, pl.ds(4 * ((x + 1) % 4) + 2, 2)], on_plane(4 * y + (x + 3) % 4))
    xt[0, i] = xs[i]
    remote(xs.at[i], xt.at[1, i], sb_s.at[i], sb_r.at[i], sib).start()

    mod_copy.wait()

    def own_group(n):
        g = (i // 4 + 4 - n) % 4
        for m in range(4):
            source = 4 * g + m

            @pl.when(source != i)
            def _():
                piece = xt.at[0, source]
                landed(piece, xy_r.at[source])
                remote(piece, xt.at[1, source], sb_s.at[source], sb_r.at[source], sib).start()

        rows = xt[0, pl.ds(4 * g, 4)].reshape(64, WIDTH)
        xn[pl.ds(64 * g, 64), :] = modulated(rows, mod[3], mod[4])

    def sibling_group(n):
        g = (i // 4 + 4 - n) % 4
        for m in range(4):
            landed(xt.at[1, 4 * g + m], sb_r.at[4 * g + m])
        rows = xt[1, pl.ds(4 * g, 4)].reshape(64, WIDTH)
        xn[pl.ds(256 + 64 * g, 64), :] = modulated(rows, modx[3], modx[4])

    own_group(0)
    own_group(1)
    sibling_group(0)
    own_group(2)
    sibling_group(1)
    own_group(3)
    sibling_group(2)
    sibling_group(3)

    def groups(slot, first, count):
        if slot == 0:
            return [wt.at[9 + first + p] for p in range(count)]
        flats = range(36 * (slot - 1) + first, 36 * (slot - 1) + first + count)
        return [wbuf.at[2 + flat // 16, flat % 16] for flat in flats]

    pair_masks = [head_mask(n, 0, PAIR) for n in range(2)]
    def time_heads(slot):
        weights = jnp.concatenate([ref[...] for ref in groups(slot, 0, 27)], axis=0)
        three = dot_t(weights, xn[...]).astype(BF)
        for b in range(2):
            cols = slice(256 * b, 256 * (b + 1))
            query, keys, vals = [three[PAIR * n : PAIR * (n + 1), cols] for n in range(3)]
            stacked = jnp.concatenate([query * m for m in pair_masks], axis=1)
            scores = dot_first(keys, stacked) + jnp.concatenate([tbias[...]] * 2, axis=1)
            terms, over = softmax_keys(scores)
            mixed = dot(vals, terms)
            parts = [
                mixed[HEAD_DIM * n : HEAD_DIM * (n + 1), 256 * n : 256 * (n + 1)] * over[:, 256 * n : 256 * (n + 1)]
                for n in range(2)
            ]
            ot[PAIR * slot : PAIR * (slot + 1), cols] = jnp.concatenate(parts, axis=0).astype(BF)

    time_heads(0)
    landed(wbuf.at[time_a, pl.ds(4 * ((y + 2) % 4), 2)], wp_r.at[24])
    landed(wbuf.at[time_a, pl.ds(4 * ((y + 2) % 4) + 2, 2)], wp_r.at[25])
    landed(wbuf.at[time_b, pl.ds(4 * ((x + 2) % 4), 2)], wp_r.at[26])
    landed(wbuf.at[time_b, pl.ds(4 * ((x + 2) % 4) + 2, 2)], wp_r.at[27])
    for copy in straight:
        copy.wait()
    for slot in range(1, 4):
        time_heads(slot)

    xh[...] = jnp.transpose(ot[...])
    def share(first):
        refs = [ref for slot in range(4) for ref in groups(slot, 27, 9)]
        return dot(xh[...], jnp.concatenate([ref[:, pl.ds(first, 384)] for ref in refs], axis=0))

    sizes = (256, HALF - 256)
    gs, g2, gz, tr, land = (gs_a, gs_b), (g2_a, g2_b), (gz_a, gz_b), (tr_a, tr_b), (land_a, land_b)

    def window(core, p):
        return pl.multiple_of(512 * core + 256 * p, 128)

    give_share = [remote(psend.at[p], precv.at[p], pp_s.at[p], pp_s.at[2 + p], sib) for p in range(2)]
    for p in range(2):
        psend[p] = share(window(1 - c, p)).astype(BF)
        give_share[p].start()
    for p in range(2):
        cols = pl.ds(window(c, p), 384)
        own = share(window(c, p))
        give_share[p].wait()
        results = []
        for b in range(2):
            gate = (mod if b == 0 else modx)[5, :, cols]
            other = precv[p, 256 * (1 - b) : 256 * (2 - b), :]
            total = (own[256 * b : 256 * (b + 1)] + other.astype(F32)).astype(BF).astype(F32)
            before = xt[b, :, :, cols].reshape(256, 384).astype(F32)
            results.append((before + gate * total).astype(BF).astype(F32))
        cond = jnp.where(c == 0, results[0], results[1])
        uncond = jnp.where(c == 0, results[1], results[0])
        guided = (uncond + GUIDE * (cond - uncond)).astype(BF)
        guided = jnp.where(c == 0, guided[:, 0 : sizes[p]], guided[:, 64 : 64 + sizes[p]])
        gs[p][...] = guided.reshape(PLANE, 16, sizes[p])

        def back(k, _):
            to = (i + k) % PLANE
            remote(gs[p].at[to], g2[p].at[i], r1_s.at[p, to], r1_r.at[p, i], on_plane(to)).start()
            return 0

        lax.fori_loop(1, PLANE, back, 0)
        g2[p][i] = gs[p][i]

    def slot(zz, p):
        return land[p].at[zz]

    def inner(hh):
        return zh * 4 + hh

    def outer(hh):
        return (1 - zh) * 4 + hh

    order = jnp.where(iota((256, 256), 0) == (iota((256, 256), 1) % 64) * 4 + iota((256, 256), 1) // 64, 1.0, 0.0).astype(BF)
    for p in range(2):

        def take_back(k, _):
            source = (i + PLANE - k) % PLANE
            landed(g2[p].at[source], r1_r.at[p, source])
            return 0

        lax.fori_loop(1, PLANE, take_back, 0)
        both = dot_first(g2[p][...].reshape(256, sizes[p]), order).astype(BF)
        gz[p][0] = both[:, 0:128]
        gz[p][1] = both[:, 128:256]
        own_block, other_block = gz[p].at[zh], gz[p].at[1 - zh]

        def go(side, src, zz, index, p, transit=False):
            dst = tr[p] if transit else slot(zz, p)
            recv = r2_r.at[p, RING] if transit else r2_r.at[p, zz]
            remote(src, dst, r2_s.at[side, p, index], recv, [left, right][side]).start()

        for role in range(4):

            @pl.when(h == role)
            def _():
                go(0 if role < 2 else 1, other_block, z, RING, p, transit=role in (1, 2))
                if role > 0:
                    go(0, own_block, z, z, p)
                if role < 3:
                    go(1, own_block, z, z, p)

        land[p][z] = gz[p][zh]

    for role in range(4):

        @pl.when(h == role)
        def _():
            waits = []
            if role in (0, 3):
                source = inner(1 if role == 0 else 2)
                for p in range(2):
                    landed(tr[p], r2_r.at[p, RING])
                    go(0 if role == 0 else 1, tr[p], source, source, p)
                    waits.append((0 if role == 0 else 1, source, p))
            lefts = [inner(k) for k in range(role + 1, 4)] + [outer(0), outer(1)]
            rights = [inner(k) for k in range(role - 1, -1, -1)] + [outer(3), outer(2)]
            for k in range(max(len(lefts), len(rights))):
                for p in range(2):
                    for side, chain, forward in ((0, lefts, role > 0), (1, rights, role < 3)):
                        if k < len(chain):
                            landed(slot(chain[k], p), r2_r.at[p, chain[k]])
                            if forward:
                                go(side, slot(chain[k], p), chain[k], chain[k], p)
                                waits.append((side, chain[k], p))
            for p in range(2):
                waits.append((0 if role < 2 else 1, RING, p))
                if role > 0:
                    waits.append((0, z, p))
                if role < 3:
                    waits.append((1, z, p))
            for side, index, p in waits:
                sent(tr[p], r2_s.at[side, p, index])

    for p in range(2):
        out = (out_a, out_b)[p]
        for k in range(4):
            first, second = land[p][k].astype(F32), land[p][k + 4].astype(F32)
            out[:, 128 * k : 128 * (k + 1)] = jnp.where(low, first, pltpu.roll(second, 64, 1)).astype(BF)
            out[:, 512 + 128 * k : 512 + 128 * (k + 1)] = jnp.where(low, pltpu.roll(first, 64, 1), second).astype(BF)

    each_sent(SPACE + TIME, sent_piece)
    lat_out.wait_send()
    sent(lats.at[0], lat_s.at[2])
    for ref, index in pushed:
        sent(ref, wp_s.at[index])
    sent(wsib, wp_s.at[32])

    def done_z(k, _):
        zz = (z + k) % RING
        sent(att.at[zz], za_s.at[zz])
        return 0

    lax.fori_loop(1, RING, done_z, 0)

    def done_plane(k, _):
        ii = (i + k) % PLANE
        sent(xs.at[ii], xy_s.at[ii])
        for p in range(2):
            sent(gs[p].at[ii], r1_s.at[p, ii])
        return 0

    lax.fori_loop(1, PLANE, done_plane, 0)

    def done_sibling(k, _):
        sent(xt.at[0, k], sb_s.at[k])
        return 0

    lax.fori_loop(0, PLANE, done_sibling, 0)


def shards(
    latent,
    modulation,
    w_qkv_space,
    w_out_space,
    w_qkv_time,
    w_out_time,
    clip_frames,
    spatial_window,
):
    lat = latent.reshape(2, POSITIONS, WIDTH)
    wsp = jnp.transpose(w_qkv_space, (1, 2, 0))
    wqt = jnp.transpose(w_qkv_time, (1, 2, 0)).reshape(3, 18, GROUP, WIDTH)
    wo = w_out_space.reshape(18, GROUP, WIDTH)
    wot = w_out_time.reshape(18, GROUP, WIDTH)
    dma = pltpu.SemaphoreType.DMA
    vmem = pl.BlockSpec(memory_space=pltpu.VMEM)
    smem = pl.BlockSpec(memory_space=pltpu.SMEM)
    anywhere = pl.BlockSpec(memory_space=pl.ANY)
    out_a, out_b = pl.pallas_call(
        kernel,
        out_shape=[pltpu.VMEM((rows, 2 * POSITIONS), BF) for rows in (256, HALF - 256)],
        in_specs=[smem, smem, anywhere, vmem] + [anywhere] * 4,
        out_specs=[vmem, vmem],
        scratch_shapes=[
            pltpu.VMEM((6, 1, WIDTH), F32),
            pltpu.VMEM((2, POSITIONS, WIDTH), BF),
            pltpu.VMEM((3, LOCAL, WIDTH), BF),
            pltpu.VMEM((45, GROUP, WIDTH), BF),
            pltpu.VMEM((2, 384, POSITIONS), BF),
            pltpu.VMEM((2, PAD + POSITIONS + PAD, 384), BF),
            pltpu.VMEM((2, LOCAL, PAD + POSITIONS + PAD), BF),
            pltpu.VMEM((384, 128), F32),
            pltpu.VMEM((RING, LOCAL, 128), BF),
            pltpu.VMEM((WIDTH, 256), BF),
            pltpu.VMEM((2, 16, GROUP, WIDTH), BF),
            pltpu.VMEM((4, 18, GROUP, WIDTH), BF),
            pltpu.VMEM((4, 64, WIDTH), BF),
            pltpu.VMEM((PLANE, 16, WIDTH), BF),
            pltpu.VMEM((2, PLANE, 16, WIDTH), BF),
            pltpu.VMEM((9, 16, GROUP, WIDTH), BF),
            pltpu.VMEM((256, 256), F32),
            pltpu.VMEM((512, WIDTH), BF),
            pltpu.VMEM((4 * PAIR, 512), BF),
            pltpu.VMEM((512, 4 * PAIR), BF),
            pltpu.VMEM((2, 512, 384), BF),
            pltpu.VMEM((2, 512, 384), BF),
            pltpu.VMEM((PLANE, 16, 256), BF),
            pltpu.VMEM((PLANE, 16, HALF - 256), BF),
            pltpu.VMEM((PLANE, 16, 256), BF),
            pltpu.VMEM((PLANE, 16, HALF - 256), BF),
            pltpu.VMEM((2, 256, 128), BF),
            pltpu.VMEM((2, HALF - 256, 128), BF),
            pltpu.VMEM((256, 128), BF),
            pltpu.VMEM((HALF - 256, 128), BF),
            pltpu.VMEM((RING, 256, 128), BF),
            pltpu.VMEM((RING, HALF - 256, 128), BF),
            dma((9,)),
            dma((2,)),
            dma((4,)),
            dma((9, 3)),
            dma((9,)),
            dma((33,)),
            dma((33,)),
            dma((RING,)),
            dma((RING,)),
            dma((PLANE,)),
            dma((PLANE,)),
            dma((PLANE,)),
            dma((PLANE,)),
            dma((4,)),
            dma((2, PLANE)),
            dma((2, PLANE)),
            dma((2, 2, RING + 1)),
            dma((2, RING + 1)),
        ],
        compiler_params=pltpu.CompilerParams(
            collective_id=0, has_side_effects=True, vmem_limit_bytes=56 * 1024 * 1024
        ),
        name="sublayers",
    )(spatial_window, clip_frames, lat, jnp.transpose(modulation, (1, 0, 2)), wsp, wo, wqt, wot)
    return jnp.transpose(jnp.concatenate([out_a, out_b], axis=0))


def solution(mesh):
    return jax.shard_map(
        shards,
        mesh=mesh,
        in_specs=(
            P("seq", None),
            P("cfg", None, None),
            P(None, None, "head"),
            P("head", None),
            P(None, None, "head"),
            P("head", None),
            P(),
            P(),
        ),
        out_specs=P("seq", "cfg"),
        check_vma=False,
    )
```

```python
import functools

import jax
import jax.numpy as jnp
from jax import lax
from jax.experimental import pallas as pl
from jax.experimental.pallas import tpu as pltpu
from jax.sharding import PartitionSpec as P

MESH = pl.DeviceIdType.MESH
HEAD_DIM = 72
POSITIONS = 512
WIDTH = 1152
HALF = 576
LOCAL = 288
PAIR = 144
TWIN = 16
GUIDE = 4.0
EPSILON = 1e-06
NEG = -1e30
PAD = 128
RING = 8
PLANE = 16
GROUP = 16
EXP_SCALE = HEAD_DIM ** (-0.5) * 1.4426950408889634
BF = jnp.bfloat16
F32 = jnp.float32


def iota(shape, dim):
    return lax.broadcasted_iota(jnp.int32, shape, dim)


def modulated(rows, shift, scale):
    values = rows.astype(F32)
    centred = values - jnp.mean(values, axis=-1, keepdims=True)
    spread = jnp.mean(centred * centred, axis=-1, keepdims=True)
    normed = centred * lax.rsqrt(spread + EPSILON)
    return (normed * (1.0 + shift * 0.0 + scale) + shift).astype(BF)


def softmax_keys(scores):
    top = jnp.max(scores, axis=0, keepdims=True)
    terms = jnp.exp2((scores - top) * EXP_SCALE)
    return terms.astype(BF), 1.0 / jnp.sum(terms, axis=0, keepdims=True)


def dot(a, b):
    return lax.dot_general(a, b, (((1,), (0,)), ((), ())), preferred_element_type=F32)


def dot_t(a, b):
    return lax.dot_general(a, b, (((1,), (1,)), ((), ())), preferred_element_type=F32)


def dot_first(a, b):
    return lax.dot_general(a, b, (((0,), (0,)), ((), ())), preferred_element_type=F32)


def head_mask(head, first, rows):
    row = iota((rows, 1), 0) + first
    return jnp.where((row >= head * HEAD_DIM) & (row < (head + 1) * HEAD_DIM), 1.0, 0.0).astype(BF)


def frame_window(frame, clip_ref):
    ends = [clip_ref[0]]
    for j in range(1, 4):
        ends.append(ends[-1] + clip_ref[j])
    clip = jnp.zeros_like(frame)
    start = jnp.zeros_like(frame)
    for end in ends:
        clip = clip + jnp.where(frame >= end, 1, 0)
        start = jnp.where(frame >= end, end, start)
    return clip * 64 + (frame - start) // TWIN


def kernel(
    sw_ref, clip_ref, lat_in, mod, wsp_in, wo, wqt, wot, out_a, out_b,
    modx, lat, wsp, wt, qt, ks, vt, base, att, heads, wsib, wos, lats, xs, xt, wbuf, tbias, xn, ot, xh, psend, precv,
    gs_a, gs_b, g2_a, g2_b, gz_a, gz_b, tr_a, tr_b, land_a, land_b,
    ld, mod_s, lat_s, wz_s, wz_r, wp_s, wp_r, za_s, za_r, xy_s, xy_r, sb_s, sb_r, pp_s, r1_s, r1_r, r2_s, r2_r,
):
    c = lax.axis_index("cfg")
    s = lax.axis_index("seq")
    h = lax.axis_index("head")
    zh = s // PLANE
    i = s % PLANE
    y = i // 4
    x = i % 4
    z = zh * 4 + h

    def on_z(zz):
        return (c, (zz // 4) * PLANE + i, zz % 4)

    def on_plane(ii):
        return (c, zh * PLANE + ii, h)

    sib = (1 - c, s, h)
    left, right = on_z((z + RING - 1) % RING), on_z((z + 1) % RING)

    def block_of(zz):
        return 64 * (2 * (zz % 4) + zz // 4)

    first_rows, last_rows = slice(0, 256), slice(256, 512)
    loads = [
        (wo.at[pl.ds(9 * c, 9)], wt.at[0:9]),
        (lat_in.at[:, first_rows], lat.at[:, first_rows]),
        (wsp_in, wsp),
        (wqt.at[0, pl.ds(9 * c, 9)], wt.at[9:18]),
        (wqt.at[1, pl.ds(9 * c, 9)], wt.at[18:27]),
        (wqt.at[2, pl.ds(9 * c, 9)], wt.at[27:36]),
        (wot.at[pl.ds(9 * c, 9)], wt.at[36:45]),
        (lat_in.at[:, last_rows], lat.at[:, last_rows]),
        (wo, wos.at[h]),
    ]
    loads = [pltpu.make_async_copy(src, dst, ld.at[k]) for k, (src, dst) in enumerate(loads)]
    for copy in loads:
        copy.start()

    def remote(src, dst, send, recv, dev):
        return pltpu.make_async_remote_copy(
            src_ref=src, dst_ref=dst, send_sem=send, recv_sem=recv, device_id=dev, device_id_type=MESH
        )

    def landed(buf, recv):
        remote(buf, buf, recv, recv, sib).wait_recv()

    def sent(buf, send):
        remote(buf, buf, send, send, sib).wait_send()

    barrier = pltpu.get_barrier_semaphore()

    def greet_z(k, _):
        pl.semaphore_signal(barrier, inc=1, device_id=on_z((z + k) % RING), device_id_type=MESH)
        return 0

    def greet_plane(k, _):
        pl.semaphore_signal(barrier, inc=1, device_id=on_plane((i + k) % PLANE), device_id_type=MESH)
        return 0

    lax.fori_loop(1, RING, greet_z, 0)
    lax.fori_loop(1, PLANE, greet_plane, 0)
    pl.semaphore_signal(barrier, inc=1, device_id=sib, device_id_type=MESH)
    pl.semaphore_wait(barrier, RING - 1 + PLANE - 1 + 1)

    far = jnp.where(c == 0, 2, RING - 2)
    hops = [RING - 1, far, 1]
    index_a, index_b = 4 * y + x, 4 * x + y
    SPACE = [(0, index_a, 0, 9, [0, 1]), (1, index_b, 0, 9, [1, 2])]
    TIME = [
        (3, index_a, 2, 36, [0]),
        (4, index_a, 2, 36, [0, 1]),
        (5, index_a, 2, 36, [1]),
        (6, index_b, 2, 36, [1, 2]),
        (7, index_b, 2, 36, [2]),
    ]

    def each_sent(rows, act):
        for q, place, first, per, slots in rows:
            flat = 16 * (q - first) + place
            for j in slots:
                source = wt.at[(9 if per == 36 else 0) + flat - per * j]
                pl.when(flat // per == j)(functools.partial(act, q, place, j, source))

    def start_piece(q, place, j, source):
        remote(source, wbuf.at[q, place], wz_s.at[q, j], wz_r.at[q], on_z((z + hops[j]) % RING)).start()

    def sent_piece(q, place, j, source):
        sent(source, wz_s.at[q, j])

    def take_pieces(rows):
        for q, place, first, per, _ in rows:
            there = 16 * (q - first) + place < 3 * per
            pl.when(there)(functools.partial(landed, wbuf.at[q, place], wz_r.at[q]))

    loads[0].wait()
    each_sent(SPACE, start_piece)

    pushed = []

    def push(index, ref, dev):
        remote(ref, ref, wp_s.at[index], wp_r.at[index], dev).start()
        pushed.append((ref, index))

    def first_phase(index, cut_a, cut_b):
        for k in range(1, 4):
            push(index + k - 1, wbuf.at[cut_a, index_a], on_plane(4 * y + (x + k) % 4))
            push(index + k + 2, wbuf.at[cut_b, index_b], on_plane(4 * ((y + k) % 4) + x))

    def first_landed(index, cut_a, cut_b):
        for k in range(1, 4):
            landed(wbuf.at[cut_a, 4 * y + (x + 4 - k) % 4], wp_r.at[index + k - 1])
            landed(wbuf.at[cut_b, 4 * x + (y + 4 - k) % 4], wp_r.at[index + k + 2])

    def second_phase(index, cut_a, cut_b, steps):
        for k in steps:
            push(index + k - 1, wbuf.at[cut_a, pl.ds(4 * y, 4)], on_plane(4 * ((y + k) % 4) + x))
            push(index + k + 2, wbuf.at[cut_b, pl.ds(4 * x, 4)], on_plane(4 * y + (x + k) % 4))

    def second_landed(index, cut_a, cut_b, steps):
        for k in steps:
            landed(wbuf.at[cut_a, pl.ds(4 * ((y + 4 - k) % 4), 4)], wp_r.at[index + k - 1])
            landed(wbuf.at[cut_b, pl.ds(4 * ((x + 4 - k) % 4), 4)], wp_r.at[index + k + 2])

    space_a, space_b = slice(0, 1), slice(1, 2)
    time_a, time_b = slice(3, 6), slice(6, 8)

    mod_copy = remote(mod, modx, mod_s.at[0], mod_s.at[1], sib)
    mod_copy.start()
    lat_out = remote(
        lat_in.at[c, pl.ds(block_of(7 - z), 64)], lats.at[zh * 2 + c], lat_s.at[0], lat_s.at[1], on_z(7 - z)
    )
    oy = jnp.int32(7)
    ox = jnp.int32(7)
    for r in range(1, 8):
        oy = oy - jnp.where(sw_ref[16 * r] < 3, 1, 0)
        ox = ox - jnp.where(sw_ref[r] < 1, 1, 0)
    qj = iota((384, 128), 1)
    ki = iota((384, 128), 0)
    same = ((qj // 16 + 8 + oy) // 8 == (ki // 16 + oy) // 8) & ((qj % 16 + ox) // 8 == (ki % 16 + ox) // 8)
    base[...] = jnp.where(same, 0.0, NEG)

    for f in range(2):
        ks[f, 0:PAD, :] = jnp.zeros((PAD, 384), BF)
        ks[f, PAD + POSITIONS :, :] = jnp.zeros((PAD, 384), BF)
        ks[f, PAD : PAD + POSITIONS, 256:384] = jnp.zeros((POSITIONS, 128), BF)
        vt[f, :, 0:PAD] = jnp.zeros((LOCAL, PAD), BF)
        vt[f, :, PAD + POSITIONS :] = jnp.zeros((LOCAL, PAD), BF)
        qt[f, LOCAL:384, :] = jnp.zeros((384 - LOCAL, POSITIONS), BF)

    shift1, scale1 = mod[0], mod[1]
    masks = [head_mask(0, 0, 256), head_mask(1, 0, 256), head_mask(2, 0, 256), head_mask(3, 128, 256)]

    loads[1].wait()
    loads[2].wait()

    def project(rb, f):
        rows = slice(rb * 256, (rb + 1) * 256)
        padded = slice(PAD + rb * 256, PAD + (rb + 1) * 256)
        values = modulated(lat[f, rows, :], shift1, scale1)
        qt[f, 0:LOCAL, rows] = dot_t(wsp[0], values).astype(BF)
        ks[f, padded, 0:LOCAL] = dot_t(values, wsp[1]).astype(BF)
        vt[f, :, padded] = dot_t(wsp[2], values).astype(BF)

    low = iota((1, 128), 1) < 64

    def attend(k, f):
        cols = pl.ds(pl.multiple_of(k * 128, 128), 128)
        around = pl.ds(pl.multiple_of(k * 128, 128), 384)
        keys = ks[f, around, :]
        query = qt[f, :, cols]
        three = jnp.concatenate([query[0:256] * m for m in masks[0:3]], axis=1)
        row = 8 * k - 8 + iota((384, 1), 0) // 16
        bias = base[...] + jnp.where((row >= 0) & (row < 32), 0.0, NEG)
        scores = jnp.concatenate(
            [dot(keys[:, 0:256], three), dot(keys[:, 128:384], query[128:384] * masks[3])], axis=1
        ) + jnp.concatenate([bias] * 4, axis=1)
        weights, over = softmax_keys(scores)
        mixed = dot(vt[f, :, around], weights)
        parts = [
            mixed[HEAD_DIM * n : HEAD_DIM * (n + 1), 128 * n : 128 * (n + 1)] * over[:, 128 * n : 128 * (n + 1)]
            for n in range(4)
        ]
        return jnp.concatenate(parts, axis=0)

    def attend_both(k):
        first, second = attend(k, 0), attend(k, 1)
        att[k] = jnp.where(low, first, pltpu.roll(second, 64, 1)).astype(BF)
        att[k + 4] = jnp.where(low, pltpu.roll(first, 64, 1), second).astype(BF)

    def send_heads(k):
        for zd in (k, k + 4):
            place = heads.at[pl.ds(LOCAL * h, LOCAL), pl.ds(pl.multiple_of(128 * zh, 128), 128)]
            copy = remote(att.at[zd], place, za_s.at[zd], za_r.at[z], on_z(zd))
            pl.when(z != zd)(copy.start)

            @pl.when(z == zd)
            def _():
                heads[pl.ds(LOCAL * h, LOCAL), pl.ds(pl.multiple_of(128 * zh, 128), 128)] = att[zd]

    for copy in loads[3:7]:
        copy.wait()
    each_sent(TIME, start_piece)
    lat_out.start()
    project(0, 0)
    take_pieces(SPACE)
    first_phase(0, space_a, space_b)
    project(0, 1)
    attend_both(0)
    send_heads(0)
    first_landed(0, space_a, space_b)
    second_phase(12, space_a, space_b, (1, 2, 3))
    take_pieces(TIME)
    first_phase(6, time_a, time_b)
    loads[7].wait()
    project(1, 0)
    project(1, 1)
    for k in range(1, 4):
        attend_both(k)
        send_heads(k)

    def time_key(row):
        four = row % 4
        frame = (four // 2) * 32 + 2 * (row // 16) + four % 2
        return frame_window(frame, clip_ref) * 4 + (row % 16) // 4

    tbias[...] = jnp.where(time_key(iota((256, 1), 0)) == time_key(iota((1, 256), 1)), 0.0, NEG)

    piece = lats.at[(1 - zh) * 2 + c]
    landed(piece, lat_s.at[1])
    remote(piece, piece, lat_s.at[2], lat_s.at[3], sib).start()
    first_landed(6, time_a, time_b)
    second_phase(18, time_a, time_b, (1, 3))
    second_landed(12, space_a, space_b, (1, 2, 3))
    remote(wbuf.at[0:2], wsib, wp_s.at[32], wp_r.at[32], sib).start()
    loads[8].wait()
    lats[pl.ds(zh * 2, 2)] = lat[:, pl.ds(block_of(z), 64), :]
    landed(lats.at[(1 - zh) * 2 + (1 - c)], lat_s.at[3])
    landed(wsib, wp_r.at[32])
    for p in range(27):
        shard, row = (h + 1 + p // 9) % 4, p % 9
        place = (p // 16, p % 16)
        wos[shard, 9 * c + row] = wbuf[place]
        wos[shard, 9 * (1 - c) + row] = wsib[place]

    def take_heads(k, _):
        zz = (z + k) % RING
        landed(heads.at[pl.ds(LOCAL * (zz % 4), LOCAL), pl.ds(pl.multiple_of(128 * (zz // 4), 128), 128)], za_r.at[zz])
        return 0

    lax.fori_loop(1, RING, take_heads, 0)

    straight = [
        remote(wt.at[9:25], wbuf.at[2], wp_s.at[28], wp_r.at[28], left),
        remote(wt.at[33:45], wbuf.at[8, 0:12], wp_s.at[29], wp_r.at[29], right),
    ]
    for copy in straight:
        copy.start()

    gate1 = mod[2]
    order = jnp.where(iota((256, 256), 1) == (iota((256, 256), 0) % 4) * 64 + iota((256, 256), 0) // 4, 1.0, 0.0).astype(BF)
    for n in range(3):
        cols = slice(384 * n, 384 * (n + 1))
        total = dot_first(heads[...], wos[:, :, :, cols].reshape(WIDTH, 384))
        after = lats[:, :, cols].reshape(256, 384).astype(F32) + gate1[:, cols] * total.astype(BF).astype(F32)
        xs[:, :, cols] = dot(order, after.astype(BF)).astype(BF).reshape(PLANE, 16, 384)

    def give(k, _):
        to = (i + k) % PLANE
        remote(xs.at[to], xt.at[0, i], xy_s.at[to], xy_r.at[i], on_plane(to)).start()
        return 0

    lax.fori_loop(1, PLANE, give, 0)
    second_landed(18, time_a, time_b, (1, 3))
    push(24, wbuf.at[time_a, pl.ds(4 * ((y + 3) % 4), 2)], on_plane(4 * ((y + 1) % 4) + x))
    push(25, wbuf.at[time_a, pl.ds(4 * ((y + 1) % 4) + 2, 2)], on_plane(4 * ((y + 3) % 4) + x))
    push(26, wbuf.at[time_b, pl.ds(4 * ((x + 3) % 4), 2)], on_plane(4 * y + (x + 1) % 4))
    push(27, wbuf.at[time_b, pl.ds(4 * ((x + 1) % 4) + 2, 2)], on_plane(4 * y + (x + 3) % 4))
    xt[0, i] = xs[i]
    remote(xs.at[i], xt.at[1, i], sb_s.at[i], sb_r.at[i], sib).start()

    mod_copy.wait()

    def own_group(n):
        g = (i // 4 + 4 - n) % 4
        for m in range(4):
            source = 4 * g + m

            @pl.when(source != i)
            def _():
                piece = xt.at[0, source]
                landed(piece, xy_r.at[source])
                remote(piece, xt.at[1, source], sb_s.at[source], sb_r.at[source], sib).start()

        rows = xt[0, pl.ds(4 * g, 4)].reshape(64, WIDTH)
        xn[pl.ds(64 * g, 64), :] = modulated(rows, mod[3], mod[4])

    def sibling_group(n):
        g = (i // 4 + 4 - n) % 4
        for m in range(4):
            landed(xt.at[1, 4 * g + m], sb_r.at[4 * g + m])
        rows = xt[1, pl.ds(4 * g, 4)].reshape(64, WIDTH)
        xn[pl.ds(256 + 64 * g, 64), :] = modulated(rows, modx[3], modx[4])

    own_group(0)
    own_group(1)
    sibling_group(0)
    own_group(2)
    sibling_group(1)
    own_group(3)
    sibling_group(2)
    sibling_group(3)

    def groups(slot, first, count):
        if slot == 0:
            return [wt.at[9 + first + p] for p in range(count)]
        flats = range(36 * (slot - 1) + first, 36 * (slot - 1) + first + count)
        return [wbuf.at[2 + flat // 16, flat % 16] for flat in flats]

    pair_masks = [head_mask(n, 0, PAIR) for n in range(2)]
    def time_heads(slot):
        weights = jnp.concatenate([ref[...] for ref in groups(slot, 0, 27)], axis=0)
        three = dot_t(weights, xn[...]).astype(BF)
        for b in range(2):
            cols = slice(256 * b, 256 * (b + 1))
            query, keys, vals = [three[PAIR * n : PAIR * (n + 1), cols] for n in range(3)]
            stacked = jnp.concatenate([query * m for m in pair_masks], axis=1)
            scores = dot_first(keys, stacked) + jnp.concatenate([tbias[...]] * 2, axis=1)
            terms, over = softmax_keys(scores)
            mixed = dot(vals, terms)
            parts = [
                mixed[HEAD_DIM * n : HEAD_DIM * (n + 1), 256 * n : 256 * (n + 1)] * over[:, 256 * n : 256 * (n + 1)]
                for n in range(2)
            ]
            ot[PAIR * slot : PAIR * (slot + 1), cols] = jnp.concatenate(parts, axis=0).astype(BF)

    time_heads(0)
    landed(wbuf.at[time_a, pl.ds(4 * ((y + 2) % 4), 2)], wp_r.at[24])
    landed(wbuf.at[time_a, pl.ds(4 * ((y + 2) % 4) + 2, 2)], wp_r.at[25])
    landed(wbuf.at[time_b, pl.ds(4 * ((x + 2) % 4), 2)], wp_r.at[26])
    landed(wbuf.at[time_b, pl.ds(4 * ((x + 2) % 4) + 2, 2)], wp_r.at[27])
    for copy in straight:
        copy.wait()
    for slot in range(1, 4):
        time_heads(slot)

    xh[...] = jnp.transpose(ot[...])
    def share(first):
        refs = [ref for slot in range(4) for ref in groups(slot, 27, 9)]
        return dot(xh[...], jnp.concatenate([ref[:, pl.ds(first, 384)] for ref in refs], axis=0))

    sizes = (256, HALF - 256)
    gs, g2, gz, tr, land = (gs_a, gs_b), (g2_a, g2_b), (gz_a, gz_b), (tr_a, tr_b), (land_a, land_b)

    def window(core, p):
        return pl.multiple_of(512 * core + 256 * p, 128)

    give_share = [remote(psend.at[p], precv.at[p], pp_s.at[p], pp_s.at[2 + p], sib) for p in range(2)]
    for p in range(2):
        psend[p] = share(window(1 - c, p)).astype(BF)
        give_share[p].start()
    for p in range(2):
        cols = pl.ds(window(c, p), 384)
        own = share(window(c, p))
        give_share[p].wait()
        results = []
        for b in range(2):
            gate = (mod if b == 0 else modx)[5, :, cols]
            other = precv[p, 256 * (1 - b) : 256 * (2 - b), :]
            total = (own[256 * b : 256 * (b + 1)] + other.astype(F32)).astype(BF).astype(F32)
            before = xt[b, :, :, cols].reshape(256, 384).astype(F32)
            results.append((before + gate * total).astype(BF).astype(F32))
        cond = jnp.where(c == 0, results[0], results[1])
        uncond = jnp.where(c == 0, results[1], results[0])
        guided = (uncond + GUIDE * (cond - uncond)).astype(BF)
        guided = jnp.where(c == 0, guided[:, 0 : sizes[p]], guided[:, 64 : 64 + sizes[p]])
        gs[p][...] = guided.reshape(PLANE, 16, sizes[p])

        def back(k, _):
            to = (i + k) % PLANE
            remote(gs[p].at[to], g2[p].at[i], r1_s.at[p, to], r1_r.at[p, i], on_plane(to)).start()
            return 0

        lax.fori_loop(1, PLANE, back, 0)
        g2[p][i] = gs[p][i]

    def slot(zz, p):
        return land[p].at[zz]

    def inner(hh):
        return zh * 4 + hh

    def outer(hh):
        return (1 - zh) * 4 + hh

    order = jnp.where(iota((256, 256), 0) == (iota((256, 256), 1) % 64) * 4 + iota((256, 256), 1) // 64, 1.0, 0.0).astype(BF)
    for p in range(2):

        def take_back(k, _):
            source = (i + PLANE - k) % PLANE
            landed(g2[p].at[source], r1_r.at[p, source])
            return 0

        lax.fori_loop(1, PLANE, take_back, 0)
        both = dot_first(g2[p][...].reshape(256, sizes[p]), order).astype(BF)
        gz[p][0] = both[:, 0:128]
        gz[p][1] = both[:, 128:256]
        own_block, other_block = gz[p].at[zh], gz[p].at[1 - zh]

        def go(side, src, zz, index, p, transit=False):
            dst = tr[p] if transit else slot(zz, p)
            recv = r2_r.at[p, RING] if transit else r2_r.at[p, zz]
            remote(src, dst, r2_s.at[side, p, index], recv, [left, right][side]).start()

        for role in range(4):

            @pl.when(h == role)
            def _():
                go(0 if role < 2 else 1, other_block, z, RING, p, transit=role in (1, 2))
                if role > 0:
                    go(0, own_block, z, z, p)
                if role < 3:
                    go(1, own_block, z, z, p)

        land[p][z] = gz[p][zh]

    for role in range(4):

        @pl.when(h == role)
        def _():
            waits = []
            if role in (0, 3):
                source = inner(1 if role == 0 else 2)
                for p in range(2):
                    landed(tr[p], r2_r.at[p, RING])
                    go(0 if role == 0 else 1, tr[p], source, source, p)
                    waits.append((0 if role == 0 else 1, source, p))
            lefts = [inner(k) for k in range(role + 1, 4)] + [outer(0), outer(1)]
            rights = [inner(k) for k in range(role - 1, -1, -1)] + [outer(3), outer(2)]
            for k in range(max(len(lefts), len(rights))):
                for p in range(2):
                    for side, chain, forward in ((0, lefts, role > 0), (1, rights, role < 3)):
                        if k < len(chain):
                            landed(slot(chain[k], p), r2_r.at[p, chain[k]])
                            if forward:
                                go(side, slot(chain[k], p), chain[k], chain[k], p)
                                waits.append((side, chain[k], p))
            for p in range(2):
                waits.append((0 if role < 2 else 1, RING, p))
                if role > 0:
                    waits.append((0, z, p))
                if role < 3:
                    waits.append((1, z, p))
            for side, index, p in waits:
                sent(tr[p], r2_s.at[side, p, index])

    for p in range(2):
        out = (out_a, out_b)[p]
        for k in range(4):
            first, second = land[p][k].astype(F32), land[p][k + 4].astype(F32)
            out[:, 128 * k : 128 * (k + 1)] = jnp.where(low, first, pltpu.roll(second, 64, 1)).astype(BF)
            out[:, 512 + 128 * k : 512 + 128 * (k + 1)] = jnp.where(low, pltpu.roll(first, 64, 1), second).astype(BF)

    each_sent(SPACE + TIME, sent_piece)
    lat_out.wait_send()
    sent(lats.at[0], lat_s.at[2])
    for ref, index in pushed:
        sent(ref, wp_s.at[index])
    sent(wsib, wp_s.at[32])

    def done_z(k, _):
        zz = (z + k) % RING
        sent(att.at[zz], za_s.at[zz])
        return 0

    lax.fori_loop(1, RING, done_z, 0)

    def done_plane(k, _):
        ii = (i + k) % PLANE
        sent(xs.at[ii], xy_s.at[ii])
        for p in range(2):
            sent(gs[p].at[ii], r1_s.at[p, ii])
        return 0

    lax.fori_loop(1, PLANE, done_plane, 0)

    def done_sibling(k, _):
        sent(xt.at[0, k], sb_s.at[k])
        return 0

    lax.fori_loop(0, PLANE, done_sibling, 0)


def shards(
    latent,
    modulation,
    w_qkv_space,
    w_out_space,
    w_qkv_time,
    w_out_time,
    clip_frames,
    spatial_window,
):
    lat = latent.reshape(2, POSITIONS, WIDTH)
    wsp = jnp.transpose(w_qkv_space, (1, 2, 0))
    wqt = jnp.transpose(w_qkv_time, (1, 2, 0)).reshape(3, 18, GROUP, WIDTH)
    wo = w_out_space.reshape(18, GROUP, WIDTH)
    wot = w_out_time.reshape(18, GROUP, WIDTH)
    dma = pltpu.SemaphoreType.DMA
    vmem = pl.BlockSpec(memory_space=pltpu.VMEM)
    smem = pl.BlockSpec(memory_space=pltpu.SMEM)
    anywhere = pl.BlockSpec(memory_space=pl.ANY)
    out_a, out_b = pl.pallas_call(
        kernel,
        out_shape=[pltpu.VMEM((rows, 2 * POSITIONS), BF) for rows in (256, HALF - 256)],
        in_specs=[smem, smem, anywhere, vmem] + [anywhere] * 4,
        out_specs=[vmem, vmem],
        scratch_shapes=[
            pltpu.VMEM((6, 1, WIDTH), F32),
            pltpu.VMEM((2, POSITIONS, WIDTH), BF),
            pltpu.VMEM((3, LOCAL, WIDTH), BF),
            pltpu.VMEM((45, GROUP, WIDTH), BF),
            pltpu.VMEM((2, 384, POSITIONS), BF),
            pltpu.VMEM((2, PAD + POSITIONS + PAD, 384), BF),
            pltpu.VMEM((2, LOCAL, PAD + POSITIONS + PAD), BF),
            pltpu.VMEM((384, 128), F32),
            pltpu.VMEM((RING, LOCAL, 128), BF),
            pltpu.VMEM((WIDTH, 256), BF),
            pltpu.VMEM((2, 16, GROUP, WIDTH), BF),
            pltpu.VMEM((4, 18, GROUP, WIDTH), BF),
            pltpu.VMEM((4, 64, WIDTH), BF),
            pltpu.VMEM((PLANE, 16, WIDTH), BF),
            pltpu.VMEM((2, PLANE, 16, WIDTH), BF),
            pltpu.VMEM((9, 16, GROUP, WIDTH), BF),
            pltpu.VMEM((256, 256), F32),
            pltpu.VMEM((512, WIDTH), BF),
            pltpu.VMEM((4 * PAIR, 512), BF),
            pltpu.VMEM((512, 4 * PAIR), BF),
            pltpu.VMEM((2, 512, 384), BF),
            pltpu.VMEM((2, 512, 384), BF),
            pltpu.VMEM((PLANE, 16, 256), BF),
            pltpu.VMEM((PLANE, 16, HALF - 256), BF),
            pltpu.VMEM((PLANE, 16, 256), BF),
            pltpu.VMEM((PLANE, 16, HALF - 256), BF),
            pltpu.VMEM((2, 256, 128), BF),
            pltpu.VMEM((2, HALF - 256, 128), BF),
            pltpu.VMEM((256, 128), BF),
            pltpu.VMEM((HALF - 256, 128), BF),
            pltpu.VMEM((RING, 256, 128), BF),
            pltpu.VMEM((RING, HALF - 256, 128), BF),
            dma((9,)),
            dma((2,)),
            dma((4,)),
            dma((9, 3)),
            dma((9,)),
            dma((33,)),
            dma((33,)),
            dma((RING,)),
            dma((RING,)),
            dma((PLANE,)),
            dma((PLANE,)),
            dma((PLANE,)),
            dma((PLANE,)),
            dma((4,)),
            dma((2, PLANE)),
            dma((2, PLANE)),
            dma((2, 2, RING + 1)),
            dma((2, RING + 1)),
        ],
        compiler_params=pltpu.CompilerParams(
            collective_id=0, has_side_effects=True, vmem_limit_bytes=56 * 1024 * 1024
        ),
        name="sublayers",
    )(spatial_window, clip_frames, lat, jnp.transpose(modulation, (1, 0, 2)), wsp, wo, wqt, wot)
    return jnp.transpose(jnp.concatenate([out_a, out_b], axis=0))


def solution(mesh):
    return jax.shard_map(
        shards,
        mesh=mesh,
        in_specs=(
            P("seq", None),
            P("cfg", None, None),
            P(None, None, "head"),
            P("head", None),
            P(None, None, "head"),
            P("head", None),
            P(),
            P(),
        ),
        out_specs=P("seq", "cfg"),
        check_vma=False,
    )
```
